32 devices in a mesh: wide: 16 (over z, x, core), narrow: 2 (over y).
Axes of the slice: x: 2, y: 2, z: 4, core: 2. Of those that a mesh axis runs over, the one named last changes fastest.
Arguments:
- ice_x: float32 [256, 10, 256], P('wide', None, 'narrow'), may hold values from -6 to 6
- ice_y: float32 [256, 10, 256], P('wide', None, 'narrow'), may hold values from -6 to 6
- ice_temp: float32 [256, 10, 256], P('wide', None, 'narrow'), may hold values from -2 to 2
- ocean_x: float32 [256, 80, 256], P('wide', None, 'narrow'), may hold values from -6 to 6
- ocean_y: float32 [256, 80, 256], P('wide', None, 'narrow'), may hold values from -6 to 6
- ocean_temp: float32 [256, 80, 256], P('wide', None, 'narrow'), may hold values from -2 to 2
- thick: float32 [256, 256], P('wide', 'narrow'), may hold values from 1 to 10
- grounded_mask: int32 [256, 256], P('wide', 'narrow'), may hold values 0 or 1
- wet_mask: int32 [256, 256], P('wide', 'narrow'), may hold values 0 or 1
- ice_links: int32 [256, 2], P('wide', 'narrow'), may hold values from -1 to 255, as said below
- ocean_links: int32 [256, 2], P('wide', 'narrow'), may hold values from -1 to 255, as said below
Outputs:
- ice_state: float32 [3, 256, 10, 256], P(None, 'wide', None, 'narrow')
- ocean_state: float32 [3, 256, 80, 256], P(None, 'wide', None, 'narrow')
- thick_out: float32 [256, 256], P('wide', 'narrow')
- melt_out: float32 [256, 256], P('wide', 'narrow')
The draws below stay inside these ranges and needn't reach their ends.
Inputs may be any that keep to these rules, and one draw needn't show every extreme that they name: `ice_links`: within one column group an ice block names an ocean block exactly when that ocean block names it back. Per column group, for any ocean tile and ice tile, at most 2 blocks of the ocean tile names a block of the ice tile, and that bound is reached in every draw, as is an ocean tile with all 16 blocks linked. `ocean_links`: the mirror of ice_links, as described there.
All inputs are finite; a program needn't handle non-finite values. No bound on the sum of `grounded_mask` or of `wet_mask` on one device may be relied on, other than what follows from the above.
Results may differ from the reference program's by a relative error of at most 0.000071.
Values sent between devices are 32-bit elements; how exact they have to be, the bound alone decides.
No kernel may reach another device: no remote copies, remote signals or barrier semaphores. Data moves between devices by JAX's collectives and lax.ppermute only.
A program may use at most 64 MiB of HBM per device.

```python
import math
import jax
import jax.numpy as jnp

TC = 128
LAYERS = 10
LEVELS = 80
PICARD = 2
NB = 16
CAP = 2
BR = 1
ROWS = 256
COLS = 256
N_WIDE = 16
N_NARROW = 2


def link_column(key):
    count = N_WIDE
    key_order, key_share, key_roll, key_anchor, key_slots = jax.random.split(key, 5)
    sigma = jax.random.permutation(key_order, count).astype(jnp.int32)
    share = 75 + jax.random.randint(key_share, (count,), 0, 26)
    rolled = jax.random.randint(key_roll, (count, NB), 0, 100)
    anchor = jax.random.randint(key_anchor, (), 0, count)
    forced = (anchor - sigma) % count < NB // CAP
    coupled = (rolled < share[:, None]) | forced[:, None]
    block_index = jnp.arange(NB, dtype=jnp.int32)
    offset = block_index // CAP
    target = (sigma[:, None] + offset[None, :]) % count
    perms = jax.vmap(lambda inner: jax.random.permutation(inner, NB))(jax.random.split(key_slots, count)).astype(jnp.int32)
    destination = target * NB + perms[target, jnp.broadcast_to(block_index[None, :], target.shape)]
    ice_side = jnp.where(coupled, destination, -1).astype(jnp.int32).reshape(-1)
    source = (jnp.arange(count, dtype=jnp.int32)[:, None] * NB + block_index[None, :]).astype(jnp.int32)
    ocean_side = jnp.full((count * NB,), -1, jnp.int32).at[destination.reshape(-1)].set(jnp.where(coupled, source, -1).reshape(-1).astype(jnp.int32))
    return jnp.stack([ice_side, ocean_side])


def link_tables(key):
    base = jax.random.fold_in(key, 7)
    return jax.vmap(link_column)(jax.random.split(base, N_NARROW))


def draw_ice_links(key, part):
    return link_tables(key)[:, 0, :].T.astype(jnp.int32)


def draw_ocean_links(key, part):
    return link_tables(key)[:, 1, :].T.astype(jnp.int32)


def plant(values, stream_key, low, high):
    longest = values.shape.index(max(values.shape))
    spots = []
    for shift in (0, 1):
        where = [jax.random.randint(jax.random.fold_in(stream_key, axis), (), 0, length) for axis, length in enumerate(values.shape)]
        where[longest] = (where[longest] + shift) % values.shape[longest]
        spots.append(tuple(where))
    return values.at[spots[0]].set(low).at[spots[1]].set(high)


def block_scale(key, shape, cuts, smallest, largest):
    def one(axis_at, blocks):
        steps = jax.random.uniform(jax.random.fold_in(jax.random.fold_in(key, 6), axis_at), (blocks,), jnp.float32, smallest / len(cuts), largest / len(cuts))
        return jnp.repeat(jnp.exp(steps), shape[axis_at] // blocks).reshape((-1,) + (1,) * (len(shape) - axis_at - 1))

    gain = one(*cuts[0])
    for cut in cuts[1:]:
        gain = gain * one(*cut)
    return gain


def centred(own_key, shape, width, most, cuts=(), kind=jnp.bfloat16):
    result = width * jax.random.normal(own_key, shape, jnp.float32)
    if cuts:
        result = result * block_scale(own_key, shape, cuts, -0.22, 0.18)
    return jnp.clip(result, -most, most).astype(kind)


def setup_inputs(seed: int = 0) -> dict:
    streams_of = jax.random.split(jax.random.key(seed), 12)
    return {
        "ice_x": centred(streams_of[0], (ROWS, LAYERS, COLS), 1.0, 6.0, ((0, 16), (2, 2)), jnp.float32),
        "ice_y": centred(streams_of[1], (ROWS, LAYERS, COLS), 1.0, 6.0, ((0, 16), (2, 2)), jnp.float32),
        "ice_temp": jnp.clip(jax.random.uniform(streams_of[2], (ROWS, LAYERS, COLS), jnp.float32, -2.0, 2.0) * block_scale(streams_of[2], (ROWS, LAYERS, COLS), ((0, 16), (2, 2)), -0.4, 0.0), -2.0, 2.0),
        "ocean_x": centred(streams_of[3], (ROWS, LEVELS, COLS), 1.0, 6.0, ((0, 16), (2, 2)), jnp.float32),
        "ocean_y": centred(streams_of[4], (ROWS, LEVELS, COLS), 1.0, 6.0, ((0, 16), (2, 2)), jnp.float32),
        "ocean_temp": jnp.clip(jax.random.uniform(streams_of[5], (ROWS, LEVELS, COLS), jnp.float32, -2.0, 2.0) * block_scale(streams_of[5], (ROWS, LEVELS, COLS), ((0, 16), (2, 2)), -0.4, 0.0), -2.0, 2.0),
        "thick": jnp.clip(jnp.exp(math.log(10.0) - 2.3025851 * jax.random.uniform(streams_of[6], (ROWS, COLS), jnp.float32) ** block_scale(streams_of[6], (ROWS, COLS), ((0, 16), (1, 2)), -0.2, 0.2)), 1.0, 10.0),
        "grounded_mask": plant((jax.random.randint(streams_of[7], (ROWS, COLS), 0, 2) < 1).astype(jnp.int32), jax.random.fold_in(streams_of[7], 1), 0, 1),
        "wet_mask": plant((jax.random.randint(streams_of[8], (ROWS, COLS), 0, 2) < 1).astype(jnp.int32), jax.random.fold_in(streams_of[8], 1), 0, 1),
        "ice_links": draw_ice_links(jax.random.fold_in(streams_of[11], 71), 0),
        "ocean_links": draw_ocean_links(jax.random.fold_in(streams_of[11], 71), 0),
    }


DIFFUSE = 0.2
GAMMA_MELT = 0.5
TIME_STEP = 0.05
SLOPE_SCALE = 0.1
STRAIN_FLOOR = 0.01
HEATING_RATE = 0.01


def to_blocks(field):
    count_rows = field.shape[0]
    return field.reshape(count_rows // BR, BR, N_NARROW, TC).transpose(0, 2, 1, 3)


def from_blocks(pieces):
    count = pieces.shape[0]
    return pieces.transpose(0, 2, 1, 3).reshape(count * BR, N_NARROW * TC)


def fetch(pieces, link_list):
    linked = (link_list >= 0).astype(jnp.float32)
    link_safe = jnp.maximum(link_list, 0).astype(jnp.int32)
    arrived = pieces[link_safe, jnp.arange(N_NARROW, dtype=jnp.int32)[None, :]]
    weight = jnp.broadcast_to(linked[:, :, None, None], arrived.shape)
    return from_blocks(arrived * weight), from_blocks(weight)


def apply_diffuse(field_pad, wet_pad):
    count_rows = field_pad.shape[0] - 2
    count_cols = field_pad.shape[2] - 2
    centre = field_pad[1:-1, :, 1:-1]
    wet_centre = wet_pad[1:-1, 1:-1]
    total = jnp.zeros_like(centre)
    for row_off, col_off in ((0, 1), (2, 1), (1, 0), (1, 2)):
        weight = wet_centre * wet_pad[row_off:row_off + count_rows, col_off:col_off + count_cols]
        total = total + weight[:, None, :] * (field_pad[row_off:row_off + count_rows, :, col_off:col_off + count_cols] - centre)
    return centre + DIFFUSE * total


def strains(padded):
    along_rows = 0.5 * (padded[2:, :, 1:-1] - padded[:-2, :, 1:-1])
    along_cols = 0.5 * (padded[1:-1, :, 2:] - padded[1:-1, :, :-2])
    middle = padded[1:-1, :, 1:-1]
    vertical = jnp.concatenate([middle[:, 1:, :] - middle[:, :-1, :], jnp.zeros_like(middle[:, :1, :])], axis=1)
    return along_rows, along_cols, vertical, middle


def layer_shift(field):
    zeros = jnp.zeros_like(field[:, :1, :])
    above = jnp.concatenate([field[:, 1:, :], zeros], axis=1)
    below = jnp.concatenate([zeros, field[:, :-1, :]], axis=1)
    return above + below


def picard(pad_x, pad_y, rate_factor, inside, stress_x, stress_y, friction):
    count_rows = pad_x.shape[0] - 4
    count_cols = pad_x.shape[2] - 4
    layers = pad_x.shape[1]
    ux, uy, uz, mid_x = strains(pad_x)
    vx, vy, vz, mid_y = strains(pad_y)
    eps2 = ux * ux + vy * vy + ux * vy + 0.25 * (uy + vx) ** 2 + 0.25 * (uz * uz + vz * vz)
    eta = rate_factor * (eps2 + STRAIN_FLOOR) ** (-1.0 / 3.0) * inside[:, None, :]
    centre = eta[1:-1, :, 1:-1]
    level = jnp.arange(layers)
    vertical_count = ((level > 0).astype(jnp.float32) + (level < layers - 1).astype(jnp.float32))[None, :, None]
    diagonal = centre * vertical_count + friction[:, None, :]
    sum_x = stress_x[:, None, :] + centre * layer_shift(mid_x[1:-1, :, 1:-1])
    sum_y = stress_y[:, None, :] + centre * layer_shift(mid_y[1:-1, :, 1:-1])
    for row_off, col_off in ((0, 1), (2, 1), (1, 0), (1, 2)):
        face = 0.5 * (centre + eta[row_off:row_off + count_rows, :, col_off:col_off + count_cols])
        diagonal = diagonal + face
        sum_x = sum_x + face * mid_x[row_off:row_off + count_rows, :, col_off:col_off + count_cols]
        sum_y = sum_y + face * mid_y[row_off:row_off + count_rows, :, col_off:col_off + count_cols]
    return sum_x / diagonal, sum_y / diagonal, centre * eps2[1:-1, :, 1:-1]


def reference(ice_x, ice_y, ice_temp, ocean_x, ocean_y, ocean_temp, thick, grounded_mask, wet_mask, ice_links, ocean_links):
    grounded = grounded_mask.astype(jnp.float32)
    wet = wet_mask.astype(jnp.float32)
    draft_field = 0.9 * thick * (1.0 - grounded)
    ocean_draft, coupled = fetch(to_blocks(draft_field), ocean_links)
    wet_pad = jnp.pad(wet, 1)
    pad_three = ((1, 1), (0, 0), (1, 1))
    ocean_heat = apply_diffuse(jnp.pad(ocean_temp, pad_three), wet_pad)
    current_x = apply_diffuse(jnp.pad(ocean_x, pad_three), wet_pad)
    current_y = apply_diffuse(jnp.pad(ocean_y, pad_three), wet_pad)
    freezing = 0.0832 - 0.761 * ocean_draft
    melt_rate = GAMMA_MELT * (ocean_heat[:, 0, :] - freezing) * wet * coupled
    ocean_heat = ocean_heat.at[:, 0, :].add(-0.2 * melt_rate)
    ice_melt, unused = fetch(to_blocks(melt_rate), ice_links)
    new_thick = thick - TIME_STEP * ice_melt * (1.0 - grounded)
    surface = new_thick * (0.1 + 0.9 * grounded)
    surface_pad = jnp.pad(surface, 1)
    stress_x = -SLOPE_SCALE * new_thick * 0.5 * (surface_pad[2:, 1:-1] - surface_pad[:-2, 1:-1])
    stress_y = -SLOPE_SCALE * new_thick * 0.5 * (surface_pad[1:-1, 2:] - surface_pad[1:-1, :-2])
    friction = 0.1 + 9.9 * grounded
    inside = jnp.pad(jnp.ones((ROWS, COLS), jnp.float32), 1)
    rate_factor = jnp.exp(0.25 * jnp.pad(ice_temp, pad_three))
    velocity_x = ice_x
    velocity_y = ice_y
    pad_two = ((2, 2), (0, 0), (2, 2))
    heating = jnp.zeros_like(velocity_x)
    for sweep_index in range(PICARD):
        velocity_x, velocity_y, heating = picard(jnp.pad(velocity_x, pad_two), jnp.pad(velocity_y, pad_two), rate_factor, inside, stress_x, stress_y, friction)
    ice_heat = ice_temp + HEATING_RATE * heating
    ice_state = jnp.stack([velocity_x, velocity_y, ice_heat])
    ocean_state = jnp.stack([current_x, current_y, ocean_heat])
    return ice_state, ocean_state, new_thick, melt_rate
```

```python
import functools

import jax
import jax.numpy as jnp
from jax import lax
from jax.experimental import pallas as pl
from jax.experimental.pallas import tpu as pltpu
from jax.sharding import PartitionSpec as P

PICARD = 2
DIFFUSE = 0.2
GAMMA_MELT = 0.5
TIME_STEP = 0.05
SLOPE_SCALE = 0.1
STRAIN_FLOOR = 0.01
HEATING_RATE = 0.01

LANES = 128
PLANE_ROWS = 8
HALO = 4
RIM = 3
VMEM = pltpu.CompilerParams(vmem_limit_bytes=48 * 1024 * 1024)
HIGHEST = lax.Precision.HIGHEST
F32 = jnp.float32

THICK, GROUNDED, OCEAN_T, WET, ICE_LINK, OCEAN_LINK, OWN_LINK = range(7)
PART, EDGE_T0, EDGE_T1, EDGE_W0, PART_WET, EDGE_W1 = range(6)


def pad8(n):
    return -(-n // 8) * 8


def iota(shape, axis):
    return lax.broadcasted_iota(jnp.int32, shape, axis)


def right_lanes(period):
    lane = iota((1, LANES), 1)
    return lane % period < HALO


def left_lanes(period):
    lane = iota((1, LANES), 1)
    return lane % period >= period - HALO


def spread(column, count=LANES):
    rows = column.shape[0]
    eye = iota((rows, count), 0) == iota((rows, count), 1)
    return jnp.sum(jnp.where(eye, column, 0.0), axis=0, keepdims=True)


def divide(whole, part):
    return jnp.floor((whole + 0.5) * (1.0 / part))


def dot(a, b):
    return jnp.dot(a, b, precision=HIGHEST, preferred_element_type=F32)


def narrow_sides(n_narrow):
    place = lax.axis_index("narrow")
    return place < n_narrow - 1, place > 0


def merged(parts, right, left, n_narrow):
    has_right, has_left = narrow_sides(n_narrow)
    from_right, from_left = parts[0], parts[-1]
    if len(parts) == 1:
        keep = (right & has_right) | (left & has_left)
        return jnp.where(keep, from_right, 0.0)
    return jnp.where(right, from_right, jnp.where(left, from_left, 0.0))


def edges_kernel(
    ice_x, ice_y, ice_t, ocean_x, ocean_y, ocean_t, thick, grounded, wet, ice_links, ocean_links,
    out, plane_t, held, sems,
):
    rows, layers, _ = ice_x.shape
    levels = ocean_x.shape[1]
    layer_rows = pad8(layers)
    half = rows // 2
    copies = []
    for f, field in enumerate((ocean_x, ocean_y, ocean_t)):
        for h in range(2):
            part = pl.ds(h * half, half)
            copies.append(pltpu.make_async_copy(field.at[part], held.at[f, part], sems.at[f, h]))
            copies[-1].start()
    lane = iota((1, LANES), 1)
    base = levels
    for f, field in enumerate((ice_x, ice_y, ice_t)):
        total = jnp.zeros((layers, LANES), F32)
        for i in range(rows):
            turned = pltpu.roll(field[i], 8 * i, 1) if i else field[i]
            total = jnp.where((lane + HALO) % LANES // 8 == i, turned, total)
        out[base : base + layer_rows, :] = jnp.zeros((layer_rows, LANES), F32)
        out[base : base + layers, :] = total
        base += layer_rows
    total = jnp.zeros((levels, LANES), F32)
    for f in range(3):
        for h in range(2):
            copies[2 * f + h].wait()
            for i in range(h * half, (h + 1) * half):
                j = f * rows + i
                tile = held[f, i]
                turned = pltpu.roll(tile, 2 * j, 1) if j else tile
                total = jnp.where((lane + 1) % LANES // 2 == j, turned, total)
                if f == 2:
                    plane_t[i : i + 1, :] = tile[0:1, :]
    out[0:levels, :] = total
    planes = (
        thick[...],
        grounded[...].astype(F32),
        plane_t[...],
        wet[...].astype(F32),
        jnp.broadcast_to(ice_links[...].astype(F32) + 1.0, (rows, LANES)),
        jnp.broadcast_to(ocean_links[...].astype(F32) + 1.0, (rows, LANES)),
    )
    total = jnp.zeros((rows, LANES), F32)
    for j, plane in enumerate(planes):
        turned = pltpu.roll(plane, 16 * j, 1) if j else plane
        total = jnp.where((lane + HALO) % LANES // 16 == j, turned, total)
    out[base : base + rows, :] = total


def plane_halo(block, group):
    lane = iota((1, LANES), 1)
    turned = pltpu.roll(block, LANES - 16 * group, 1) if group else block
    return jnp.where((lane < HALO) | (lane >= LANES - HALO), turned, 0.0)


def ranks(own_col, member_col, order_sub, order_lane, own_row):
    hits = (own_col == own_row) & member_col & (order_sub < order_lane)
    return jnp.sum(hits.astype(F32), axis=0, keepdims=True)


def ocean_slots(link_col, rows, n_wide, cap, block):
    link_row = spread(link_col)
    parts = []
    for link in (link_col, link_row):
        number = link - 1.0
        tile = divide(number, rows)
        inner = number - tile * rows
        ok = link > 0.5
        parts.append(
            (
                tile,
                (
                    ok,
                    ok & (inner >= rows - RIM) & (tile < n_wide - 1.5),
                    ok & (inner < RIM) & (tile > 0.5),
                ),
            )
        )
    (tile_col, member_col), (tile_row, member_row) = parts
    order_sub, order_lane = iota((rows, LANES), 0), iota((rows, LANES), 1)
    place = iota((n_wide * block, LANES), 0).astype(F32)
    total = jnp.zeros((n_wide * block, LANES), F32)
    for k, shift in enumerate((0.0, 1.0, -1.0)):
        rank = ranks(tile_col, member_col[k], order_sub, order_lane, tile_row)
        target = jnp.where(
            member_row[k], (tile_row + shift) * block + (k * cap + rank), -1.0
        )
        total = total + (place == target).astype(F32)
    return total[:, :rows]


def draft_slots(link_col, rows, n_wide, cap, block):
    link_row = spread(link_col)
    tile_col, tile_row = divide(link_col - 1.0, rows), divide(link_row - 1.0, rows)
    order_sub, order_lane = iota((rows, LANES), 0), iota((rows, LANES), 1)
    rank = ranks(tile_col, link_col > 0.5, order_sub, order_lane, tile_row)
    target = jnp.where(link_row > 0.5, tile_row * block + (3 * cap + rank), -1.0)
    place = iota((n_wide * block, LANES), 0).astype(F32)
    return (place == target).astype(F32)[:, :rows]


def send_kernel(
    n_wide, n_narrow, cap, block, n_parts, levels,
    *refs,
):
    parts, refs = refs[:n_parts], refs[n_parts:]
    (
        ice_x, ice_y, ice_t, x_first, x_last, y_first, y_last, t_first, t_last, plane_t,
        thick, grounded, wet, ice_links, ocean_links, up, down, blocks,
    ) = refs
    rows, layers, _ = ice_x.shape
    layer_rows = pad8(layers)
    lane = iota((1, LANES), 1)
    base = levels + 3 * layer_rows
    plane_block = merged(
        [p[base : base + rows, :] for p in parts], right_lanes(16), left_lanes(16), n_narrow
    )
    link_own = ice_links[...].astype(F32) + 1.0
    plane_block = jnp.where(
        (lane + HALO) % LANES // 16 == OWN_LINK, link_own, plane_block
    )
    thick_plane = thick[...]
    grounded_plane = grounded[...].astype(F32)
    wet_plane = wet[...].astype(F32)
    at = 0
    for lasts, firsts in ((x_last, x_first), (y_last, y_first), (t_last, t_first)):
        up[at : at + levels, :] = lasts[0]
        down[at : at + levels, :] = firsts[0]
        at += levels
    for field in (ice_x, ice_y, ice_t):
        for i in range(HALO):
            up[at : at + layer_rows, :] = jnp.zeros((layer_rows, LANES), F32)
            down[at : at + layer_rows, :] = jnp.zeros((layer_rows, LANES), F32)
            up[at : at + layers, :] = field[rows - HALO + i]
            down[at : at + layers, :] = field[i]
            at += layer_rows
    strip = merged(
        [p[levels:base, :] for p in parts], right_lanes(8), left_lanes(8), n_narrow
    )
    up[at : at + 3 * layer_rows, :] = strip
    down[at : at + 3 * layer_rows, :] = strip
    at += 3 * layer_rows
    for plane in (thick_plane, grounded_plane, wet_plane, plane_block):
        up[at : at + PLANE_ROWS, :] = plane[rows - PLANE_ROWS :, :]
        down[at : at + PLANE_ROWS, :] = plane[:PLANE_ROWS, :]
        at += PLANE_ROWS
    wet_all = jnp.concatenate([wet_plane, plane_halo(plane_block, WET)], axis=1)
    warm = wet_all * jnp.concatenate([plane_t[...], plane_halo(plane_block, OCEAN_T)], axis=1)
    width = 2 * LANES
    row = iota((rows, width), 0)
    sums = []
    for value in (wet_all, warm):
        total = pltpu.roll(value, 1, 1) + pltpu.roll(value, width - 1, 1)
        total = total + jnp.where(row > 0, pltpu.roll(value, 1, 0), 0.0)
        sums.append(total + jnp.where(row < rows - 1, pltpu.roll(value, rows - 1, 0), 0.0))
    mixed = warm + DIFFUSE * (wet_all * sums[1] - warm * sums[0])
    draft = 0.9 * thick_plane * (1.0 - grounded_plane)
    own_slots = ocean_slots(ocean_links[...].astype(F32) + 1.0, rows, n_wide, cap, block)
    main = dot(own_slots, jnp.concatenate([mixed[:, :LANES], wet_plane], axis=1))
    count = n_wide * block
    slot = iota((count, 1), 0) % block
    first = main[:, :LANES] + dot(draft_slots(link_own, rows, n_wide, cap, block), draft)
    second = jnp.where(
        slot == 3 * cap,
        wet_plane[0:1, :],
        jnp.where(slot == 3 * cap + 1, wet_plane[rows - 1 : rows, :], main[:, LANES:]),
    )
    edge = (lane < HALO) | (lane >= LANES - HALO)
    mixed_edge = jnp.where(edge, mixed[:, LANES:], 0.0)
    wet_edge = wet_all[:, LANES:]
    warm_edge = warm[:, LANES:]
    packed = mixed_edge + pltpu.roll(wet_edge, 16 * PART_WET, 1)
    links = plane_halo(plane_block, OCEAN_LINK)
    if n_narrow == 2:
        third = dot(
            ocean_slots(jnp.max(links, axis=1, keepdims=True), rows, n_wide, cap, block), packed
        )
    else:
        third = dot(
            ocean_slots(links[:, 0:1], rows, n_wide, cap, block),
            jnp.where(right_lanes(16), packed, 0.0),
        ) + dot(
            ocean_slots(links[:, LANES - 1 : LANES], rows, n_wide, cap, block),
            jnp.where(left_lanes(16), packed, 0.0),
        )
    last = rows - 1
    ends = (
        pltpu.roll(warm_edge[0:1, :], 16 * EDGE_T0, 1)
        + pltpu.roll(warm_edge[last:, :], 16 * EDGE_T1, 1)
        + pltpu.roll(wet_edge[0:1, :], 16 * EDGE_W0, 1)
        + pltpu.roll(wet_edge[last:, :], 16 * EDGE_W1, 1)
    )
    third = jnp.where(
        slot == 3 * cap,
        warm[0:1, :LANES],
        jnp.where(slot == 3 * cap + 1, warm[last:, :LANES], third + ends),
    )
    for k, value in enumerate((first, second, third)):
        blocks[:, k * block : (k + 1) * block, :] = value.reshape(n_wide, block, LANES)


def ocean_kernel(
    n_narrow, n_parts,
    *refs,
):
    parts, refs = refs[:n_parts], refs[n_parts:]
    ocean_x, ocean_y, ocean_t, up, down, wet, out, held, coef, in_sems, out_sems = refs
    rows, levels, _ = ocean_x.shape
    chunks = in_sems.shape[1]
    step = rows // chunks
    copies = {}
    for f, field in enumerate((ocean_x, ocean_y, ocean_t)):
        for h in range(chunks):
            copy = pltpu.make_async_copy(
                field.at[pl.ds(h * step, step)],
                held.at[f, pl.ds(1 + h * step, step)],
                in_sems.at[f, h],
            )
            copy.start()
            copies[f, h] = copy
    lane = iota((1, LANES), 1)
    strip_base = parts[0].shape[0] - rows
    plane_block = merged(
        [p[strip_base:, :] for p in parts], right_lanes(16), left_lanes(16), n_narrow
    )
    plane_at = up.shape[0] - 2 * PLANE_ROWS
    wet_plane = wet[...].astype(F32)
    wet_halo = plane_halo(plane_block, WET)
    row = iota((rows, LANES), 0)
    above = jnp.where(
        row == 0,
        up[plane_at + PLANE_ROWS - 1 : plane_at + PLANE_ROWS, :],
        pltpu.roll(wet_plane, 1, 0),
    )
    below = jnp.where(row == rows - 1, down[plane_at : plane_at + 1, :], pltpu.roll(wet_plane, rows - 1, 0))
    before = pltpu.roll(jnp.where(lane == LANES - 1, wet_halo, wet_plane), 1, 1)
    after = pltpu.roll(jnp.where(lane == 0, wet_halo, wet_plane), LANES - 1, 1)
    scale = DIFFUSE * wet_plane
    coef[0] = scale * above
    coef[1] = scale * below
    coef[2] = scale * before
    coef[3] = scale * after
    coef[4] = 1.0 - scale * (above + below + before + after)
    for f in range(3):
        held[f, 0] = up[f * levels : (f + 1) * levels, :]
        held[f, rows + 1] = down[f * levels : (f + 1) * levels, :]
    odd = lane % 2 == 1
    halo = merged([p[0:levels, :] for p in parts], ~odd, odd, n_narrow)
    first, last = lane == 0, lane == LANES - 1
    writes = []
    for f in range(3):
        for h in range(chunks):
            copies[f, h].wait()
        for h in range(chunks):
            for i in range(h * step, (h + 1) * step):
                j = f * rows + i
                side = pltpu.roll(halo, LANES - 2 * j, 1) if j else halo
                centre = held[f, i + 1]
                left = pltpu.roll(jnp.where(last, side, centre), 1, 1)
                right = pltpu.roll(jnp.where(first, side, centre), LANES - 1, 1)
                value = centre * coef[4, i : i + 1, :]
                value = value + held[f, i] * coef[0, i : i + 1, :]
                value = value + held[f, i + 2] * coef[1, i : i + 1, :]
                value = value + left * coef[2, i : i + 1, :]
                value = value + right * coef[3, i : i + 1, :]
                held[f + 3, i] = value
            part = pl.ds(h * step, step)
            copy = pltpu.make_async_copy(held.at[f + 3, part], out.at[f, part], out_sems.at[f, h])
            copy.start()
            writes.append(copy)
    for copy in writes:
        copy.wait()


def ice_slots(link_col, kind_col, rows, cap, block, count, n_wide):
    link_row = spread(link_col)
    kind_row = spread(kind_col)
    number = link_col - 1.0
    tile = divide(number, rows)
    inner = number - tile * rows
    tile_row = divide(link_row - 1.0, rows)
    ok = (link_col > 0.5) & (kind_col > -0.5)
    ok_row = (link_row > 0.5) & (kind_row > -0.5)
    hits = (tile == tile_row) & (kind_col == kind_row) & ok_row & (link_row < link_col)
    rank = jnp.sum(hits.astype(F32), axis=1, keepdims=True)
    place = iota((link_col.shape[0], count), 1).astype(F32)

    def hot(keep, target):
        return (place == jnp.where(keep, target, -1.0)).astype(F32)

    top, bottom = inner < 0.5, inner > rows - 1.5
    edge = ok & (top | bottom)
    near = jnp.where(top, tile - 1.0, tile + 1.0)
    near_ok = edge & (near > -0.5) & (near < n_wide - 0.5)
    slot = hot(ok, tile * block + kind_col * cap + rank)
    near_edge = hot(near_ok, near * block + jnp.where(top, 3.0 * cap + 1.0, 3.0 * cap))
    own_edge = hot(edge, tile * block + jnp.where(top, 3.0 * cap, 3.0 * cap + 1.0))
    near_slot = hot(near_ok, near * block)
    own_slot = hot(edge, tile * block)
    return slot, near_edge, own_edge, near_slot, own_slot, top


def final_kernel(
    n_wide, n_narrow, cap, block, n_parts, levels,
    *refs,
):
    parts, refs = refs[:n_parts], refs[n_parts:]
    (
        ice_x, ice_y, ice_t, up, down, blocks, thick, grounded, wet, ice_links, ocean_links, ocean_in,
        ice_out, ocean_out, thick_out, melt_out,
        vel, rate, eta, push, side, heat, flat, top_level, sems,
    ) = refs
    rows, layers, _ = ice_x.shape
    layer_rows = pad8(layers)
    fetch = pltpu.make_async_copy(ocean_in.at[2, :, pl.ds(0, 8), :], top_level, sems.at[0])
    fetch.start()
    width = 2 * LANES
    lane = iota((1, LANES), 1)
    wide_lane = iota((1, width), 1)
    place_wide = lax.axis_index("wide")
    has_right, has_left = narrow_sides(n_narrow)
    has_up, has_down = place_wide > 0, place_wide < n_wide - 1
    base = levels + 3 * layer_rows
    plane_block = merged(
        [p[base : base + rows, :] for p in parts], right_lanes(16), left_lanes(16), n_narrow
    )
    plane_at = up.shape[0] - 4 * PLANE_ROWS
    tall = rows + 2 * PLANE_ROWS

    def plane(k):
        at = plane_at + k * PLANE_ROWS
        return up[at : at + PLANE_ROWS, :], down[at : at + PLANE_ROWS, :]

    thick_up, thick_down = plane(0)
    grounded_up, grounded_down = plane(1)
    block_up, block_down = plane(3)
    block_tall = jnp.concatenate([block_up, plane_block, block_down], axis=0)
    thick_main = thick[...]
    thick_tall = jnp.concatenate(
        [
            jnp.concatenate([thick_up, thick_main, thick_down], axis=0),
            plane_halo(block_tall, THICK),
        ],
        axis=1,
    )
    grounded_tall = jnp.concatenate(
        [
            jnp.concatenate([grounded_up, grounded[...].astype(F32), grounded_down], axis=0),
            plane_halo(block_tall, GROUNDED),
        ],
        axis=1,
    )
    tall_row = iota((tall, 1), 0)
    kind = jnp.where(
        (tall_row >= PLANE_ROWS) & (tall_row < PLANE_ROWS + rows),
        0.0,
        jnp.where(
            (tall_row >= PLANE_ROWS - RIM) & (tall_row < PLANE_ROWS),
            1.0,
            jnp.where(
                (tall_row >= PLANE_ROWS + rows) & (tall_row < PLANE_ROWS + rows + RIM), 2.0, -1.0
            ),
        ),
    )
    count = n_wide * block
    first = blocks[:, 0:block, :].reshape(count, LANES)
    second = blocks[:, block : 2 * block, :].reshape(count, LANES)
    third = blocks[:, 2 * block : 3 * block, :].reshape(count, LANES)
    own_link = jnp.concatenate(
        [
            block_up[:, 16 * OWN_LINK : 16 * OWN_LINK + 1],
            ice_links[...].astype(F32) + 1.0,
            block_down[:, 16 * OWN_LINK : 16 * OWN_LINK + 1],
        ],
        axis=0,
    )
    slot, near_edge, own_edge, _, _, _ = ice_slots(
        own_link, kind, rows, cap, block, count, n_wide
    )
    got = dot(slot, jnp.concatenate([first, second], axis=1))
    near = dot(near_edge, jnp.concatenate([second, third], axis=1))
    own = dot(own_edge, third)
    wet_main = got[:, LANES:]
    mixed_main = got[:, :LANES] + DIFFUSE * (
        wet_main * near[:, LANES:] - near[:, :LANES] * own
    )

    def halo_melt(link_col):
        slot, _, _, near_slot, own_slot, top = ice_slots(
            link_col, kind, rows, cap, block, count, n_wide
        )
        got = dot(slot, third)
        near = dot(near_slot, third)
        own = dot(own_slot, third)

        def group(value, j):
            return pltpu.roll(value, LANES - 16 * j, 1) if j else value

        wet_got = group(got, PART_WET)
        near_warm = jnp.where(top, group(near, EDGE_T1), group(near, EDGE_T0))
        near_wet = jnp.where(top, group(near, EDGE_W1), group(near, EDGE_W0))
        own_warm = jnp.where(top, group(own, EDGE_T0), group(own, EDGE_T1))
        return got + DIFFUSE * (wet_got * near_warm - near_wet * own_warm), wet_got

    links = plane_halo(block_tall, ICE_LINK)
    if n_narrow == 2:
        mixed_side, wet_side = halo_melt(jnp.max(links, axis=1, keepdims=True))
    else:
        mixed_side, wet_side = (
            jnp.where(lane < HALO, a, b)
            for a, b in zip(halo_melt(links[:, 0:1]), halo_melt(links[:, LANES - 1 : LANES]))
        )
    mixed_tall = jnp.concatenate([mixed_main, mixed_side], axis=1)
    wet_tall = jnp.concatenate([wet_main, wet_side], axis=1)
    inside = (
        ((tall_row >= PLANE_ROWS) | has_up)
        & ((tall_row < PLANE_ROWS + rows) | has_down)
        & (
            (wide_lane < LANES)
            | ((wide_lane < LANES + HALO) & has_right)
            | ((wide_lane >= width - HALO) & has_left)
        )
    ).astype(F32)
    open_ice = 1.0 - grounded_tall
    draft_tall = 0.9 * thick_tall * open_ice
    melt_tall = GAMMA_MELT * (mixed_tall - wet_tall * (0.0832 - 0.761 * draft_tall))
    new_thick = (thick_tall - TIME_STEP * melt_tall * open_ice) * inside
    thick_out[...] = new_thick[PLANE_ROWS : PLANE_ROWS + rows, :LANES]
    surface = new_thick * (0.1 + 0.9 * grounded_tall)
    push_scale = (-0.5 * SLOPE_SCALE) * new_thick
    flat[0] = push_scale * (pltpu.roll(surface, tall - 1, 0) - pltpu.roll(surface, 1, 0))
    flat[1] = push_scale * (pltpu.roll(surface, width - 1, 1) - pltpu.roll(surface, 1, 1))
    flat[2] = 0.1 + 9.9 * grounded_tall
    flat[3] = inside
    ocean_link = ocean_links[...].astype(F32) + 1.0
    ocean_row = spread(ocean_link)
    tile = divide(ocean_link - 1.0, rows)
    tile_row = divide(ocean_row - 1.0, rows)
    hits = (tile == tile_row) & (ocean_row > 0.5) & (ocean_row < ocean_link)
    rank = jnp.sum(hits.astype(F32), axis=1, keepdims=True)
    coupled = ocean_link > 0.5
    target = jnp.where(coupled, tile * block + 3 * cap + rank, -1.0)
    ocean_draft = dot((iota((rows, count), 1).astype(F32) == target).astype(F32), first)
    fetch.wait()
    heat_top = jnp.concatenate([top_level[i, 0:1, :] for i in range(rows)], axis=0)
    melt = (
        GAMMA_MELT
        * (heat_top - (0.0832 - 0.761 * ocean_draft))
        * wet[...].astype(F32)
        * coupled.astype(F32)
    )
    melt_out[...] = melt
    new_top = heat_top - 0.2 * melt
    for i in range(rows):
        top_level[i, 0:1, :] = new_top[i : i + 1, :]
    store = pltpu.make_async_copy(top_level, ocean_out.at[2, :, pl.ds(0, 8), :], sems.at[1])
    store.start()
    n_ice = rows + 2 * HALO
    offset = PLANE_ROWS - HALO
    ice_at = 3 * levels
    strip_at = ice_at + 3 * HALO * layer_rows
    strip = merged(
        [p[levels:base, :] for p in parts], right_lanes(8), left_lanes(8), n_narrow
    )
    edge = (lane < HALO) | (lane >= LANES - HALO)
    for f, field in enumerate((ice_x, ice_y, ice_t)):
        strips = (
            up[strip_at + f * layer_rows : strip_at + (f + 1) * layer_rows, :],
            strip[f * layer_rows : (f + 1) * layer_rows, :],
            down[strip_at + f * layer_rows : strip_at + (f + 1) * layer_rows, :],
        )
        for b in range(n_ice):
            i = b - HALO
            if i < 0:
                at = ice_at + (f * HALO + b) * layer_rows
                main, source, i = up[at : at + layer_rows, :], strips[0], rows + i
            elif i < rows:
                main = jnp.concatenate(
                    [field[i], jnp.zeros((layer_rows - layers, LANES), F32)], axis=0
                )
                source = strips[1]
            else:
                at = ice_at + (f * HALO + i - rows) * layer_rows
                main, source, i = down[at : at + layer_rows, :], strips[2], i - rows
            turned = pltpu.roll(source, (LANES - 8 * i) % LANES, 1) if i else source
            beside = jnp.where(edge, turned, 0.0)
            if f < 2:
                vel[f, b, :, 0:LANES] = main
                vel[f, b, :, LANES:width] = beside
            else:
                mask = inside[b + offset : b + offset + 1, :]
                rate[b, :, 0:LANES] = jnp.exp(0.25 * main) * mask[:, :LANES]
                rate[b, :, LANES:width] = jnp.exp(0.25 * beside) * mask[:, LANES:]
    level = iota((layer_rows, 1), 0)
    not_last = (level < layers - 1).astype(F32)
    links_up_down = (level > 0).astype(F32) + not_last
    real = (level < layers).astype(F32)

    def strain(b, sweep):
        u, v = vel[2 * sweep, b], vel[2 * sweep + 1, b]
        u_left, u_right = pltpu.roll(u, 1, 1), pltpu.roll(u, width - 1, 1)
        v_left, v_right = pltpu.roll(v, 1, 1), pltpu.roll(v, width - 1, 1)
        ux = vel[2 * sweep, b + 1] - vel[2 * sweep, b - 1]
        vx = vel[2 * sweep + 1, b + 1] - vel[2 * sweep + 1, b - 1]
        uy, vy = u_right - u_left, v_right - v_left
        uz = (pltpu.roll(u, layer_rows - 1, 0) - u) * not_last
        vz = (pltpu.roll(v, layer_rows - 1, 0) - v) * not_last
        cross = uy + vx
        eps2 = 0.25 * (ux * (ux + vy) + vy * vy + 0.25 * (cross * cross) + (uz * uz + vz * vz))
        value = rate[b] * jnp.exp((-1.0 / 3.0) * jnp.log(eps2 + STRAIN_FLOOR))
        eta[b] = value
        push[0, b] = value * u
        push[1, b] = value * v
        side[0, b] = u_left + u_right
        side[1, b] = v_left + v_right
        if sweep == PICARD - 1:
            heat[b] = (value * eps2)[:, :LANES]

    def relax(b, sweep):
        last = sweep == PICARD - 1
        span = LANES if last else width
        a = b + offset
        centre = eta[b]
        around = eta[b - 1] + eta[b + 1] + pltpu.roll(centre, 1, 1) + pltpu.roll(centre, width - 1, 1)
        diagonal = centre * (2.0 + links_up_down) + 0.5 * around + flat[2, pl.ds(a, 1), :]
        inverse = 1.0 / diagonal[:, :span]
        for f in range(2):
            field = vel[2 * sweep + f, b]
            total = 0.5 * (vel[2 * sweep + f, b - 1] + vel[2 * sweep + f, b + 1] + side[f, b])
            total = total + pltpu.roll(field, 1, 0) + pltpu.roll(field, layer_rows - 1, 0)
            pushed = push[f, b]
            near = push[f, b - 1] + push[f, b + 1]
            near = near + pltpu.roll(pushed, 1, 1) + pltpu.roll(pushed, width - 1, 1)
            total = (centre * total + 0.5 * near + flat[f, pl.ds(a, 1), :])[:, :span] * inverse
            if last:
                ice_out[f, b - HALO] = total[:layers, :]
            else:
                vel[2 * sweep + 2 + f, b] = total * (real * flat[3, pl.ds(a, 1), :])
        if last:
            ice_out[2, b - HALO] = ice_t[b - HALO] + HEATING_RATE * heat[b][:layers, :]

    for sweep in range(PICARD):
        reach = 2 * (PICARD - 1 - sweep)
        low, high = HALO - reach, HALO + rows + reach
        lax.fori_loop(low - 1, high + 1, lambda b, c: (strain(b, sweep), c)[1], 0)
        lax.fori_loop(low, high, lambda b, c: (relax(b, sweep), c)[1], 0)
    store.wait()


def local(
    ice_x, ice_y, ice_temp, ocean_x, ocean_y, ocean_temp, thick, grounded_mask, wet_mask, ice_links, ocean_links,
):
    n_wide, n_narrow = lax.axis_size("wide"), lax.axis_size("narrow")
    rows, layers, columns = ice_x.shape
    levels = ocean_x.shape[1]
    layer_rows = pad8(layers)
    cap = max(1, 2 * rows // n_wide)
    block = pad8(max(4 * cap, 3 * cap + 2))
    assert columns == LANES and ice_links.shape[0] == rows
    whole = pl.BlockSpec(memory_space=pltpu.VMEM)
    anywhere = pl.BlockSpec(memory_space=pl.ANY)

    def edge_row(i):
        return pl.BlockSpec((1, levels, columns), lambda _: (i, 0, 0))

    message, plane_t = pl.pallas_call(
        edges_kernel,
        name="edges",
        out_shape=(
            jax.ShapeDtypeStruct((levels + 3 * layer_rows + rows, LANES), F32),
            jax.ShapeDtypeStruct((rows, LANES), F32),
        ),
        in_specs=[whole] * 3 + [anywhere] * 3 + [whole] * 5,
        out_specs=(whole, whole),
        scratch_shapes=[
            pltpu.VMEM((3, rows, levels, columns), F32),
            pltpu.SemaphoreType.DMA((3, 2)),
        ],
        compiler_params=VMEM,
    )(ice_x, ice_y, ice_temp, ocean_x, ocean_y, ocean_temp, thick, grounded_mask, wet_mask, ice_links, ocean_links)
    if n_narrow == 2:
        parts = [lax.ppermute(message, "narrow", [(0, 1), (1, 0)])]
    else:
        ahead = [(i, i + 1) for i in range(n_narrow - 1)]
        parts = [
            lax.ppermute(message, "narrow", [(j, i) for i, j in ahead]),
            lax.ppermute(message, "narrow", ahead),
        ]
    tall = 3 * levels + 3 * HALO * layer_rows + 3 * layer_rows + 4 * PLANE_ROWS
    to_down, to_up, blocks = pl.pallas_call(
        functools.partial(send_kernel, n_wide, n_narrow, cap, block, len(parts), levels),
        name="send",
        out_shape=(
            jax.ShapeDtypeStruct((tall, LANES), F32),
            jax.ShapeDtypeStruct((tall, LANES), F32),
            jax.ShapeDtypeStruct((n_wide, 3 * block, LANES), F32),
        ),
        in_specs=[whole] * (len(parts) + 3)
        + [edge_row(0), edge_row(rows - 1)] * 3
        + [whole] * 6,
        out_specs=(whole,) * 3,
        grid=(1,),
        compiler_params=VMEM,
    )(
        *parts, ice_x, ice_y, ice_temp, ocean_x, ocean_x, ocean_y, ocean_y, ocean_temp, ocean_temp,
        plane_t, thick, grounded_mask, wet_mask, ice_links, ocean_links,
    )
    blocks = lax.all_to_all(blocks, "wide", split_axis=0, concat_axis=0, tiled=True)
    ahead = [(i, i + 1) for i in range(n_wide - 1)]
    up = lax.ppermute(to_down, "wide", ahead)
    down = lax.ppermute(to_up, "wide", [(j, i) for i, j in ahead])
    chunks = 2
    ocean = pl.pallas_call(
        functools.partial(ocean_kernel, n_narrow, len(parts)),
        name="ocean",
        out_shape=jax.ShapeDtypeStruct((3, rows, levels, columns), F32),
        in_specs=[whole] * len(parts) + [anywhere] * 3 + [whole] * 3,
        out_specs=anywhere,
        scratch_shapes=[
            pltpu.VMEM((6, rows + 2, levels, columns), F32),
            pltpu.VMEM((5, rows, LANES), F32),
            pltpu.SemaphoreType.DMA((3, chunks)),
            pltpu.SemaphoreType.DMA((3, chunks)),
        ],
        compiler_params=VMEM,
        cost_estimate=pl.CostEstimate(flops=10_000_000, bytes_accessed=8_000_000, transcendentals=0),
    )(*parts, ocean_x, ocean_y, ocean_temp, up, down, wet_mask)
    n_ice = rows + 2 * HALO
    n_tall = rows + 2 * PLANE_ROWS
    wide = 2 * LANES
    return pl.pallas_call(
        functools.partial(final_kernel, n_wide, n_narrow, cap, block, len(parts), levels),
        name="final",
        out_shape=(
            jax.ShapeDtypeStruct((3, rows, layers, columns), F32),
            jax.ShapeDtypeStruct((3, rows, levels, columns), F32),
            jax.ShapeDtypeStruct((rows, columns), F32),
            jax.ShapeDtypeStruct((rows, columns), F32),
        ),
        in_specs=[whole] * (len(parts) + 11) + [anywhere],
        out_specs=(whole, anywhere, whole, whole),
        input_output_aliases={len(parts) + 11: 1},
        scratch_shapes=[
            pltpu.VMEM((2 * PICARD, n_ice, layer_rows, wide), F32),
            pltpu.VMEM((n_ice, layer_rows, wide), F32),
            pltpu.VMEM((n_ice, layer_rows, wide), F32),
            pltpu.VMEM((2, n_ice, layer_rows, wide), F32),
            pltpu.VMEM((2, n_ice, layer_rows, wide), F32),
            pltpu.VMEM((n_ice, layer_rows, LANES), F32),
            pltpu.VMEM((4, n_tall, wide), F32),
            pltpu.VMEM((rows, 8, LANES), F32),
            pltpu.SemaphoreType.DMA((2,)),
        ],
        compiler_params=VMEM,
    )(*parts, ice_x, ice_y, ice_temp, up, down, blocks, thick, grounded_mask, wet_mask, ice_links, ocean_links, ocean)


def solution(mesh):
    column = P("wide", None, "narrow")
    plane = P("wide", "narrow")
    return jax.shard_map(
        local,
        mesh=mesh,
        in_specs=(column,) * 6 + (plane,) * 5,
        out_specs=(P(None, "wide", None, "narrow"), P(None, "wide", None, "narrow"), plane, plane),
        check_vma=False,
    )
```

```python
import functools

import jax
import jax.numpy as jnp
from jax import lax
from jax.experimental import pallas as pl
from jax.experimental.pallas import tpu as pltpu
from jax.sharding import PartitionSpec as P

PICARD = 2
DIFFUSE = 0.2
GAMMA_MELT = 0.5
TIME_STEP = 0.05
SLOPE_SCALE = 0.1
STRAIN_FLOOR = 0.01
HEATING_RATE = 0.01

LANES = 128
TILE = 8
HALO = 4
RIM = 3
VMEM = pltpu.CompilerParams(vmem_limit_bytes=48 * 1024 * 1024)
HIGHEST = lax.Precision.HIGHEST
F32 = jnp.float32

THICK, GROUNDED, OCEAN_T, WET, ICE_LINK, OCEAN_LINK, OWN_LINK = range(7)
PLANES = 6
PART, EDGE_T0, EDGE_T1, EDGE_W0, PART_WET, EDGE_W1 = range(6)


def iota(shape, axis):
    return lax.broadcasted_iota(jnp.int32, shape, axis)


def right_lanes(period):
    lane = iota((1, LANES), 1)
    return lane % period < HALO


def left_lanes(period):
    lane = iota((1, LANES), 1)
    return lane % period >= period - HALO


def spread(column, count=LANES):
    rows = column.shape[0]
    eye = iota((rows, count), 0) == iota((rows, count), 1)
    return jnp.sum(jnp.where(eye, column, 0.0), axis=0, keepdims=True)


def upright(row):
    count = row.shape[1]
    eye = iota((count, count), 0) == iota((count, count), 1)
    return jnp.sum(jnp.where(eye, row, 0.0), axis=1, keepdims=True)


def turn(value, shift, axis):
    shift %= value.shape[axis]
    return pltpu.roll(value, shift, axis) if shift else value


def fetch_all(pairs, sems):
    copies = [pltpu.make_async_copy(a, b, sems.at[i]) for i, (a, b) in enumerate(pairs)]
    for copy in copies:
        copy.start()
    return copies


def divide(whole, part):
    return jnp.floor((whole + 0.5) * (1.0 / part))


def dot(a, b):
    return jnp.dot(a, b, precision=HIGHEST, preferred_element_type=F32)


def narrow_sides(n_narrow):
    place = lax.axis_index("narrow")
    return place < n_narrow - 1, place > 0


def merged(parts, right, left, n_narrow):
    has_right, has_left = narrow_sides(n_narrow)
    from_right, from_left = parts[0], parts[-1]
    if len(parts) == 1:
        keep = (right & has_right) | (left & has_left)
        return jnp.where(keep, from_right, 0.0)
    return jnp.where(right, from_right, jnp.where(left, from_left, 0.0))


def ice_group(index):
    return divmod(index, LANES // 8)


def edges_kernel(
    ice_x, ice_y, ice_t, ocean_t, thick, grounded, wet, ice_links, ocean_links,
    out, planes, ice, top, thick_v, grounded_v, wet_v, links_v, sems,
):
    layers, rows, _ = ice_x.shape
    copies = fetch_all(
        (
            (thick, thick_v),
            (grounded, grounded_v),
            (wet, wet_v),
            (ice_links, links_v.at[0]),
            (ocean_links, links_v.at[1]),
            (ocean_t.at[:, pl.ds(0, TILE), :], top),
            (ice_x, ice.at[0]),
            (ice_y, ice.at[1]),
            (ice_t, ice.at[2]),
        ),
        sems,
    )
    lane = iota((1, LANES), 1)
    for copy in copies[:6]:
        copy.wait()
    planes[THICK] = thick_v[...]
    planes[GROUNDED] = grounded_v[...].astype(F32)
    for i in range(rows):
        planes[OCEAN_T, i : i + 1, :] = top[i, 0:1, :]
    planes[WET] = wet_v[...].astype(F32)
    for k in range(2):
        link = upright(links_v[k].astype(F32)) + 1.0
        planes[ICE_LINK + k] = jnp.broadcast_to(link, (rows, LANES))
    total = jnp.zeros((rows, LANES), F32)
    for j in range(PLANES):
        total = jnp.where((lane + HALO) % LANES // 16 == j, turn(planes[j], 16 * j, 1), total)
    out[0] = total
    for copy in copies[6:]:
        copy.wait()
    tiles = {}
    for index in range(3 * layers):
        tile, group = ice_group(index)
        turned = turn(ice[index // layers, index % layers], 8 * group, 1)
        before = tiles.get(tile, jnp.zeros((rows, LANES), F32))
        tiles[tile] = jnp.where((lane + HALO) % LANES // 8 == group, turned, before)
    for tile, value in tiles.items():
        out[1 + tile] = value


def plane_halo(block, group):
    lane = iota((1, LANES), 1)
    turned = turn(block, -16 * group, 1)
    return jnp.where((lane < HALO) | (lane >= LANES - HALO), turned, 0.0)


def mix_kernel(
    ocean_x, ocean_y, ocean_t, ice_x, ice_y, ice_t, planes,
    out, strip, up, down, held, ice, ocean_sems, ice_sems,
):
    rows, levels, _ = ocean_x.shape
    layers = ice_x.shape[0]
    chunks = ocean_sems.shape[0] // 3
    step = rows // chunks
    pairs = [
        (field.at[pl.ds(h * step, step)], held.at[f, pl.ds(h * step, step)])
        for f, field in enumerate((ocean_x, ocean_y, ocean_t))
        for h in range(chunks)
    ]
    copies = fetch_all(pairs, ocean_sems)
    ice_copies = fetch_all([(a, ice.at[f]) for f, a in enumerate((ice_x, ice_y, ice_t))], ice_sems)
    lane = iota((1, LANES), 1)
    row = iota((rows, LANES), 0)
    wet = planes[WET]
    around = (
        jnp.where(row > 0, turn(wet, 1, 0), 0.0),
        jnp.where(row < rows - 1, turn(wet, -1, 0), 0.0),
        jnp.where(lane > 0, turn(wet, 1, 1), 0.0),
        jnp.where(lane < LANES - 1, turn(wet, -1, 1), 0.0),
    )
    scale = DIFFUSE * wet
    coef = [scale * value for value in around]
    centre_coef = 1.0 - (coef[0] + coef[1] + coef[2] + coef[3])
    total = jnp.zeros((levels, LANES), F32)
    for f in range(3):
        for h in range(chunks):
            copies[f * chunks + h].wait()
        for i in range(rows):
            j = f * rows + i
            centre = held[f, i]
            total = jnp.where((lane + 1) % LANES // 2 == j, turn(centre, 2 * j, 1), total)
            value = centre * centre_coef[i : i + 1, :]
            value = value + turn(centre, 1, 1) * coef[2][i : i + 1, :]
            value = value + turn(centre, -1, 1) * coef[3][i : i + 1, :]
            if i > 0:
                value = value + held[f, i - 1] * coef[0][i : i + 1, :]
            if i < rows - 1:
                value = value + held[f, i + 1] * coef[1][i : i + 1, :]
            out[f, i] = value
        up[f * levels : (f + 1) * levels, :] = held[f, rows - 1]
        down[f * levels : (f + 1) * levels, :] = held[f, 0]
    strip[...] = total
    for copy in ice_copies:
        copy.wait()
    at = 3 * levels
    upper = iota((TILE, 1), 0) >= HALO
    half = ice_pairs(layers)
    for m in range(half):
        ends = []
        for index in (m, m + half):
            index = min(index, 3 * layers - 1)
            f, k = divmod(index, layers)
            ends.append((ice[f, k, rows - TILE :, :], ice[f, k, :TILE, :]))
        up[at : at + TILE, :] = jnp.where(upper, ends[0][0], turn(ends[1][0], HALO, 0))
        down[at : at + TILE, :] = jnp.where(upper, turn(ends[1][1], HALO, 0), ends[0][1])
        at += TILE
    for j in (THICK, GROUNDED, WET):
        up[at : at + TILE, :] = planes[j, rows - TILE :, :]
        down[at : at + TILE, :] = planes[j, :TILE, :]
        at += TILE


def ice_pairs(layers):
    return -(-3 * layers // 2)


def ranks(own_col, member_col, order_sub, order_lane, own_row):
    hits = (own_col == own_row) & member_col & (order_sub < order_lane)
    return jnp.sum(hits.astype(F32), axis=0, keepdims=True)


def ocean_slots(link_col, rows, n_wide, cap, block):
    link_row = spread(link_col)
    parts = []
    for link in (link_col, link_row):
        number = link - 1.0
        tile = divide(number, rows)
        inner = number - tile * rows
        ok = link > 0.5
        parts.append(
            (
                tile,
                (
                    ok,
                    ok & (inner >= rows - RIM) & (tile < n_wide - 1.5),
                    ok & (inner < RIM) & (tile > 0.5),
                ),
            )
        )
    (tile_col, member_col), (tile_row, member_row) = parts
    order_sub, order_lane = iota((rows, LANES), 0), iota((rows, LANES), 1)
    place = iota((n_wide * block, LANES), 0).astype(F32)
    total = jnp.zeros((n_wide * block, LANES), F32)
    for k, shift in enumerate((0.0, 1.0, -1.0)):
        rank = ranks(tile_col, member_col[k], order_sub, order_lane, tile_row)
        target = jnp.where(
            member_row[k], (tile_row + shift) * block + (k * cap + rank), -1.0
        )
        total = total + (place == target).astype(F32)
    return total[:, :rows]


def draft_slots(link_col, rows, n_wide, cap, block):
    link_row = spread(link_col)
    tile_col, tile_row = divide(link_col - 1.0, rows), divide(link_row - 1.0, rows)
    order_sub, order_lane = iota((rows, LANES), 0), iota((rows, LANES), 1)
    rank = ranks(tile_col, link_col > 0.5, order_sub, order_lane, tile_row)
    target = jnp.where(link_row > 0.5, tile_row * block + (3 * cap + rank), -1.0)
    place = iota((n_wide * block, LANES), 0).astype(F32)
    return (place == target).astype(F32)[:, :rows]


def send_kernel(
    n_wide, n_narrow, cap, block, n_parts, own_rows,
    *refs,
):
    parts, refs = refs[:n_parts], refs[n_parts:]
    planes, up_own, down_own, up, down, blocks = refs
    rows = planes.shape[1]
    lane = iota((1, LANES), 1)
    plane_block = merged([p[0] for p in parts], right_lanes(16), left_lanes(16), n_narrow)
    link_own = planes[ICE_LINK]
    sent_block = jnp.where((lane + HALO) % LANES // 16 == OWN_LINK, link_own, plane_block)
    thick_plane, grounded_plane, wet_plane = planes[THICK], planes[GROUNDED], planes[WET]
    up[0:own_rows, :] = up_own[...]
    down[0:own_rows, :] = down_own[...]
    strips = [
        merged([p[1 + t] for p in parts], right_lanes(8), left_lanes(8), n_narrow)
        for t in range(parts[0].shape[0] - 1)
    ]
    at = own_rows
    for value in (sent_block, *strips):
        up[at : at + TILE, :] = value[rows - TILE :, :]
        down[at : at + TILE, :] = value[:TILE, :]
        at += TILE
    wet_all = jnp.concatenate([wet_plane, plane_halo(plane_block, WET)], axis=1)
    warm = wet_all * jnp.concatenate([planes[OCEAN_T], plane_halo(plane_block, OCEAN_T)], axis=1)
    width = 2 * LANES
    row = iota((rows, width), 0)
    sums = []
    for value in (wet_all, warm):
        total = pltpu.roll(value, 1, 1) + pltpu.roll(value, width - 1, 1)
        total = total + jnp.where(row > 0, pltpu.roll(value, 1, 0), 0.0)
        sums.append(total + jnp.where(row < rows - 1, pltpu.roll(value, rows - 1, 0), 0.0))
    mixed = warm + DIFFUSE * (wet_all * sums[1] - warm * sums[0])
    draft = 0.9 * thick_plane * (1.0 - grounded_plane)
    own_slots = ocean_slots(planes[OCEAN_LINK][:, 0:1], rows, n_wide, cap, block)
    main = dot(own_slots, jnp.concatenate([mixed[:, :LANES], wet_plane], axis=1))
    count = n_wide * block
    slot = iota((count, 1), 0) % block
    first = main[:, :LANES] + dot(draft_slots(link_own[:, 0:1], rows, n_wide, cap, block), draft)
    second = jnp.where(
        slot == 3 * cap,
        wet_plane[0:1, :],
        jnp.where(slot == 3 * cap + 1, wet_plane[rows - 1 : rows, :], main[:, LANES:]),
    )
    edge = (lane < HALO) | (lane >= LANES - HALO)
    mixed_edge = jnp.where(edge, mixed[:, LANES:], 0.0)
    wet_edge = wet_all[:, LANES:]
    warm_edge = warm[:, LANES:]
    packed = mixed_edge + pltpu.roll(wet_edge, 16 * PART_WET, 1)
    links = plane_halo(plane_block, OCEAN_LINK)
    if n_narrow == 2:
        third = dot(
            ocean_slots(jnp.max(links, axis=1, keepdims=True), rows, n_wide, cap, block), packed
        )
    else:
        third = dot(
            ocean_slots(links[:, 0:1], rows, n_wide, cap, block),
            jnp.where(right_lanes(16), packed, 0.0),
        ) + dot(
            ocean_slots(links[:, LANES - 1 : LANES], rows, n_wide, cap, block),
            jnp.where(left_lanes(16), packed, 0.0),
        )
    last = rows - 1
    ends = (
        pltpu.roll(warm_edge[0:1, :], 16 * EDGE_T0, 1)
        + pltpu.roll(warm_edge[last:, :], 16 * EDGE_T1, 1)
        + pltpu.roll(wet_edge[0:1, :], 16 * EDGE_W0, 1)
        + pltpu.roll(wet_edge[last:, :], 16 * EDGE_W1, 1)
    )
    third = jnp.where(
        slot == 3 * cap,
        warm[0:1, :LANES],
        jnp.where(slot == 3 * cap + 1, warm[last:, :LANES], third + ends),
    )
    for k, value in enumerate((first, second, third)):
        blocks[:, k * block : (k + 1) * block, :] = value.reshape(n_wide, block, LANES)


def patch_kernel(
    n_narrow, n_strips, n_parts,
    *refs,
):
    strips, refs = refs[:n_strips], refs[n_strips:]
    parts, refs = refs[:n_parts], refs[n_parts:]
    mixed, own, up_own, down_own, up, down, planes, out, held, sems = refs
    _, rows, levels, _ = mixed.shape
    chunks = sems.shape[0] // 3
    step = rows // chunks
    lane = iota((1, LANES), 1)
    first, last = lane == 0, lane == LANES - 1
    wet = planes[WET]
    wet_at = up_own.shape[0] - TILE
    block = merged([p[0] for p in parts], right_lanes(16), left_lanes(16), n_narrow)
    wet_halo = plane_halo(block, WET)
    weight = DIFFUSE * wet * jnp.where(first, turn(wet_halo, 1, 1), turn(wet_halo, -1, 1))
    weight = jnp.where(first | last, weight, 0.0)
    even = lane % 2 == 0
    packed_weight = jnp.zeros((1, LANES), F32)
    for j in range(3 * rows):
        i = j % rows
        packed_weight = packed_weight + turn(weight[i : i + 1, :], 2 * j, 1)
    came = merged([p[...] for p in strips], even, ~even, n_narrow)
    extra = packed_weight * (jnp.where(even, turn(came, 1, 1), turn(came, -1, 1)) - own[...])
    above = DIFFUSE * wet[0:1, :] * up[wet_at + TILE - 1 : wet_at + TILE, :]
    below = DIFFUSE * wet[rows - 1 : rows, :] * down[wet_at : wet_at + 1, :]
    edge = first | last
    writes = []
    for f in range(3):
        for h in range(chunks):
            for i in range(h * step, (h + 1) * step):
                value = mixed[f, i] + jnp.where(edge, turn(extra, -2 * (f * rows + i), 1), 0.0)
                part = pl.ds(f * levels, levels)
                if i == 0:
                    value = value + above * (up[part, :] - down_own[part, :])
                if i == rows - 1:
                    value = value + below * (down[part, :] - up_own[part, :])
                held[f, i] = value
            part = pl.ds(h * step, step)
            writes.append(
                pltpu.make_async_copy(
                    held.at[f, part], out.at[f, part], sems.at[f * chunks + h]
                )
            )
            writes[-1].start()
    for copy in writes:
        copy.wait()


def ice_slots(link_col, kind_col, rows, cap, block, count, n_wide):
    link_row = spread(link_col)
    kind_row = spread(kind_col)
    number = link_col - 1.0
    tile = divide(number, rows)
    inner = number - tile * rows
    tile_row = divide(link_row - 1.0, rows)
    ok = (link_col > 0.5) & (kind_col > -0.5)
    ok_row = (link_row > 0.5) & (kind_row > -0.5)
    hits = (tile == tile_row) & (kind_col == kind_row) & ok_row & (link_row < link_col)
    rank = jnp.sum(hits.astype(F32), axis=1, keepdims=True)
    place = iota((link_col.shape[0], count), 1).astype(F32)

    def hot(keep, target):
        return (place == jnp.where(keep, target, -1.0)).astype(F32)

    top, bottom = inner < 0.5, inner > rows - 1.5
    edge = ok & (top | bottom)
    near = jnp.where(top, tile - 1.0, tile + 1.0)
    near_ok = edge & (near > -0.5) & (near < n_wide - 0.5)
    slot = hot(ok, tile * block + kind_col * cap + rank)
    near_edge = hot(near_ok, near * block + jnp.where(top, 3.0 * cap + 1.0, 3.0 * cap))
    own_edge = hot(edge, tile * block + jnp.where(top, 3.0 * cap, 3.0 * cap + 1.0))
    near_slot = hot(near_ok, near * block)
    own_slot = hot(edge, tile * block)
    return slot, near_edge, own_edge, near_slot, own_slot, top


def final_kernel(
    n_wide, n_narrow, cap, block, n_parts, levels, own_rows,
    *refs,
):
    parts, refs = refs[:n_parts], refs[n_parts:]
    (
        ice_x, ice_y, ice_t, up, down, blocks, planes, ocean_in,
        ice_out, ocean_out, thick_out, melt_out,
        ice, vel, rate, flat, top_level, sems,
    ) = refs
    layers, rows, _ = ice_x.shape
    copies = fetch_all(
        (
            (ocean_in.at[2, :, pl.ds(0, TILE), :], top_level),
            (ice_x, ice.at[0]),
            (ice_y, ice.at[1]),
            (ice_t, ice.at[2]),
        ),
        sems,
    )
    width = 2 * LANES
    tall = rows + TILE
    lane = iota((1, LANES), 1)
    wide_lane = iota((1, width), 1)
    place_wide = lax.axis_index("wide")
    has_right, has_left = narrow_sides(n_narrow)
    has_up, has_down = place_wide > 0, place_wide < n_wide - 1
    under = iota((TILE, 1), 0) < HALO
    ice_at = 3 * levels
    plane_at = own_rows - 3 * TILE

    def rim(at):
        part = pl.ds(at, TILE)
        return jnp.where(under, down[part, :], up[part, :])

    def extended(value, at):
        return jnp.concatenate([value, rim(at)], axis=0)

    plane_block = merged([p[0] for p in parts], right_lanes(16), left_lanes(16), n_narrow)
    block_tall = extended(plane_block, own_rows)
    thick_tall = jnp.concatenate(
        [extended(planes[THICK], plane_at), plane_halo(block_tall, THICK)], axis=1
    )
    grounded_tall = jnp.concatenate(
        [extended(planes[GROUNDED], plane_at + TILE), plane_halo(block_tall, GROUNDED)], axis=1
    )
    tall_row = iota((tall, 1), 0)
    kind = jnp.where(
        tall_row < rows,
        0.0,
        jnp.where(tall_row < rows + RIM, 2.0, jnp.where(tall_row >= tall - RIM, 1.0, -1.0)),
    )
    count = n_wide * block
    first = blocks[:, 0:block, :].reshape(count, LANES)
    second = blocks[:, block : 2 * block, :].reshape(count, LANES)
    third = blocks[:, 2 * block : 3 * block, :].reshape(count, LANES)
    own_link = jnp.concatenate(
        [
            planes[ICE_LINK][:, 0:1],
            rim(own_rows)[:, 16 * OWN_LINK : 16 * OWN_LINK + 1],
        ],
        axis=0,
    )
    slot, near_edge, own_edge, _, _, _ = ice_slots(
        own_link, kind, rows, cap, block, count, n_wide
    )
    got = dot(slot, jnp.concatenate([first, second], axis=1))
    near = dot(near_edge, jnp.concatenate([second, third], axis=1))
    own = dot(own_edge, third)
    wet_main = got[:, LANES:]
    mixed_main = got[:, :LANES] + DIFFUSE * (
        wet_main * near[:, LANES:] - near[:, :LANES] * own
    )

    def halo_melt(link_col):
        slot, _, _, near_slot, own_slot, top = ice_slots(
            link_col, kind, rows, cap, block, count, n_wide
        )
        got = dot(slot, third)
        near = dot(near_slot, third)
        own = dot(own_slot, third)

        def group(value, j):
            return pltpu.roll(value, LANES - 16 * j, 1) if j else value

        wet_got = group(got, PART_WET)
        near_warm = jnp.where(top, group(near, EDGE_T1), group(near, EDGE_T0))
        near_wet = jnp.where(top, group(near, EDGE_W1), group(near, EDGE_W0))
        own_warm = jnp.where(top, group(own, EDGE_T0), group(own, EDGE_T1))
        return got + DIFFUSE * (wet_got * near_warm - near_wet * own_warm), wet_got

    links = plane_halo(block_tall, ICE_LINK)
    if n_narrow == 2:
        mixed_side, wet_side = halo_melt(jnp.max(links, axis=1, keepdims=True))
    else:
        mixed_side, wet_side = (
            jnp.where(lane < HALO, a, b)
            for a, b in zip(halo_melt(links[:, 0:1]), halo_melt(links[:, LANES - 1 : LANES]))
        )
    mixed_tall = jnp.concatenate([mixed_main, mixed_side], axis=1)
    wet_tall = jnp.concatenate([wet_main, wet_side], axis=1)
    inside = (
        ((tall_row < rows) | ((tall_row < rows + HALO) & has_down) | ((tall_row >= rows + HALO) & has_up))
        & (
            (wide_lane < LANES)
            | ((wide_lane < LANES + HALO) & has_right)
            | ((wide_lane >= width - HALO) & has_left)
        )
    ).astype(F32)
    open_ice = 1.0 - grounded_tall
    draft_tall = 0.9 * thick_tall * open_ice
    melt_tall = GAMMA_MELT * (mixed_tall - wet_tall * (0.0832 - 0.761 * draft_tall))
    new_thick = (thick_tall - TIME_STEP * melt_tall * open_ice) * inside
    thick_out[...] = new_thick[:rows, :LANES]
    surface = new_thick * (0.1 + 0.9 * grounded_tall)
    push_scale = (-0.5 * SLOPE_SCALE) * new_thick
    flat[0] = push_scale * (turn(surface, -1, 0) - turn(surface, 1, 0))
    flat[1] = push_scale * (turn(surface, -1, 1) - turn(surface, 1, 1))
    flat[2] = 0.1 + 9.9 * grounded_tall
    flat[3] = inside
    ocean_link = planes[OCEAN_LINK][:, 0:1]
    ocean_row = spread(ocean_link)
    tile = divide(ocean_link - 1.0, rows)
    tile_row = divide(ocean_row - 1.0, rows)
    hits = (tile == tile_row) & (ocean_row > 0.5) & (ocean_row < ocean_link)
    rank = jnp.sum(hits.astype(F32), axis=1, keepdims=True)
    coupled = ocean_link > 0.5
    target = jnp.where(coupled, tile * block + 3 * cap + rank, -1.0)
    ocean_draft = dot((iota((rows, count), 1).astype(F32) == target).astype(F32), first)
    copies[0].wait()
    heat_top = jnp.concatenate([top_level[i, 0:1, :] for i in range(rows)], axis=0)
    melt = (
        GAMMA_MELT
        * (heat_top - (0.0832 - 0.761 * ocean_draft))
        * planes[WET]
        * coupled.astype(F32)
    )
    melt_out[...] = melt
    new_top = heat_top - 0.2 * melt
    for i in range(rows):
        top_level[i, 0:1, :] = new_top[i : i + 1, :]
    store = pltpu.make_async_copy(top_level, ocean_out.at[2, :, pl.ds(0, TILE), :], sems.at[4])
    store.start()
    strips = [
        extended(
            merged([p[1 + t] for p in parts], right_lanes(8), left_lanes(8), n_narrow),
            own_rows + (1 + t) * TILE,
        )
        for t in range(parts[0].shape[0] - 1)
    ]
    edge = (lane < HALO) | (lane >= LANES - HALO)
    half = ice_pairs(layers)
    for copy in copies[1:]:
        copy.wait()
    for index in range(3 * layers):
        f, k = divmod(index, layers)
        beyond = rim(ice_at + index % half * TILE)
        if index >= half:
            part = pl.ds(ice_at + index % half * TILE, TILE)
            beyond = turn(jnp.where(under, up[part, :], down[part, :]), HALO, 0)
        tile, group = ice_group(index)
        beside = jnp.where(edge, turn(strips[tile], -8 * group, 1), 0.0)
        value = jnp.concatenate(
            [jnp.concatenate([ice[f, k], beyond], axis=0), beside], axis=1
        )
        if f < 2:
            vel[f, k] = value
        else:
            rate[k] = jnp.exp(0.25 * value) * inside

    def around(value):
        return turn(value, 1, 0) + turn(value, -1, 0) + turn(value, 1, 1) + turn(value, -1, 1)

    for sweep in range(PICARD):
        last = sweep == PICARD - 1
        for k in range(layers):
            u, v = vel[2 * sweep, k], vel[2 * sweep + 1, k]
            ends = [
                [turn(w, s, axis) for axis in (0, 1) for s in (-1, 1)] for w in (u, v)
            ]
            ux, uy = ends[0][0] - ends[0][1], ends[0][2] - ends[0][3]
            vx, vy = ends[1][0] - ends[1][1], ends[1][2] - ends[1][3]
            cross = uy + vx
            eps2 = ux * (ux + vy) + vy * vy + 0.25 * (cross * cross)
            if k < layers - 1:
                uz, vz = vel[2 * sweep, k + 1] - u, vel[2 * sweep + 1, k + 1] - v
                eps2 = eps2 + (uz * uz + vz * vz)
            eps2 = 0.25 * eps2
            eta = rate[k] * jnp.exp((-1.0 / 3.0) * jnp.log(eps2 + STRAIN_FLOOR))
            links_up_down = float((k > 0) + (k < layers - 1))
            diagonal = eta * (2.0 + links_up_down) + 0.5 * around(eta) + flat[2]
            if last:
                diagonal = diagonal[:rows, :LANES]
            inverse = 1.0 / diagonal
            for f, w in enumerate((u, v)):
                total = 0.5 * (ends[f][0] + ends[f][1] + ends[f][2] + ends[f][3])
                if k > 0:
                    total = total + vel[2 * sweep + f, k - 1]
                if k < layers - 1:
                    total = total + vel[2 * sweep + f, k + 1]
                total = eta * total + 0.5 * around(eta * w) + flat[f]
                if last:
                    ice_out[f, k] = total[:rows, :LANES] * inverse
                else:
                    vel[2 * sweep + 2 + f, k] = total * inverse * flat[3]
            if last:
                ice_out[2, k] = ice[2, k] + HEATING_RATE * (eta * eps2)[:rows, :LANES]
    store.wait()


def local(
    ice_x, ice_y, ice_temp, ocean_x, ocean_y, ocean_temp, thick, grounded_mask, wet_mask, ice_links, ocean_links,
):
    n_wide, n_narrow = lax.axis_size("wide"), lax.axis_size("narrow")
    rows, layers, columns = ice_x.shape
    levels = ocean_x.shape[1]
    cap = max(1, 2 * rows // n_wide)
    block = -(-max(4 * cap, 3 * cap + 2) // TILE) * TILE
    assert columns == LANES and ice_links.shape[0] == rows
    ice_fields = [x.transpose(1, 0, 2) for x in (ice_x, ice_y, ice_temp)]
    links = [x.reshape(1, rows) for x in (ice_links, ocean_links)]
    fields = [ocean_x, ocean_y, ocean_temp]
    here = pl.BlockSpec(memory_space=pltpu.VMEM)
    far = pl.BlockSpec(memory_space=pltpu.HBM)

    def array(*shape):
        return jax.ShapeDtypeStruct(shape, F32)

    def cost(microseconds):
        return pl.CostEstimate(
            flops=0, bytes_accessed=int(microseconds * 3.0e6), transcendentals=0
        )

    n_tiles = ice_group(3 * layers - 1)[0] + 1
    dma = pltpu.SemaphoreType.DMA
    message, planes = pl.pallas_call(
        edges_kernel,
        name="edges",
        out_shape=(array(1 + n_tiles, rows, LANES), array(PLANES, rows, LANES)),
        in_specs=[far] * 9,
        out_specs=(here, here),
        scratch_shapes=[
            pltpu.VMEM((3, layers, rows, LANES), F32),
            pltpu.VMEM((rows, TILE, LANES), F32),
            pltpu.VMEM((rows, LANES), F32),
            pltpu.VMEM((rows, LANES), jnp.int32),
            pltpu.VMEM((rows, LANES), jnp.int32),
            pltpu.VMEM((2, 1, rows), jnp.int32),
            dma((9,)),
        ],
        compiler_params=VMEM,
        cost_estimate=cost(1.5),
    )(*ice_fields, ocean_temp, thick, grounded_mask, wet_mask, *links)

    def narrow(value):
        if n_narrow == 2:
            return [lax.ppermute(value, "narrow", [(0, 1), (1, 0)])]
        ahead = [(i, i + 1) for i in range(n_narrow - 1)]
        return [
            lax.ppermute(value, "narrow", [(j, i) for i, j in ahead]),
            lax.ppermute(value, "narrow", ahead),
        ]

    parts = narrow(message)
    n_parts = len(parts)
    own_rows = 3 * levels + ice_pairs(layers) * TILE + 3 * TILE
    chunks = 2
    mixed, own_strip, up_own, down_own = pl.pallas_call(
        mix_kernel,
        name="mix",
        out_shape=(
            array(3, rows, levels, LANES), array(levels, LANES), array(own_rows, LANES), array(own_rows, LANES),
        ),
        in_specs=[far] * 6 + [here],
        out_specs=(here,) * 4,
        scratch_shapes=[
            pltpu.VMEM((3, rows, levels, LANES), F32),
            pltpu.VMEM((3, layers, rows, LANES), F32),
            dma((3 * chunks,)),
            dma((3,)),
        ],
        compiler_params=VMEM,
        cost_estimate=cost(3.0),
    )(*fields, *ice_fields, planes)
    total_rows = own_rows + (1 + n_tiles) * TILE
    to_down, to_up, blocks = pl.pallas_call(
        functools.partial(send_kernel, n_wide, n_narrow, cap, block, n_parts, own_rows),
        name="send",
        out_shape=(
            array(total_rows, LANES), array(total_rows, LANES), array(n_wide, 3 * block, LANES),
        ),
        in_specs=[here] * (n_parts + 3),
        out_specs=(here,) * 3,
        compiler_params=VMEM,
        cost_estimate=cost(1.3),
    )(*parts, planes, up_own, down_own)
    blocks = lax.all_to_all(blocks, "wide", split_axis=0, concat_axis=0, tiled=True)
    ahead = [(i, i + 1) for i in range(n_wide - 1)]
    up = lax.ppermute(to_down, "wide", ahead)
    down = lax.ppermute(to_up, "wide", [(j, i) for i, j in ahead])
    strips = narrow(own_strip)
    ocean = pl.pallas_call(
        functools.partial(patch_kernel, n_narrow, len(strips), n_parts),
        name="patch",
        out_shape=array(3, rows, levels, LANES),
        in_specs=[here] * (len(strips) + n_parts + 7),
        out_specs=far,
        scratch_shapes=[
            pltpu.VMEM((3, rows, levels, LANES), F32),
            dma((3 * chunks,)),
        ],
        compiler_params=VMEM,
        cost_estimate=cost(2.0),
    )(*strips, *parts, mixed, own_strip, up_own, down_own, up, down, planes)
    wide = 2 * LANES
    tall = rows + TILE
    ice, ocean, thick_out, melt_out = pl.pallas_call(
        functools.partial(
            final_kernel, n_wide, n_narrow, cap, block, n_parts, levels, own_rows
        ),
        name="final",
        out_shape=(
            array(3, layers, rows, LANES), array(3, rows, levels, LANES), array(rows, LANES), array(rows, LANES),
        ),
        in_specs=[here] * n_parts + [far] * 3 + [here] * 4 + [far],
        out_specs=(here, far, here, here),
        input_output_aliases={n_parts + 7: 1},
        scratch_shapes=[
            pltpu.VMEM((3, layers, rows, LANES), F32),
            pltpu.VMEM((2 * PICARD, layers, tall, wide), F32),
            pltpu.VMEM((layers, tall, wide), F32),
            pltpu.VMEM((4, tall, wide), F32),
            pltpu.VMEM((rows, TILE, LANES), F32),
            dma((5,)),
        ],
        compiler_params=VMEM,
        cost_estimate=cost(7.0),
    )(*parts, *ice_fields, up, down, blocks, planes, ocean)
    return ice.transpose(0, 2, 1, 3), ocean, thick_out, melt_out


def solution(mesh):
    column = P("wide", None, "narrow")
    plane = P("wide", "narrow")
    return jax.shard_map(
        local,
        mesh=mesh,
        in_specs=(column,) * 6 + (plane,) * 5,
        out_specs=(P(None, "wide", None, "narrow"), P(None, "wide", None, "narrow"), plane, plane),
        check_vma=False,
    )
```

```python
import functools

import jax
import jax.numpy as jnp
from jax import lax
from jax.experimental import pallas as pl
from jax.experimental.pallas import tpu as pltpu
from jax.sharding import PartitionSpec as P

PICARD = 2
DIFFUSE = 0.2
GAMMA_MELT = 0.5
TIME_STEP = 0.05
SLOPE_SCALE = 0.1
STRAIN_FLOOR = 0.01
HEATING_RATE = 0.01

LANES = 128
TILE = 8
HALO = 4
RIM = 3
VMEM = pltpu.CompilerParams(vmem_limit_bytes=16 * 1024 * 1024)
F32 = jnp.float32

THICK, GROUNDED, OCEAN_T, WET, ICE_LINK, OCEAN_LINK = range(6)
PLANES = 6
CORNER = (THICK, GROUNDED, ICE_LINK)
PART, EDGE_T0, EDGE_T1, EDGE_W0, PART_WET, EDGE_W1 = range(6)


def iota(shape, axis):
    return lax.broadcasted_iota(jnp.int32, shape, axis)


def right_lanes(period):
    lane = iota((1, LANES), 1)
    return lane % period < HALO


def left_lanes(period):
    lane = iota((1, LANES), 1)
    return lane % period >= period - HALO


def spread(column, count=LANES):
    rows = column.shape[0]
    eye = iota((rows, count), 0) == iota((rows, count), 1)
    return jnp.sum(jnp.where(eye, column, 0.0), axis=0, keepdims=True)


def upright(row):
    count = row.shape[1]
    eye = iota((count, count), 0) == iota((count, count), 1)
    return jnp.sum(jnp.where(eye, row, 0.0), axis=1, keepdims=True)


def turn(value, shift, axis):
    shift %= value.shape[axis]
    return pltpu.roll(value, shift, axis) if shift else value


def fetch_all(pairs, sems):
    copies = [pltpu.make_async_copy(a, b, sems.at[i]) for i, (a, b) in enumerate(pairs)]
    for copy in copies:
        copy.start()
    return copies


def divide(whole, part):
    return jnp.floor((whole + 0.5) * (1.0 / part))


def pick(hot, value):
    hot = hot.astype(jnp.bfloat16)
    pieces = []
    for _ in range(3):
        pieces.append(value.astype(jnp.bfloat16))
        value = value - pieces[-1].astype(F32)
    a, b, c = (jnp.dot(hot, p, preferred_element_type=F32) for p in pieces)
    return (c + b) + a


def narrow_sides(n_narrow):
    place = lax.axis_index("narrow")
    return place < n_narrow - 1, place > 0


def merged(parts, right, left, n_narrow):
    has_right, has_left = narrow_sides(n_narrow)
    from_right, from_left = parts[0], parts[-1]
    if len(parts) == 1:
        keep = (right & has_right) | (left & has_left)
        return jnp.where(keep, from_right, 0.0)
    return jnp.where(right, from_right, jnp.where(left, from_left, 0.0))


def ice_group(index):
    return divmod(index, LANES // 8)


def ice_tiles(layers):
    return ice_group(3 * layers - 1)[0] + 1


def ice_pairs(layers):
    return -(-3 * layers // 2)


class Places:
    def __init__(self, levels, layers):
        self.ice = 3 * levels
        self.thick = self.ice + ice_pairs(layers) * TILE
        self.grounded = self.thick + TILE
        self.wet = self.grounded + TILE
        self.link = self.wet + TILE
        self.end = self.link + TILE


def odd_place():
    return lax.axis_index("wide") % 2 == 1


def pack_ice(tile_of, layers):
    lane = iota((1, LANES), 1)
    tiles = [None] * ice_tiles(layers)
    for index in range(3 * layers):
        tile, group = ice_group(index)
        turned = turn(tile_of(*divmod(index, layers)), 8 * group, 1)
        before = jnp.zeros_like(turned) if group == 0 else tiles[tile]
        tiles[tile] = jnp.where((lane + HALO) % LANES // 8 == group, turned, before)
    return tiles


def pack_planes(planes):
    lane = iota((1, LANES), 1)
    total = None
    for j, plane in planes.items():
        turned = turn(plane, 16 * j, 1)
        before = jnp.zeros_like(turned) if total is None else total
        total = jnp.where((lane + HALO) % LANES // 16 == j, turned, before)
    return total


def edges_kernel(
    ice_x, ice_y, ice_t, ocean_x, ocean_y, ocean_t, thick, grounded, wet, ice_links, ocean_links,
    out, pair, cross, planes, ice, field, thick_v, grounded_v, wet_v, links_v, sems, field_sems,
):
    layers, rows, _ = ice_x.shape
    levels = ocean_x.shape[1]
    chunks = field_sems.shape[0] // 3
    step = rows // chunks
    copies = fetch_all(
        (
            (ice_x, ice.at[0]),
            (ice_y, ice.at[1]),
            (ice_t, ice.at[2]),
            (thick, thick_v),
            (grounded, grounded_v),
            (wet, wet_v),
            (ice_links, links_v.at[0]),
            (ocean_links, links_v.at[1]),
        ),
        sems,
    )
    field_copies = fetch_all(
        [
            (source.at[pl.ds(h * step, step)], field.at[f, pl.ds(h * step, step)])
            for f, source in reversed(list(enumerate((ocean_x, ocean_y, ocean_t))))
            for h in range(chunks)
        ],
        field_sems,
    )
    places = Places(levels, layers)
    odd = odd_place()

    def send(at, size, lasts, firsts):
        pair[at : at + size, :] = jnp.where(odd, firsts, lasts)
        cross[at : at + size, :] = jnp.where(odd, lasts, firsts)

    lane = iota((1, LANES), 1)
    for copy in copies:
        copy.wait()
    for tile, value in enumerate(pack_ice(lambda f, k: ice[f, k], layers)):
        out[(1 + tile) * rows : (2 + tile) * rows, :] = value
    upper = iota((TILE, 1), 0) >= HALO
    half = ice_pairs(layers)
    for m in range(half):
        ends = []
        for index in (m, m + half):
            f, k = divmod(min(index, 3 * layers - 1), layers)
            ends.append((ice[f, k, rows - TILE :, :], ice[f, k, :TILE, :]))
        send(
            places.ice + m * TILE,
            TILE,
            jnp.where(upper, ends[0][0], turn(ends[1][0], HALO, 0)),
            jnp.where(upper, turn(ends[1][1], HALO, 0), ends[0][1]),
        )
    planes[THICK] = thick_v[...]
    planes[GROUNDED] = grounded_v[...].astype(F32)
    planes[WET] = wet_v[...].astype(F32)
    for k in range(2):
        link = upright(links_v[k].astype(F32)) + 1.0
        planes[ICE_LINK + k] = jnp.broadcast_to(link, (rows, LANES))
    for at, j in (
        (places.thick, THICK), (places.grounded, GROUNDED), (places.wet, WET), (places.link, ICE_LINK),
    ):
        send(at, TILE, planes[j, rows - TILE :, :], planes[j, :TILE, :])
    total = jnp.zeros((levels, LANES), F32)
    for n, f in enumerate((2, 1, 0)):
        for h in range(chunks):
            field_copies[n * chunks + h].wait()
            for i in range(h * step, (h + 1) * step):
                j = f * rows + i
                turned = turn(field[f, i], 2 * j, 1)
                total = jnp.where((lane + 1) % LANES // 2 == j, turned, total)
        send(f * levels, levels, field[f, rows - 1], field[f, 0])
        if f == 2:
            for i in range(rows):
                planes[OCEAN_T, i : i + 1, :] = field[2, i, 0:1, :]
            out[0:rows, :] = pack_planes({j: planes[j] for j in range(PLANES)})
    out[(1 + ice_tiles(layers)) * rows :, :] = total


def plane_halo(block, group):
    lane = iota((1, LANES), 1)
    turned = turn(block, -16 * group, 1)
    return jnp.where((lane < HALO) | (lane >= LANES - HALO), turned, 0.0)


def merged_planes(parts, rows, n_narrow):
    return merged([p[0:rows, :] for p in parts], right_lanes(16), left_lanes(16), n_narrow)


def merged_ice(parts, rows, n_tiles, n_narrow):
    return [
        merged(
            [p[(1 + t) * rows : (2 + t) * rows, :] for p in parts],
            right_lanes(8), left_lanes(8), n_narrow,
        )
        for t in range(n_tiles)
    ]


def ranks(own_col, member_col, order_sub, order_lane, own_row):
    hits = (own_col == own_row) & member_col & (order_sub < order_lane)
    return jnp.sum(hits.astype(F32), axis=0, keepdims=True)


def ocean_slots(link_col, rows, n_wide, cap, block):
    link_row = spread(link_col)
    parts = []
    for link in (link_col, link_row):
        number = link - 1.0
        tile = divide(number, rows)
        inner = number - tile * rows
        ok = link > 0.5
        parts.append(
            (
                tile,
                (
                    ok,
                    ok & (inner >= rows - RIM) & (tile < n_wide - 1.5),
                    ok & (inner < RIM) & (tile > 0.5),
                ),
            )
        )
    (tile_col, member_col), (tile_row, member_row) = parts
    order_sub, order_lane = iota((rows, LANES), 0), iota((rows, LANES), 1)
    place = iota((n_wide * block, LANES), 0).astype(F32)
    total = jnp.zeros((n_wide * block, LANES), F32)
    for k, shift in enumerate((0.0, 1.0, -1.0)):
        rank = ranks(tile_col, member_col[k], order_sub, order_lane, tile_row)
        target = jnp.where(
            member_row[k], (tile_row + shift) * block + (k * cap + rank), -1.0
        )
        total = total + (place == target).astype(F32)
    return total[:, :rows]


def draft_slots(link_col, rows, n_wide, cap, block):
    link_row = spread(link_col)
    tile_col, tile_row = divide(link_col - 1.0, rows), divide(link_row - 1.0, rows)
    order_sub, order_lane = iota((rows, LANES), 0), iota((rows, LANES), 1)
    rank = ranks(tile_col, link_col > 0.5, order_sub, order_lane, tile_row)
    target = jnp.where(link_row > 0.5, tile_row * block + (3 * cap + rank), -1.0)
    place = iota((n_wide * block, LANES), 0).astype(F32)
    return (place == target).astype(F32)[:, :rows]


def blocks_kernel(n_wide, n_narrow, cap, block, n_parts, *refs):
    parts, refs = refs[:n_parts], refs[n_parts:]
    planes, blocks = refs
    rows = planes.shape[1]
    lane = iota((1, LANES), 1)
    plane_block = merged_planes(parts, rows, n_narrow)
    thick_plane, grounded_plane, wet_plane = planes[THICK], planes[GROUNDED], planes[WET]
    wet_all = jnp.concatenate([wet_plane, plane_halo(plane_block, WET)], axis=1)
    warm = wet_all * jnp.concatenate([planes[OCEAN_T], plane_halo(plane_block, OCEAN_T)], axis=1)
    width = 2 * LANES
    row = iota((rows, width), 0)
    sums = []
    for value in (wet_all, warm):
        total = pltpu.roll(value, 1, 1) + pltpu.roll(value, width - 1, 1)
        total = total + jnp.where(row > 0, pltpu.roll(value, 1, 0), 0.0)
        sums.append(total + jnp.where(row < rows - 1, pltpu.roll(value, rows - 1, 0), 0.0))
    mixed = warm + DIFFUSE * (wet_all * sums[1] - warm * sums[0])
    draft = 0.9 * thick_plane * (1.0 - grounded_plane)
    own_slots = ocean_slots(planes[OCEAN_LINK][:, 0:1], rows, n_wide, cap, block)
    main = pick(own_slots, jnp.concatenate([mixed[:, :LANES], wet_plane], axis=1))
    count = n_wide * block
    slot = iota((count, 1), 0) % block
    first = main[:, :LANES] + pick(draft_slots(planes[ICE_LINK][:, 0:1], rows, n_wide, cap, block), draft)
    second = jnp.where(
        slot == 3 * cap,
        wet_plane[0:1, :],
        jnp.where(slot == 3 * cap + 1, wet_plane[rows - 1 : rows, :], main[:, LANES:]),
    )
    edge = (lane < HALO) | (lane >= LANES - HALO)
    mixed_edge = jnp.where(edge, mixed[:, LANES:], 0.0)
    wet_edge = wet_all[:, LANES:]
    warm_edge = warm[:, LANES:]
    packed = mixed_edge + pltpu.roll(wet_edge, 16 * PART_WET, 1)
    links = plane_halo(plane_block, OCEAN_LINK)
    if n_narrow == 2:
        third = pick(
            ocean_slots(jnp.max(links, axis=1, keepdims=True), rows, n_wide, cap, block), packed
        )
    else:
        third = pick(
            ocean_slots(links[:, 0:1], rows, n_wide, cap, block),
            jnp.where(right_lanes(16), packed, 0.0),
        ) + pick(
            ocean_slots(links[:, LANES - 1 : LANES], rows, n_wide, cap, block),
            jnp.where(left_lanes(16), packed, 0.0),
        )
    last = rows - 1
    ends = (
        pltpu.roll(warm_edge[0:1, :], 16 * EDGE_T0, 1)
        + pltpu.roll(warm_edge[last:, :], 16 * EDGE_T1, 1)
        + pltpu.roll(wet_edge[0:1, :], 16 * EDGE_W0, 1)
        + pltpu.roll(wet_edge[last:, :], 16 * EDGE_W1, 1)
    )
    third = jnp.where(
        slot == 3 * cap,
        warm[0:1, :LANES],
        jnp.where(slot == 3 * cap + 1, warm[last:, :LANES], third + ends),
    )
    for k, value in enumerate((first, second, third)):
        blocks[:, k * block : (k + 1) * block, :] = value.reshape(n_wide, block, LANES)


def beyond_ice(up, down, places, layers, f, k):
    under = iota((TILE, 1), 0) < HALO
    index, half = f * layers + k, ice_pairs(layers)
    at = places.ice + index % half * TILE
    if index < half:
        return jnp.where(under, down(at, TILE), up(at, TILE))
    return turn(jnp.where(under, up(at, TILE), down(at, TILE)), HALO, 0)


def came_from(pair, cross):
    odd = odd_place()

    def up(at, size):
        return jnp.where(odd, pair[pl.ds(at, size), :], cross[pl.ds(at, size), :])

    def down(at, size):
        return jnp.where(odd, cross[pl.ds(at, size), :], pair[pl.ds(at, size), :])

    return up, down


def corners_kernel(levels, layers, pair, cross, out):
    places = Places(levels, layers)
    up, down = came_from(pair, cross)
    under = iota((TILE, 1), 0) < HALO
    tiles = pack_ice(lambda f, k: beyond_ice(up, down, places, layers, f, k), layers)
    planes = {}
    for j, at in zip(CORNER, (places.thick, places.grounded, places.link)):
        planes[j] = jnp.where(under, down(at, TILE), up(at, TILE))
    for n, tile in enumerate((pack_planes(planes), *tiles)):
        out[n * TILE : (n + 1) * TILE, :] = tile


def ocean_kernel(n_narrow, n_parts, n_tiles, layers, *refs):
    parts, refs = refs[:n_parts], refs[n_parts:]
    ocean_x, ocean_y, ocean_t, pair, cross, planes, out, top, field, held, sems = refs
    rows, levels, _ = ocean_x.shape
    places = Places(levels, layers)
    chunks = sems.shape[0] // 6
    step = rows // chunks
    reads = fetch_all(
        [
            (source.at[pl.ds(h * step, step)], field.at[f, pl.ds(h * step, step)])
            for f, source in enumerate((ocean_x, ocean_y, ocean_t))
            for h in range(chunks)
        ],
        sems,
    )
    up, down = came_from(pair, cross)
    lane = iota((1, LANES), 1)
    row = iota((rows, LANES), 0)
    first, last = lane == 0, lane == LANES - 1
    wet = planes[WET]
    wet_halo = plane_halo(merged_planes(parts, rows, n_narrow), WET)
    scale = DIFFUSE * wet
    coef = (
        scale * jnp.where(row > 0, turn(wet, 1, 0), up(places.wet + TILE - 1, 1)),
        scale * jnp.where(row < rows - 1, turn(wet, -1, 0), down(places.wet, 1)),
        scale * turn(jnp.where(last, wet_halo, wet), 1, 1),
        scale * turn(jnp.where(first, wet_halo, wet), -1, 1),
    )
    centre_coef = 1.0 - (coef[0] + coef[1] + coef[2] + coef[3])
    even = lane % 2 == 0
    strip_at = (1 + n_tiles) * rows
    side = merged([p[strip_at:, :] for p in parts], even, ~even, n_narrow)
    writes = []
    for f in range(3):
        for h in range(chunks):
            reads[f * chunks + h].wait()
        for h in range(chunks):
            for i in range(h * step, (h + 1) * step):
                centre = field[f, i]
                halo = turn(side, -2 * (f * rows + i), 1)
                above = field[f, i - 1] if i > 0 else up(f * levels, levels)
                below = field[f, i + 1] if i < rows - 1 else down(f * levels, levels)
                value = centre * centre_coef[i : i + 1, :]
                value = value + above * coef[0][i : i + 1, :]
                value = value + below * coef[1][i : i + 1, :]
                value = value + turn(jnp.where(last, halo, centre), 1, 1) * coef[2][i : i + 1, :]
                value = value + turn(jnp.where(first, halo, centre), -1, 1) * coef[3][i : i + 1, :]
                held[f, i] = value
                if f == 2:
                    top[i] = value[0:TILE, :]
            part = pl.ds(h * step, step)
            level = pl.ds(TILE, levels - TILE) if f == 2 else pl.ds(0, levels)
            copy = pltpu.make_async_copy(
                held.at[f, part, level],
                out.at[f, part, level],
                sems.at[(3 + f) * chunks + h],
            )
            copy.start()
            writes.append(copy)
    for copy in writes:
        copy.wait()


def ice_slots(link_col, kind_col, rows, cap, block, count, n_wide):
    link_row = spread(link_col)
    kind_row = spread(kind_col)
    number = link_col - 1.0
    tile = divide(number, rows)
    inner = number - tile * rows
    tile_row = divide(link_row - 1.0, rows)
    ok = (link_col > 0.5) & (kind_col > -0.5)
    ok_row = (link_row > 0.5) & (kind_row > -0.5)
    hits = (tile == tile_row) & (kind_col == kind_row) & ok_row & (link_row < link_col)
    rank = jnp.sum(hits.astype(F32), axis=1, keepdims=True)
    place = iota((link_col.shape[0], count), 1).astype(F32)

    def hot(keep, target):
        return (place == jnp.where(keep, target, -1.0)).astype(F32)

    top, bottom = inner < 0.5, inner > rows - 1.5
    edge = ok & (top | bottom)
    near = jnp.where(top, tile - 1.0, tile + 1.0)
    near_ok = edge & (near > -0.5) & (near < n_wide - 0.5)
    slot = hot(ok, tile * block + kind_col * cap + rank)
    near_edge = hot(near_ok, near * block + jnp.where(top, 3.0 * cap + 1.0, 3.0 * cap))
    own_edge = hot(edge, tile * block + jnp.where(top, 3.0 * cap, 3.0 * cap + 1.0))
    near_slot = hot(near_ok, near * block)
    own_slot = hot(edge, tile * block)
    return slot, near_edge, own_edge, near_slot, own_slot, bottom.astype(F32)


def around(value):
    return turn(value, 1, 0) + turn(value, -1, 0) + turn(value, 1, 1) + turn(value, -1, 1)


def sweep_layer(vel, k, layers, rate, friction):
    u, v = vel(0, k), vel(1, k)
    ends = [[turn(w, s, axis) for axis in (0, 1) for s in (-1, 1)] for w in (u, v)]
    ux, uy = ends[0][0] - ends[0][1], ends[0][2] - ends[0][3]
    vx, vy = ends[1][0] - ends[1][1], ends[1][2] - ends[1][3]
    cross = uy + vx
    eps2 = ux * (ux + vy) + vy * vy + 0.25 * (cross * cross)
    if k < layers - 1:
        uz, vz = vel(0, k + 1) - u, vel(1, k + 1) - v
        eps2 = eps2 + (uz * uz + vz * vz)
    eps2 = 0.25 * eps2
    eta = rate * jnp.exp((-1.0 / 3.0) * jnp.log(eps2 + STRAIN_FLOOR))
    links_up_down = float((k > 0) + (k < layers - 1))
    diagonal = eta * (2.0 + links_up_down) + 0.5 * around(eta) + friction
    sums = []
    for f, w in enumerate((u, v)):
        total = 0.5 * (ends[f][0] + ends[f][1] + ends[f][2] + ends[f][3])
        if k > 0:
            total = total + vel(f, k - 1)
        if k < layers - 1:
            total = total + vel(f, k + 1)
        sums.append(eta * total + 0.5 * around(eta * w))
    return sums, 1.0 / diagonal, eta * eps2


FLAT = ("thick", "grounded", "inside")


def first_kernel(n_wide, n_narrow, cap, block, n_parts, levels, *refs):
    parts, refs = refs[:n_parts], refs[n_parts:]
    corners, refs = refs[:n_parts], refs[n_parts:]
    ice, pair, cross, planes, sums, inverse, rate, flat, hots, ends, vel = refs
    _, layers, rows, _ = ice.shape
    places = Places(levels, layers)
    n_tiles = ice_tiles(layers)
    up, down = came_from(pair, cross)
    lane = iota((1, LANES), 1)
    width = 2 * LANES
    tall = rows + TILE
    wide_lane = iota((1, width), 1)
    place_wide = lax.axis_index("wide")
    has_right, has_left = narrow_sides(n_narrow)
    has_up, has_down = place_wide > 0, place_wide < n_wide - 1
    under = iota((TILE, 1), 0) < HALO

    def rim(at):
        return jnp.where(under, down(at, TILE), up(at, TILE))

    def below(a, b):
        return jnp.concatenate([a, b], axis=0)

    corner_planes = merged(
        [c[0:TILE, :] for c in corners], right_lanes(16), left_lanes(16), n_narrow
    )
    corner_ice = [
        merged(
            [c[(1 + t) * TILE : (2 + t) * TILE, :] for c in corners],
            right_lanes(8), left_lanes(8), n_narrow,
        )
        for t in range(n_tiles)
    ]
    block_tall = below(merged_planes(parts, rows, n_narrow), corner_planes)
    flat[0] = jnp.concatenate(
        [below(planes[THICK], rim(places.thick)), plane_halo(block_tall, THICK)], axis=1
    )
    grounded_tall = jnp.concatenate(
        [below(planes[GROUNDED], rim(places.grounded)), plane_halo(block_tall, GROUNDED)], axis=1
    )
    flat[1] = grounded_tall
    tall_row = iota((tall, 1), 0)
    inside = (
        ((tall_row < rows) | ((tall_row < rows + HALO) & has_down) | ((tall_row >= rows + HALO) & has_up))
        & (
            (wide_lane < LANES)
            | ((wide_lane < LANES + HALO) & has_right)
            | ((wide_lane >= width - HALO) & has_left)
        )
    ).astype(F32)
    flat[2] = inside
    kind = jnp.where(
        tall_row < rows,
        0.0,
        jnp.where(tall_row < rows + RIM, 2.0, jnp.where(tall_row >= tall - RIM, 1.0, -1.0)),
    )
    count = n_wide * block
    own_link = below(planes[ICE_LINK], rim(places.link))[:, 0:1]
    slots = (rows, cap, block, count, n_wide)
    found = list(ice_slots(own_link, kind, *slots)[:3])
    links = plane_halo(block_tall, ICE_LINK)
    if n_narrow == 2:
        sides = [jnp.max(links, axis=1, keepdims=True)]
    else:
        sides = [links[:, 0:1], links[:, LANES - 1 : LANES]]
    for link in sides:
        slot, _, _, near_slot, own_slot, bottom = ice_slots(link, kind, *slots)
        ends[(len(found) - 3) // 3] = jnp.broadcast_to(bottom, (tall, LANES))
        found += [slot, near_slot, own_slot]
    for n, hot in enumerate(found):
        hots[n * tall : (n + 1) * tall, :] = hot
    ocean_link = planes[OCEAN_LINK][:, 0:1]
    ocean_row = spread(ocean_link)
    tile = divide(ocean_link - 1.0, rows)
    tile_row = divide(ocean_row - 1.0, rows)
    hits = (tile == tile_row) & (ocean_row > 0.5) & (ocean_row < ocean_link)
    rank = jnp.sum(hits.astype(F32), axis=1, keepdims=True)
    target = jnp.where(ocean_link > 0.5, tile * block + 3 * cap + rank, -1.0)
    hots[len(found) * tall :, :] = (iota((rows, count), 1).astype(F32) == target).astype(F32)
    strips = [
        below(a, b) for a, b in zip(merged_ice(parts, rows, n_tiles, n_narrow), corner_ice)
    ]
    edge = (lane < HALO) | (lane >= LANES - HALO)
    for index in range(3 * layers):
        f, k = divmod(index, layers)
        beyond = beyond_ice(up, down, places, layers, f, k)
        t, group = ice_group(index)
        beside = jnp.where(edge, turn(strips[t], -8 * group, 1), 0.0)
        value = jnp.concatenate([below(ice[f, k], beyond), beside], axis=1)
        if f < 2:
            vel[f, k] = value
        else:
            rate[k] = jnp.exp(0.25 * value) * inside
    friction = 0.1 + 9.9 * grounded_tall
    for k in range(layers):
        both, over, _ = sweep_layer(lambda f, n: vel[f, n], k, layers, rate[k], friction)
        for f in range(2):
            sums[f, k] = both[f]
        inverse[k] = over * inside


def final_kernel(n_wide, n_narrow, cap, block, *refs):
    (
        blocks, hots, ends, planes, ice, top, sums, inverse, rate, flat, ocean_in,
        ice_out, ocean_out, thick_out, melt_out,
        vel, result, thin, melted, new_top, sems,
    ) = refs
    _, layers, rows, _ = ice.shape
    tall, width = flat.shape[1:]
    lane = iota((1, LANES), 1)
    count = n_wide * block
    parts = [
        blocks[:, n * block : (n + 1) * block, :].reshape(count, LANES) for n in range(3)
    ]
    found = pick(hots[...], jnp.concatenate(parts, axis=1))

    def got(n, part):
        return found[n * tall : (n + 1) * tall, part * LANES : (part + 1) * LANES]

    wet_main = got(0, 1)
    mixed_main = got(0, 0) + DIFFUSE * (wet_main * got(1, 2) - got(1, 1) * got(2, 2))
    sides = []
    for n in range(3, 3 * (1 if n_narrow == 2 else 2) + 3, 3):
        value, near, own = got(n, 2), got(n + 1, 2), got(n + 2, 2)

        def group(row, j):
            return turn(row, -16 * j, 1)

        wet_got = group(value, PART_WET)
        bottom = ends[n // 3 - 1] > 0.5
        near_warm = jnp.where(bottom, group(near, EDGE_T0), group(near, EDGE_T1))
        near_wet = jnp.where(bottom, group(near, EDGE_W0), group(near, EDGE_W1))
        own_warm = jnp.where(bottom, group(own, EDGE_T1), group(own, EDGE_T0))
        sides.append((value + DIFFUSE * (wet_got * near_warm - near_wet * own_warm), wet_got))
    if len(sides) == 1:
        mixed_side, wet_side = sides[0]
    else:
        mixed_side, wet_side = (jnp.where(lane < HALO, a, b) for a, b in zip(*sides))
    mixed_tall = jnp.concatenate([mixed_main, mixed_side], axis=1)
    wet_tall = jnp.concatenate([wet_main, wet_side], axis=1)
    thick_tall, grounded_tall, inside = flat[0], flat[1], flat[2]
    open_ice = 1.0 - grounded_tall
    draft_tall = 0.9 * thick_tall * open_ice
    melt_tall = GAMMA_MELT * (mixed_tall - wet_tall * (0.0832 - 0.761 * draft_tall))
    new_thick = (thick_tall - TIME_STEP * melt_tall * open_ice) * inside
    thin[...] = new_thick[:rows, :LANES]
    n_hots = hots.shape[0] - rows
    ocean_draft = found[n_hots:, :LANES]
    heat_top = jnp.concatenate([top[i, 0:1, :] for i in range(rows)], axis=0)
    coupled = (planes[OCEAN_LINK] > 0.5).astype(F32)
    melt = GAMMA_MELT * (heat_top - (0.0832 - 0.761 * ocean_draft)) * planes[WET] * coupled
    melted[...] = melt
    cooled = heat_top - 0.2 * melt
    new_top[...] = top[...]
    for i in range(rows):
        new_top[i, 0:1, :] = cooled[i : i + 1, :]
    writes = fetch_all(
        (
            (new_top, ocean_out.at[2, :, pl.ds(0, TILE), :]),
            (thin, thick_out),
            (melted, melt_out),
        ),
        sems,
    )
    surface = new_thick * (0.1 + 0.9 * grounded_tall)
    scale = (-0.5 * SLOPE_SCALE) * new_thick
    stress = (
        scale * (turn(surface, -1, 0) - turn(surface, 1, 0)),
        scale * (turn(surface, -1, 1) - turn(surface, 1, 1)),
    )
    friction = 0.1 + 9.9 * grounded_tall
    for f in range(2):
        for k in range(layers):
            vel[0, f, k] = (sums[f, k] + stress[f]) * inverse[k]
    for sweep in range(1, PICARD):
        last = sweep == PICARD - 1
        old = sweep - 1
        for k in range(layers):
            both, over, heat = sweep_layer(
                lambda f, n: vel[old, f, n], k, layers, rate[k], friction
            )
            for f in range(2):
                value = (both[f] + stress[f]) * over
                if last:
                    result[f, k] = value[:rows, :LANES]
                else:
                    vel[sweep, f, k] = value * inside
            if last:
                result[2, k] = ice[2, k] + HEATING_RATE * heat[:rows, :LANES]
                copy = pltpu.make_async_copy(
                    result.at[:, k], ice_out.at[:, k], sems.at[len(writes)]
                )
                copy.start()
                writes.append(copy)
    for copy in writes:
        copy.wait()


def local(
    ice_x, ice_y, ice_temp, ocean_x, ocean_y, ocean_temp, thick, grounded_mask, wet_mask, ice_links, ocean_links,
):
    n_wide, n_narrow = lax.axis_size("wide"), lax.axis_size("narrow")
    rows, layers, columns = ice_x.shape
    levels = ocean_x.shape[1]
    cap = max(1, 2 * rows // n_wide)
    block = -(-max(4 * cap, 3 * cap + 2) // TILE) * TILE
    assert columns == LANES and ice_links.shape[0] == rows

    def stay(value):
        return pltpu.with_memory_space_constraint(value, pltpu.HBM)

    ice_fields = [stay(x.transpose(1, 0, 2)) for x in (ice_x, ice_y, ice_temp)]
    links = [stay(x.reshape(1, rows)) for x in (ice_links, ocean_links)]
    fields = [stay(x) for x in (ocean_x, ocean_y, ocean_temp)]
    planes_in = [stay(x) for x in (thick, grounded_mask, wet_mask)]
    here = pl.BlockSpec(memory_space=pltpu.VMEM)
    far = pl.BlockSpec(memory_space=pltpu.HBM)
    unread = pl.BlockSpec(memory_space=pl.ANY)
    dma = pltpu.SemaphoreType.DMA

    def array(*shape):
        return jax.ShapeDtypeStruct(shape, F32)

    def kept(*shape):
        return pltpu.VMEM(shape, F32)

    def near(*values):
        return [pltpu.with_memory_space_constraint(value, pltpu.VMEM) for value in values]

    def call(kernel, name, microseconds, out_shape, in_specs, out_specs, scratch=(), **more):
        estimate = pl.CostEstimate(
            flops=int(microseconds * 1.0e9), bytes_accessed=int(microseconds * 3.0e6), transcendentals=0
        )
        return pl.pallas_call(
            kernel, name=name, out_shape=out_shape, in_specs=in_specs, out_specs=out_specs,
            scratch_shapes=scratch, compiler_params=VMEM, cost_estimate=estimate, **more,
        )

    n_tiles = ice_tiles(layers)
    places = Places(levels, layers)
    chunks = 2
    message, to_pair, to_cross, planes, ice = call(
        edges_kernel, "edges", 100.0,
        (
            kept((1 + n_tiles) * rows + levels, LANES), kept(places.end, LANES), kept(places.end, LANES),
            kept(PLANES, rows, LANES), kept(3, layers, rows, LANES),
        ),
        [far] * 11, (here,) * 5,
        [
            pltpu.VMEM((3, rows, levels, LANES), F32),
            pltpu.VMEM((rows, LANES), F32),
            pltpu.VMEM((rows, LANES), jnp.int32),
            pltpu.VMEM((rows, LANES), jnp.int32),
            pltpu.VMEM((2, 1, rows), jnp.int32),
            dma((8,)),
            dma((3 * chunks,)),
        ],
    )(*ice_fields, *fields, *planes_in, *links)

    def narrow(value):
        if n_narrow == 2:
            return [lax.ppermute(value, "narrow", [(0, 1), (1, 0)])]
        ahead = [(i, i + 1) for i in range(n_narrow - 1)]
        return [
            lax.ppermute(value, "narrow", [(j, i) for i, j in ahead]),
            lax.ppermute(value, "narrow", ahead),
        ]

    parts = narrow(message)
    n_parts = len(parts)
    assert n_wide % 2 == 0
    swaps = [[(i, i + 1) for i in range(start, n_wide - 1, 2)] for start in (0, 1)]
    pair, cross = (
        lax.ppermute(value, "wide", swap + [(j, i) for i, j in swap])
        for value, swap in zip((to_pair, to_cross), swaps)
    )
    blocks = call(
        functools.partial(blocks_kernel, n_wide, n_narrow, cap, block, n_parts), "blocks", 100.0,
        kept(n_wide, 3 * block, LANES), [here] * (n_parts + 1), here,
    )(*near(*parts, planes))
    blocks = lax.all_to_all(blocks, "wide", split_axis=0, concat_axis=0, tiled=True)
    corners = narrow(
        call(
            functools.partial(corners_kernel, levels, layers), "corners", 1.0,
            kept((1 + n_tiles) * TILE, LANES), [here] * 2, here,
        )(*near(pair, cross))
    )
    ocean, top = call(
        functools.partial(ocean_kernel, n_narrow, n_parts, n_tiles, layers), "ocean", 100.0,
        (array(3, rows, levels, LANES), kept(rows, TILE, LANES)),
        [here] * n_parts + [far] * 3 + [here] * 3, (far, here),
        [
            pltpu.VMEM((3, rows, levels, LANES), F32),
            pltpu.VMEM((3, rows, levels, LANES), F32),
            dma((6 * chunks,)),
        ],
    )(*near(*parts), *fields, *near(pair, cross, planes))
    wide = 2 * LANES
    tall = rows + TILE
    n_sides = 1 if n_narrow == 2 else 2
    sums, inverse, rate, flat, hots, ends = call(
        functools.partial(first_kernel, n_wide, n_narrow, cap, block, n_parts, levels), "first", 100.0,
        (
            kept(2, layers, tall, wide), kept(layers, tall, wide), kept(layers, tall, wide), kept(3, tall, wide),
            kept((3 + 3 * n_sides) * tall + rows, n_wide * block), kept(n_sides, tall, LANES),
        ),
        [here] * (2 * n_parts + 4), (here,) * 6,
        [pltpu.VMEM((2, layers, tall, wide), F32)],
    )(*near(*parts, *corners, ice, pair, cross, planes))
    ice, ocean, thick_out, melt_out = call(
        functools.partial(final_kernel, n_wide, n_narrow, cap, block), "final", 3.0,
        (
            array(3, layers, rows, LANES), array(3, rows, levels, LANES),
            array(rows, LANES), array(rows, LANES),
        ),
        [here] * 10 + [far], (far,) * 4,
        [
            pltpu.VMEM((PICARD - 1, 2, layers, tall, wide), F32),
            pltpu.VMEM((3, layers, rows, LANES), F32),
            pltpu.VMEM((rows, LANES), F32),
            pltpu.VMEM((rows, LANES), F32),
            pltpu.VMEM((rows, TILE, LANES), F32),
            dma((3 + layers,)),
        ],
        input_output_aliases={10: 1},
    )(*near(blocks, hots, ends, planes, ice, top, sums, inverse, rate, flat), ocean)
    return ice.transpose(0, 2, 1, 3), ocean, thick_out, melt_out


def solution(mesh):
    column = P("wide", None, "narrow")
    plane = P("wide", "narrow")
    return jax.shard_map(
        local,
        mesh=mesh,
        in_specs=(column,) * 6 + (plane,) * 5,
        out_specs=(P(None, "wide", None, "narrow"), P(None, "wide", None, "narrow"), plane, plane),
        check_vma=False,
    )
```

```python
import functools

import jax
import jax.numpy as jnp
from jax import lax
from jax.experimental import pallas as pl
from jax.experimental.pallas import tpu as pltpu
from jax.sharding import PartitionSpec as P

PICARD = 2
DIFFUSE = 0.2
GAMMA_MELT = 0.5
TIME_STEP = 0.05
SLOPE_SCALE = 0.1
STRAIN_FLOOR = 0.01
HEATING_RATE = 0.01

LANES = 128
TILE = 8
HALO = 4
RIM = 3
VMEM = pltpu.CompilerParams(vmem_limit_bytes=16 * 1024 * 1024)
F32 = jnp.float32

THICK, GROUNDED, OCEAN_T, WET, ICE_LINK, OCEAN_LINK = range(6)
PLANES = 6
CORNER = (THICK, GROUNDED, ICE_LINK)
PART, EDGE_T0, EDGE_T1, EDGE_W0, PART_WET, EDGE_W1 = range(6)


def iota(shape, axis):
    return lax.broadcasted_iota(jnp.int32, shape, axis)


def right_lanes(period):
    lane = iota((1, LANES), 1)
    return lane % period < HALO


def left_lanes(period):
    lane = iota((1, LANES), 1)
    return lane % period >= period - HALO


def spread(column, count=LANES):
    rows = column.shape[0]
    eye = iota((rows, count), 0) == iota((rows, count), 1)
    return jnp.sum(jnp.where(eye, column, 0.0), axis=0, keepdims=True)


def upright(row):
    count = row.shape[1]
    eye = iota((count, count), 0) == iota((count, count), 1)
    return jnp.sum(jnp.where(eye, row, 0.0), axis=1, keepdims=True)


def turn(value, shift, axis):
    shift %= value.shape[axis]
    return pltpu.roll(value, shift, axis) if shift else value


def fetch_all(pairs, sems):
    copies = [pltpu.make_async_copy(a, b, sems.at[i]) for i, (a, b) in enumerate(pairs)]
    for copy in copies:
        copy.start()
    return copies


def divide(whole, part):
    return jnp.floor((whole + 0.5) * (1.0 / part))


def pick(hot, value):
    hot = hot.astype(jnp.bfloat16)
    pieces = []
    for _ in range(3):
        pieces.append(value.astype(jnp.bfloat16))
        value = value - pieces[-1].astype(F32)
    a, b, c = (jnp.dot(hot, p, preferred_element_type=F32) for p in pieces)
    return (c + b) + a


def narrow_sides(n_narrow):
    place = lax.axis_index("narrow")
    return place < n_narrow - 1, place > 0


def merged(parts, right, left, n_narrow):
    has_right, has_left = narrow_sides(n_narrow)
    from_right, from_left = parts[0], parts[-1]
    if len(parts) == 1:
        keep = (right & has_right) | (left & has_left)
        return jnp.where(keep, from_right, 0.0)
    return jnp.where(right, from_right, jnp.where(left, from_left, 0.0))


def ice_group(index):
    return divmod(index, LANES // 8)


def ice_tiles(layers):
    return ice_group(3 * layers - 1)[0] + 1


def ice_pairs(layers):
    return -(-3 * layers // 2)


class Places:
    def __init__(self, levels, layers):
        self.ice = 3 * levels
        self.thick = self.ice + ice_pairs(layers) * TILE
        self.grounded = self.thick + TILE
        self.wet = self.grounded + TILE
        self.link = self.wet + TILE
        self.end = self.link + TILE


def odd_place():
    return lax.axis_index("wide") % 2 == 1


def pack_ice(tile_of, layers):
    lane = iota((1, LANES), 1)
    tiles = [None] * ice_tiles(layers)
    for index in range(3 * layers):
        tile, group = ice_group(index)
        turned = turn(tile_of(*divmod(index, layers)), 8 * group, 1)
        before = jnp.zeros_like(turned) if group == 0 else tiles[tile]
        tiles[tile] = jnp.where((lane + HALO) % LANES // 8 == group, turned, before)
    return tiles


def pack_planes(planes):
    lane = iota((1, LANES), 1)
    total = None
    for j, plane in planes.items():
        turned = turn(plane, 16 * j, 1)
        before = jnp.zeros_like(turned) if total is None else total
        total = jnp.where((lane + HALO) % LANES // 16 == j, turned, before)
    return total


def edges_kernel(
    ice_x, ice_y, ice_t, ocean_x, ocean_y, ocean_t, thick, grounded, wet, ice_links, ocean_links,
    out, pair, cross, planes, ice, field, thick_v, grounded_v, wet_v, links_v, sems, field_sems,
):
    layers, rows, _ = ice_x.shape
    levels = ocean_x.shape[1]
    chunks = field_sems.shape[0] // 3
    step = rows // chunks
    copies = fetch_all(
        (
            (ice_x, ice.at[0]),
            (ice_y, ice.at[1]),
            (ice_t, ice.at[2]),
            (thick, thick_v),
            (grounded, grounded_v),
            (wet, wet_v),
            (ice_links, links_v.at[0]),
            (ocean_links, links_v.at[1]),
        ),
        sems,
    )
    field_copies = fetch_all(
        [
            (source.at[pl.ds(h * step, step)], field.at[f, pl.ds(h * step, step)])
            for f, source in reversed(list(enumerate((ocean_x, ocean_y, ocean_t))))
            for h in range(chunks)
        ],
        field_sems,
    )
    places = Places(levels, layers)
    odd = odd_place()

    def send(at, size, lasts, firsts):
        pair[at : at + size, :] = jnp.where(odd, firsts, lasts)
        cross[at : at + size, :] = jnp.where(odd, lasts, firsts)

    lane = iota((1, LANES), 1)
    for copy in copies:
        copy.wait()
    for tile, value in enumerate(pack_ice(lambda f, k: ice[f, k], layers)):
        out[(1 + tile) * rows : (2 + tile) * rows, :] = value
    upper = iota((TILE, 1), 0) >= HALO
    half = ice_pairs(layers)
    for m in range(half):
        ends = []
        for index in (m, m + half):
            f, k = divmod(min(index, 3 * layers - 1), layers)
            ends.append((ice[f, k, rows - TILE :, :], ice[f, k, :TILE, :]))
        send(
            places.ice + m * TILE,
            TILE,
            jnp.where(upper, ends[0][0], turn(ends[1][0], HALO, 0)),
            jnp.where(upper, turn(ends[1][1], HALO, 0), ends[0][1]),
        )
    planes[THICK] = thick_v[...]
    planes[GROUNDED] = grounded_v[...].astype(F32)
    planes[WET] = wet_v[...].astype(F32)
    for k in range(2):
        link = upright(links_v[k].astype(F32)) + 1.0
        planes[ICE_LINK + k] = jnp.broadcast_to(link, (rows, LANES))
    for at, j in (
        (places.thick, THICK), (places.grounded, GROUNDED), (places.wet, WET), (places.link, ICE_LINK),
    ):
        send(at, TILE, planes[j, rows - TILE :, :], planes[j, :TILE, :])
    total = jnp.zeros((levels, LANES), F32)
    for n, f in enumerate((2, 1, 0)):
        for h in range(chunks):
            field_copies[n * chunks + h].wait()
            for i in range(h * step, (h + 1) * step):
                j = f * rows + i
                turned = turn(field[f, i], 2 * j, 1)
                total = jnp.where((lane + 1) % LANES // 2 == j, turned, total)
        send(f * levels, levels, field[f, rows - 1], field[f, 0])
        if f == 2:
            for i in range(rows):
                planes[OCEAN_T, i : i + 1, :] = field[2, i, 0:1, :]
            out[0:rows, :] = pack_planes({j: planes[j] for j in range(PLANES)})
    out[(1 + ice_tiles(layers)) * rows :, :] = total


def plane_halo(block, group):
    lane = iota((1, LANES), 1)
    turned = turn(block, -16 * group, 1)
    return jnp.where((lane < HALO) | (lane >= LANES - HALO), turned, 0.0)


def merged_planes(parts, rows, n_narrow):
    return merged([p[0:rows, :] for p in parts], right_lanes(16), left_lanes(16), n_narrow)


def merged_ice(parts, rows, n_tiles, n_narrow):
    return [
        merged(
            [p[(1 + t) * rows : (2 + t) * rows, :] for p in parts],
            right_lanes(8), left_lanes(8), n_narrow,
        )
        for t in range(n_tiles)
    ]


def ranks(own_col, member_col, order_sub, order_lane, own_row):
    hits = (own_col == own_row) & member_col & (order_sub < order_lane)
    return jnp.sum(hits.astype(F32), axis=0, keepdims=True)


def ocean_slots(link_col, rows, n_wide, cap, block):
    link_row = spread(link_col)
    parts = []
    for link in (link_col, link_row):
        number = link - 1.0
        tile = divide(number, rows)
        inner = number - tile * rows
        ok = link > 0.5
        parts.append(
            (
                tile,
                (
                    ok,
                    ok & (inner >= rows - RIM) & (tile < n_wide - 1.5),
                    ok & (inner < RIM) & (tile > 0.5),
                ),
            )
        )
    (tile_col, member_col), (tile_row, member_row) = parts
    order_sub, order_lane = iota((rows, LANES), 0), iota((rows, LANES), 1)
    place = iota((n_wide * block, LANES), 0).astype(F32)
    total = jnp.zeros((n_wide * block, LANES), F32)
    for k, shift in enumerate((0.0, 1.0, -1.0)):
        rank = ranks(tile_col, member_col[k], order_sub, order_lane, tile_row)
        target = jnp.where(
            member_row[k], (tile_row + shift) * block + (k * cap + rank), -1.0
        )
        total = total + (place == target).astype(F32)
    return total[:, :rows]


def draft_slots(link_col, rows, n_wide, cap, block):
    link_row = spread(link_col)
    tile_col, tile_row = divide(link_col - 1.0, rows), divide(link_row - 1.0, rows)
    order_sub, order_lane = iota((rows, LANES), 0), iota((rows, LANES), 1)
    rank = ranks(tile_col, link_col > 0.5, order_sub, order_lane, tile_row)
    target = jnp.where(link_row > 0.5, tile_row * block + (3 * cap + rank), -1.0)
    place = iota((n_wide * block, LANES), 0).astype(F32)
    return (place == target).astype(F32)[:, :rows]


def blocks_kernel(n_wide, n_narrow, cap, block, n_parts, *refs):
    parts, refs = refs[:n_parts], refs[n_parts:]
    planes, blocks = refs
    rows = planes.shape[1]
    lane = iota((1, LANES), 1)
    plane_block = merged_planes(parts, rows, n_narrow)
    thick_plane, grounded_plane, wet_plane = planes[THICK], planes[GROUNDED], planes[WET]
    wet_all = jnp.concatenate([wet_plane, plane_halo(plane_block, WET)], axis=1)
    warm = wet_all * jnp.concatenate([planes[OCEAN_T], plane_halo(plane_block, OCEAN_T)], axis=1)
    width = 2 * LANES
    row = iota((rows, width), 0)
    sums = []
    for value in (wet_all, warm):
        total = pltpu.roll(value, 1, 1) + pltpu.roll(value, width - 1, 1)
        total = total + jnp.where(row > 0, pltpu.roll(value, 1, 0), 0.0)
        sums.append(total + jnp.where(row < rows - 1, pltpu.roll(value, rows - 1, 0), 0.0))
    mixed = warm + DIFFUSE * (wet_all * sums[1] - warm * sums[0])
    draft = 0.9 * thick_plane * (1.0 - grounded_plane)
    own_slots = ocean_slots(planes[OCEAN_LINK][:, 0:1], rows, n_wide, cap, block)
    main = pick(own_slots, jnp.concatenate([mixed[:, :LANES], wet_plane], axis=1))
    count = n_wide * block
    slot = iota((count, 1), 0) % block
    first = main[:, :LANES] + pick(draft_slots(planes[ICE_LINK][:, 0:1], rows, n_wide, cap, block), draft)
    second = jnp.where(
        slot == 3 * cap,
        wet_plane[0:1, :],
        jnp.where(slot == 3 * cap + 1, wet_plane[rows - 1 : rows, :], main[:, LANES:]),
    )
    edge = (lane < HALO) | (lane >= LANES - HALO)
    mixed_edge = jnp.where(edge, mixed[:, LANES:], 0.0)
    wet_edge = wet_all[:, LANES:]
    warm_edge = warm[:, LANES:]
    packed = mixed_edge + pltpu.roll(wet_edge, 16 * PART_WET, 1)
    links = plane_halo(plane_block, OCEAN_LINK)
    if n_narrow == 2:
        third = pick(
            ocean_slots(jnp.max(links, axis=1, keepdims=True), rows, n_wide, cap, block), packed
        )
    else:
        third = pick(
            ocean_slots(links[:, 0:1], rows, n_wide, cap, block),
            jnp.where(right_lanes(16), packed, 0.0),
        ) + pick(
            ocean_slots(links[:, LANES - 1 : LANES], rows, n_wide, cap, block),
            jnp.where(left_lanes(16), packed, 0.0),
        )
    last = rows - 1
    ends = (
        pltpu.roll(warm_edge[0:1, :], 16 * EDGE_T0, 1)
        + pltpu.roll(warm_edge[last:, :], 16 * EDGE_T1, 1)
        + pltpu.roll(wet_edge[0:1, :], 16 * EDGE_W0, 1)
        + pltpu.roll(wet_edge[last:, :], 16 * EDGE_W1, 1)
    )
    third = jnp.where(
        slot == 3 * cap,
        warm[0:1, :LANES],
        jnp.where(slot == 3 * cap + 1, warm[last:, :LANES], third + ends),
    )
    for k, value in enumerate((first, second, third)):
        blocks[:, k * block : (k + 1) * block, :] = value.reshape(n_wide, block, LANES)


def beyond_ice(up, down, places, layers, f, k):
    under = iota((TILE, 1), 0) < HALO
    index, half = f * layers + k, ice_pairs(layers)
    at = places.ice + index % half * TILE
    if index < half:
        return jnp.where(under, down(at, TILE), up(at, TILE))
    return turn(jnp.where(under, up(at, TILE), down(at, TILE)), HALO, 0)


def came_from(pair, cross):
    odd = odd_place()

    def up(at, size):
        return jnp.where(odd, pair[pl.ds(at, size), :], cross[pl.ds(at, size), :])

    def down(at, size):
        return jnp.where(odd, cross[pl.ds(at, size), :], pair[pl.ds(at, size), :])

    return up, down


def corners_kernel(levels, layers, pair, cross, out):
    places = Places(levels, layers)
    up, down = came_from(pair, cross)
    under = iota((TILE, 1), 0) < HALO
    tiles = pack_ice(lambda f, k: beyond_ice(up, down, places, layers, f, k), layers)
    planes = {}
    for j, at in zip(CORNER, (places.thick, places.grounded, places.link)):
        planes[j] = jnp.where(under, down(at, TILE), up(at, TILE))
    for n, tile in enumerate((pack_planes(planes), *tiles)):
        out[n * TILE : (n + 1) * TILE, :] = tile


def ocean_kernel(n_narrow, n_parts, n_tiles, layers, *refs):
    parts, refs = refs[:n_parts], refs[n_parts:]
    ocean_x, ocean_y, ocean_t, pair, cross, planes, out, top, field, held, sems = refs
    rows, levels, _ = ocean_x.shape
    places = Places(levels, layers)
    chunks = sems.shape[0] // 6
    step = rows // chunks
    reads = fetch_all(
        [
            (source.at[pl.ds(h * step, step)], field.at[f, pl.ds(h * step, step)])
            for f, source in enumerate((ocean_x, ocean_y, ocean_t))
            for h in range(chunks)
        ],
        sems,
    )
    up, down = came_from(pair, cross)
    lane = iota((1, LANES), 1)
    row = iota((rows, LANES), 0)
    first, last = lane == 0, lane == LANES - 1
    wet = planes[WET]
    wet_halo = plane_halo(merged_planes(parts, rows, n_narrow), WET)
    scale = DIFFUSE * wet
    coef = (
        scale * jnp.where(row > 0, turn(wet, 1, 0), up(places.wet + TILE - 1, 1)),
        scale * jnp.where(row < rows - 1, turn(wet, -1, 0), down(places.wet, 1)),
        scale * jnp.where(first, 0.0, turn(wet, 1, 1)),
        scale * jnp.where(last, 0.0, turn(wet, -1, 1)),
    )
    edge = first | last
    weight = jnp.where(first, turn(wet_halo, 1, 1), turn(wet_halo, -1, 1))
    weight = scale * jnp.where(edge, weight, 0.0)
    centre_coef = 1.0 - (coef[0] + coef[1] + coef[2] + coef[3] + weight)
    even = lane % 2 == 0
    strip_at = (1 + n_tiles) * rows
    came = merged([p[strip_at:, :] for p in parts], even, ~even, n_narrow)
    came = jnp.where(even, turn(came, 1, 1), turn(came, -1, 1))
    packed = [turn(weight[i : i + 1, :], 2 * i, 1) for i in range(rows)]
    packed = functools.reduce(lambda a, b: a + b, packed)
    packed = packed + turn(packed, 2 * rows, 1) + turn(packed, 4 * rows, 1)
    side = packed * came
    writes = []
    for f in range(3):
        reads[f * chunks].wait()
        for h in range(chunks):
            for i in range(h * step, (h + 1) * step):
                if i == (h + 1) * step - 1 and h < chunks - 1:
                    reads[f * chunks + h + 1].wait()
                centre = field[f, i]
                above = field[f, i - 1] if i > 0 else up(f * levels, levels)
                below = field[f, i + 1] if i < rows - 1 else down(f * levels, levels)
                value = centre * centre_coef[i : i + 1, :]
                value = value + above * coef[0][i : i + 1, :]
                value = value + below * coef[1][i : i + 1, :]
                value = value + turn(centre, 1, 1) * coef[2][i : i + 1, :]
                value = value + turn(centre, -1, 1) * coef[3][i : i + 1, :]
                value = value + jnp.where(edge, turn(side, -2 * (f * rows + i), 1), 0.0)
                held[f, i] = value
                if f == 2:
                    top[i] = value[0:TILE, :]
            part = pl.ds(h * step, step)
            level = pl.ds(TILE, levels - TILE) if f == 2 else pl.ds(0, levels)
            copy = pltpu.make_async_copy(
                held.at[f, part, level],
                out.at[f, part, level],
                sems.at[(3 + f) * chunks + h],
            )
            copy.start()
            writes.append(copy)
    for copy in writes:
        copy.wait()


def ice_slots(link_col, kind_col, rows, cap, block, count, n_wide):
    link_row = spread(link_col)
    kind_row = spread(kind_col)
    number = link_col - 1.0
    tile = divide(number, rows)
    inner = number - tile * rows
    tile_row = divide(link_row - 1.0, rows)
    ok = (link_col > 0.5) & (kind_col > -0.5)
    ok_row = (link_row > 0.5) & (kind_row > -0.5)
    hits = (tile == tile_row) & (kind_col == kind_row) & ok_row & (link_row < link_col)
    rank = jnp.sum(hits.astype(F32), axis=1, keepdims=True)
    place = iota((link_col.shape[0], count), 1).astype(F32)

    def hot(keep, target):
        return (place == jnp.where(keep, target, -1.0)).astype(F32)

    top, bottom = inner < 0.5, inner > rows - 1.5
    edge = ok & (top | bottom)
    near = jnp.where(top, tile - 1.0, tile + 1.0)
    near_ok = edge & (near > -0.5) & (near < n_wide - 0.5)
    slot = hot(ok, tile * block + kind_col * cap + rank)
    near_edge = hot(near_ok, near * block + jnp.where(top, 3.0 * cap + 1.0, 3.0 * cap))
    own_edge = hot(edge, tile * block + jnp.where(top, 3.0 * cap, 3.0 * cap + 1.0))
    near_slot = hot(near_ok, near * block)
    own_slot = hot(edge, tile * block)
    return slot, near_edge, own_edge, near_slot, own_slot, bottom.astype(F32)


def around(value):
    return turn(value, 1, 0) + turn(value, -1, 0) + turn(value, 1, 1) + turn(value, -1, 1)


def sweep_layer(vel, k, layers, rate, friction):
    u, v = vel(0, k), vel(1, k)
    ends = [[turn(w, s, axis) for axis in (0, 1) for s in (-1, 1)] for w in (u, v)]
    ux, uy = ends[0][0] - ends[0][1], ends[0][2] - ends[0][3]
    vx, vy = ends[1][0] - ends[1][1], ends[1][2] - ends[1][3]
    cross = uy + vx
    eps2 = ux * (ux + vy) + vy * vy + 0.25 * (cross * cross)
    if k < layers - 1:
        uz, vz = vel(0, k + 1) - u, vel(1, k + 1) - v
        eps2 = eps2 + (uz * uz + vz * vz)
    eps2 = 0.25 * eps2
    eta = rate * jnp.exp((-1.0 / 3.0) * jnp.log(eps2 + STRAIN_FLOOR))
    links_up_down = float((k > 0) + (k < layers - 1))
    diagonal = eta * (2.0 + links_up_down) + 0.5 * around(eta) + friction
    sums = []
    for f, w in enumerate((u, v)):
        total = 0.5 * (ends[f][0] + ends[f][1] + ends[f][2] + ends[f][3])
        if k > 0:
            total = total + vel(f, k - 1)
        if k < layers - 1:
            total = total + vel(f, k + 1)
        sums.append(eta * total + 0.5 * around(eta * w))
    return sums, 1.0 / diagonal, eta * eps2


FLAT = ("thick", "grounded", "inside")


def first_kernel(n_wide, n_narrow, cap, block, n_parts, levels, *refs):
    parts, refs = refs[:n_parts], refs[n_parts:]
    corners, refs = refs[:n_parts], refs[n_parts:]
    ice, pair, cross, planes, sums, inverse, rate, flat, hots, ends, vel = refs
    _, layers, rows, _ = ice.shape
    places = Places(levels, layers)
    n_tiles = ice_tiles(layers)
    up, down = came_from(pair, cross)
    lane = iota((1, LANES), 1)
    width = 2 * LANES
    tall = rows + TILE
    wide_lane = iota((1, width), 1)
    place_wide = lax.axis_index("wide")
    has_right, has_left = narrow_sides(n_narrow)
    has_up, has_down = place_wide > 0, place_wide < n_wide - 1
    under = iota((TILE, 1), 0) < HALO

    def rim(at):
        return jnp.where(under, down(at, TILE), up(at, TILE))

    def below(a, b):
        return jnp.concatenate([a, b], axis=0)

    corner_planes = merged(
        [c[0:TILE, :] for c in corners], right_lanes(16), left_lanes(16), n_narrow
    )
    corner_ice = [
        merged(
            [c[(1 + t) * TILE : (2 + t) * TILE, :] for c in corners],
            right_lanes(8), left_lanes(8), n_narrow,
        )
        for t in range(n_tiles)
    ]
    block_tall = below(merged_planes(parts, rows, n_narrow), corner_planes)
    flat[0] = jnp.concatenate(
        [below(planes[THICK], rim(places.thick)), plane_halo(block_tall, THICK)], axis=1
    )
    grounded_tall = jnp.concatenate(
        [below(planes[GROUNDED], rim(places.grounded)), plane_halo(block_tall, GROUNDED)], axis=1
    )
    flat[1] = grounded_tall
    tall_row = iota((tall, 1), 0)
    inside = (
        ((tall_row < rows) | ((tall_row < rows + HALO) & has_down) | ((tall_row >= rows + HALO) & has_up))
        & (
            (wide_lane < LANES)
            | ((wide_lane < LANES + HALO) & has_right)
            | ((wide_lane >= width - HALO) & has_left)
        )
    ).astype(F32)
    flat[2] = inside
    kind = jnp.where(
        tall_row < rows,
        0.0,
        jnp.where(tall_row < rows + RIM, 2.0, jnp.where(tall_row >= tall - RIM, 1.0, -1.0)),
    )
    count = n_wide * block
    own_link = below(planes[ICE_LINK], rim(places.link))[:, 0:1]
    slots = (rows, cap, block, count, n_wide)
    found = list(ice_slots(own_link, kind, *slots)[:3])
    links = plane_halo(block_tall, ICE_LINK)
    if n_narrow == 2:
        sides = [jnp.max(links, axis=1, keepdims=True)]
    else:
        sides = [links[:, 0:1], links[:, LANES - 1 : LANES]]
    for link in sides:
        slot, _, _, near_slot, own_slot, bottom = ice_slots(link, kind, *slots)
        ends[(len(found) - 3) // 3] = jnp.broadcast_to(bottom, (tall, LANES))
        found += [slot, near_slot, own_slot]
    for n, hot in enumerate(found):
        hots[n * tall : (n + 1) * tall, :] = hot
    ocean_link = planes[OCEAN_LINK][:, 0:1]
    ocean_row = spread(ocean_link)
    tile = divide(ocean_link - 1.0, rows)
    tile_row = divide(ocean_row - 1.0, rows)
    hits = (tile == tile_row) & (ocean_row > 0.5) & (ocean_row < ocean_link)
    rank = jnp.sum(hits.astype(F32), axis=1, keepdims=True)
    target = jnp.where(ocean_link > 0.5, tile * block + 3 * cap + rank, -1.0)
    hots[len(found) * tall :, :] = (iota((rows, count), 1).astype(F32) == target).astype(F32)
    strips = [
        below(a, b) for a, b in zip(merged_ice(parts, rows, n_tiles, n_narrow), corner_ice)
    ]
    edge = (lane < HALO) | (lane >= LANES - HALO)
    for index in range(3 * layers):
        f, k = divmod(index, layers)
        beyond = beyond_ice(up, down, places, layers, f, k)
        t, group = ice_group(index)
        beside = jnp.where(edge, turn(strips[t], -8 * group, 1), 0.0)
        value = jnp.concatenate([below(ice[f, k], beyond), beside], axis=1)
        if f < 2:
            vel[f, k] = value
        else:
            rate[k] = jnp.exp(0.25 * value) * inside
    friction = 0.1 + 9.9 * grounded_tall
    for k in range(layers):
        both, over, _ = sweep_layer(lambda f, n: vel[f, n], k, layers, rate[k], friction)
        for f in range(2):
            sums[f, k] = both[f]
        inverse[k] = over * inside


def final_kernel(n_wide, n_narrow, cap, block, *refs):
    (
        blocks, hots, ends, planes, ice, top, sums, inverse, rate, flat, ocean_in,
        ice_out, ocean_out, thick_out, melt_out,
        vel, result, thin, melted, new_top, sems,
    ) = refs
    _, layers, rows, _ = ice.shape
    tall, width = flat.shape[1:]
    lane = iota((1, LANES), 1)
    count = n_wide * block
    parts = [
        blocks[:, n * block : (n + 1) * block, :].reshape(count, LANES) for n in range(3)
    ]
    found = pick(hots[...], jnp.concatenate(parts, axis=1))

    def got(n, part):
        return found[n * tall : (n + 1) * tall, part * LANES : (part + 1) * LANES]

    wet_main = got(0, 1)
    mixed_main = got(0, 0) + DIFFUSE * (wet_main * got(1, 2) - got(1, 1) * got(2, 2))
    sides = []
    for n in range(3, 3 * (1 if n_narrow == 2 else 2) + 3, 3):
        value, near, own = got(n, 2), got(n + 1, 2), got(n + 2, 2)

        def group(row, j):
            return turn(row, -16 * j, 1)

        wet_got = group(value, PART_WET)
        bottom = ends[n // 3 - 1] > 0.5
        near_warm = jnp.where(bottom, group(near, EDGE_T0), group(near, EDGE_T1))
        near_wet = jnp.where(bottom, group(near, EDGE_W0), group(near, EDGE_W1))
        own_warm = jnp.where(bottom, group(own, EDGE_T1), group(own, EDGE_T0))
        sides.append((value + DIFFUSE * (wet_got * near_warm - near_wet * own_warm), wet_got))
    if len(sides) == 1:
        mixed_side, wet_side = sides[0]
    else:
        mixed_side, wet_side = (jnp.where(lane < HALO, a, b) for a, b in zip(*sides))
    mixed_tall = jnp.concatenate([mixed_main, mixed_side], axis=1)
    wet_tall = jnp.concatenate([wet_main, wet_side], axis=1)
    thick_tall, grounded_tall, inside = flat[0], flat[1], flat[2]
    open_ice = 1.0 - grounded_tall
    draft_tall = 0.9 * thick_tall * open_ice
    melt_tall = GAMMA_MELT * (mixed_tall - wet_tall * (0.0832 - 0.761 * draft_tall))
    new_thick = (thick_tall - TIME_STEP * melt_tall * open_ice) * inside
    thin[...] = new_thick[:rows, :LANES]
    n_hots = hots.shape[0] - rows
    ocean_draft = found[n_hots:, :LANES]
    heat_top = jnp.concatenate([top[i, 0:1, :] for i in range(rows)], axis=0)
    coupled = (planes[OCEAN_LINK] > 0.5).astype(F32)
    melt = GAMMA_MELT * (heat_top - (0.0832 - 0.761 * ocean_draft)) * planes[WET] * coupled
    melted[...] = melt
    cooled = heat_top - 0.2 * melt
    new_top[...] = top[...]
    for i in range(rows):
        new_top[i, 0:1, :] = cooled[i : i + 1, :]
    writes = fetch_all(
        (
            (new_top, ocean_out.at[2, :, pl.ds(0, TILE), :]),
            (thin, thick_out),
            (melted, melt_out),
        ),
        sems,
    )
    surface = new_thick * (0.1 + 0.9 * grounded_tall)
    scale = (-0.5 * SLOPE_SCALE) * new_thick
    stress = (
        scale * (turn(surface, -1, 0) - turn(surface, 1, 0)),
        scale * (turn(surface, -1, 1) - turn(surface, 1, 1)),
    )
    friction = 0.1 + 9.9 * grounded_tall
    for f in range(2):
        for k in range(layers):
            vel[0, f, k] = (sums[f, k] + stress[f]) * inverse[k]
    for sweep in range(1, PICARD):
        last = sweep == PICARD - 1
        old = sweep - 1
        for k in range(layers):
            both, over, heat = sweep_layer(
                lambda f, n: vel[old, f, n], k, layers, rate[k], friction
            )
            for f in range(2):
                value = (both[f] + stress[f]) * over
                if last:
                    result[f, k] = value[:rows, :LANES]
                else:
                    vel[sweep, f, k] = value * inside
            if last:
                result[2, k] = ice[2, k] + HEATING_RATE * heat[:rows, :LANES]
                copy = pltpu.make_async_copy(
                    result.at[:, k], ice_out.at[:, k], sems.at[len(writes)]
                )
                copy.start()
                writes.append(copy)
    for copy in writes:
        copy.wait()


def local(
    ice_x, ice_y, ice_temp, ocean_x, ocean_y, ocean_temp, thick, grounded_mask, wet_mask, ice_links, ocean_links,
):
    n_wide, n_narrow = lax.axis_size("wide"), lax.axis_size("narrow")
    rows, layers, columns = ice_x.shape
    levels = ocean_x.shape[1]
    cap = max(1, 2 * rows // n_wide)
    block = -(-max(4 * cap, 3 * cap + 2) // TILE) * TILE
    assert columns == LANES and ice_links.shape[0] == rows

    def stay(value):
        return pltpu.with_memory_space_constraint(value, pltpu.HBM)

    ice_fields = [stay(x.transpose(1, 0, 2)) for x in (ice_x, ice_y, ice_temp)]
    links = [stay(x.reshape(1, rows)) for x in (ice_links, ocean_links)]
    fields = [stay(x) for x in (ocean_x, ocean_y, ocean_temp)]
    planes_in = [stay(x) for x in (thick, grounded_mask, wet_mask)]
    here = pl.BlockSpec(memory_space=pltpu.VMEM)
    far = pl.BlockSpec(memory_space=pltpu.HBM)
    unread = pl.BlockSpec(memory_space=pl.ANY)
    dma = pltpu.SemaphoreType.DMA

    def array(*shape):
        return jax.ShapeDtypeStruct(shape, F32)

    def kept(*shape):
        return pltpu.VMEM(shape, F32)

    def near(*values):
        return [pltpu.with_memory_space_constraint(value, pltpu.VMEM) for value in values]

    def call(kernel, name, microseconds, out_shape, in_specs, out_specs, scratch=(), **more):
        estimate = pl.CostEstimate(
            flops=int(microseconds * 1.0e9), bytes_accessed=int(microseconds * 3.0e6), transcendentals=0
        )
        return pl.pallas_call(
            kernel, name=name, out_shape=out_shape, in_specs=in_specs, out_specs=out_specs,
            scratch_shapes=scratch, compiler_params=VMEM, cost_estimate=estimate, **more,
        )

    n_tiles = ice_tiles(layers)
    places = Places(levels, layers)
    chunks = 1
    message, to_pair, to_cross, planes, ice = call(
        edges_kernel, "edges", 100.0,
        (
            kept((1 + n_tiles) * rows + levels, LANES), kept(places.end, LANES), kept(places.end, LANES),
            kept(PLANES, rows, LANES), kept(3, layers, rows, LANES),
        ),
        [far] * 11, (here,) * 5,
        [
            pltpu.VMEM((3, rows, levels, LANES), F32),
            pltpu.VMEM((rows, LANES), F32),
            pltpu.VMEM((rows, LANES), jnp.int32),
            pltpu.VMEM((rows, LANES), jnp.int32),
            pltpu.VMEM((2, 1, rows), jnp.int32),
            dma((8,)),
            dma((3 * chunks,)),
        ],
    )(*ice_fields, *fields, *planes_in, *links)

    def narrow(value):
        if n_narrow == 2:
            return [lax.ppermute(value, "narrow", [(0, 1), (1, 0)])]
        ahead = [(i, i + 1) for i in range(n_narrow - 1)]
        return [
            lax.ppermute(value, "narrow", [(j, i) for i, j in ahead]),
            lax.ppermute(value, "narrow", ahead),
        ]

    parts = narrow(message)
    n_parts = len(parts)
    assert n_wide % 2 == 0
    swaps = [[(i, i + 1) for i in range(start, n_wide - 1, 2)] for start in (0, 1)]
    pair, cross = (
        lax.ppermute(value, "wide", swap + [(j, i) for i, j in swap])
        for value, swap in zip((to_pair, to_cross), swaps)
    )
    blocks = call(
        functools.partial(blocks_kernel, n_wide, n_narrow, cap, block, n_parts), "blocks", 100.0,
        kept(n_wide, 3 * block, LANES), [here] * (n_parts + 1), here,
    )(*near(*parts, planes))
    blocks = lax.all_to_all(blocks, "wide", split_axis=0, concat_axis=0, tiled=True)
    corners = narrow(
        call(
            functools.partial(corners_kernel, levels, layers), "corners", 1.0,
            kept((1 + n_tiles) * TILE, LANES), [here] * 2, here,
        )(*near(pair, cross))
    )
    ocean, top = call(
        functools.partial(ocean_kernel, n_narrow, n_parts, n_tiles, layers), "ocean", 100.0,
        (array(3, rows, levels, LANES), kept(rows, TILE, LANES)),
        [here] * n_parts + [far] * 3 + [here] * 3, (far, here),
        [
            pltpu.VMEM((3, rows, levels, LANES), F32),
            pltpu.VMEM((3, rows, levels, LANES), F32),
            dma((6 * chunks,)),
        ],
    )(*near(*parts), *fields, *near(pair, cross, planes))
    wide = 2 * LANES
    tall = rows + TILE
    n_sides = 1 if n_narrow == 2 else 2
    sums, inverse, rate, flat, hots, ends = call(
        functools.partial(first_kernel, n_wide, n_narrow, cap, block, n_parts, levels), "first", 100.0,
        (
            kept(2, layers, tall, wide), kept(layers, tall, wide), kept(layers, tall, wide), kept(3, tall, wide),
            kept((3 + 3 * n_sides) * tall + rows, n_wide * block), kept(n_sides, tall, LANES),
        ),
        [here] * (2 * n_parts + 4), (here,) * 6,
        [pltpu.VMEM((2, layers, tall, wide), F32)],
    )(*near(*parts, *corners, ice, pair, cross, planes))
    ice, ocean, thick_out, melt_out = call(
        functools.partial(final_kernel, n_wide, n_narrow, cap, block), "final", 3.0,
        (
            array(3, layers, rows, LANES), array(3, rows, levels, LANES),
            array(rows, LANES), array(rows, LANES),
        ),
        [here] * 10 + [far], (far,) * 4,
        [
            pltpu.VMEM((PICARD - 1, 2, layers, tall, wide), F32),
            pltpu.VMEM((3, layers, rows, LANES), F32),
            pltpu.VMEM((rows, LANES), F32),
            pltpu.VMEM((rows, LANES), F32),
            pltpu.VMEM((rows, TILE, LANES), F32),
            dma((3 + layers,)),
        ],
        input_output_aliases={10: 1},
    )(*near(blocks, hots, ends, planes, ice, top, sums, inverse, rate, flat), ocean)
    return ice.transpose(0, 2, 1, 3), ocean, thick_out, melt_out


def solution(mesh):
    column = P("wide", None, "narrow")
    plane = P("wide", "narrow")
    return jax.shard_map(
        local,
        mesh=mesh,
        in_specs=(column,) * 6 + (plane,) * 5,
        out_specs=(P(None, "wide", None, "narrow"), P(None, "wide", None, "narrow"), plane, plane),
        check_vma=False,
    )
```

```python
import functools

import jax
import jax.numpy as jnp
from jax import lax
from jax.experimental import pallas as pl
from jax.experimental.pallas import tpu as pltpu
from jax.sharding import PartitionSpec as P

PICARD = 2
DIFFUSE = 0.2
GAMMA_MELT = 0.5
TIME_STEP = 0.05
SLOPE_SCALE = 0.1
STRAIN_FLOOR = 0.01
HEATING_RATE = 0.01

LANES = 128
TILE = 8
ORDER = (2, 1, 3, 0)
HALO = 4
RIM = 3
VMEM = pltpu.CompilerParams(vmem_limit_bytes=16 * 1024 * 1024)
F32 = jnp.float32

THICK, GROUNDED, OCEAN_T, WET, ICE_LINK, OCEAN_LINK = range(6)
PLANES = 6
CORNER = (THICK, GROUNDED, ICE_LINK)
PART, EDGE_T0, EDGE_T1, EDGE_W0, PART_WET, EDGE_W1 = range(6)


def iota(shape, axis):
    return lax.broadcasted_iota(jnp.int32, shape, axis)


def right_lanes(period):
    lane = iota((1, LANES), 1)
    return lane % period < HALO


def left_lanes(period):
    lane = iota((1, LANES), 1)
    return lane % period >= period - HALO


def spread(column, count=LANES):
    rows = column.shape[0]
    eye = iota((rows, count), 0) == iota((rows, count), 1)
    return jnp.sum(jnp.where(eye, column, 0.0), axis=0, keepdims=True)


def upright(row):
    count = row.shape[1]
    eye = iota((count, count), 0) == iota((count, count), 1)
    return jnp.sum(jnp.where(eye, row, 0.0), axis=1, keepdims=True)


def turn(value, shift, axis):
    shift %= value.shape[axis]
    return pltpu.roll(value, shift, axis) if shift else value


def fetch_all(pairs, sems):
    copies = [pltpu.make_async_copy(a, b, sems.at[i]) for i, (a, b) in enumerate(pairs)]
    for copy in copies:
        copy.start()
    return copies


def divide(whole, part):
    return jnp.floor((whole + 0.5) * (1.0 / part))


def pick(hot, value):
    hot = hot.astype(jnp.bfloat16)
    pieces = []
    for _ in range(3):
        pieces.append(value.astype(jnp.bfloat16))
        value = value - pieces[-1].astype(F32)
    a, b, c = (jnp.dot(hot, p, preferred_element_type=F32) for p in pieces)
    return (c + b) + a


def narrow_sides(n_narrow):
    place = lax.axis_index("narrow")
    return place < n_narrow - 1, place > 0


def merged(parts, right, left, n_narrow):
    has_right, has_left = narrow_sides(n_narrow)
    from_right, from_left = parts[0], parts[-1]
    if len(parts) == 1:
        keep = (right & has_right) | (left & has_left)
        return jnp.where(keep, from_right, 0.0)
    return jnp.where(right, from_right, jnp.where(left, from_left, 0.0))


def ice_group(index):
    return divmod(index, LANES // 8)


def ice_tiles(layers):
    return ice_group(3 * layers - 1)[0] + 1


def ice_pairs(layers):
    return -(-3 * layers // 2)


class Places:
    def __init__(self, levels, layers):
        self.ice = 3 * levels
        self.thick = self.ice + ice_pairs(layers) * TILE
        self.grounded = self.thick + TILE
        self.wet = self.grounded + TILE
        self.link = self.wet + TILE
        self.end = self.link + TILE


def odd_place():
    return lax.axis_index("wide") % 2 == 1


def pack_ice(tile_of, layers):
    lane = iota((1, LANES), 1)
    tiles = [None] * ice_tiles(layers)
    for index in range(3 * layers):
        tile, group = ice_group(index)
        turned = turn(tile_of(*divmod(index, layers)), 8 * group, 1)
        before = jnp.zeros_like(turned) if group == 0 else tiles[tile]
        tiles[tile] = jnp.where((lane + HALO) % LANES // 8 == group, turned, before)
    return tiles


def pack_planes(planes):
    lane = iota((1, LANES), 1)
    total = None
    for j, plane in planes.items():
        turned = turn(plane, 16 * j, 1)
        before = jnp.zeros_like(turned) if total is None else total
        total = jnp.where((lane + HALO) % LANES // 16 == j, turned, before)
    return total


def edges_kernel(
    ice_x, ice_y, ice_t, ocean_x, ocean_y, ocean_t, thick, grounded, wet, ice_links, ocean_links,
    out, pair, cross, planes, ice, field, thick_v, grounded_v, wet_v, links_v, sems, field_sems,
):
    layers, rows, _ = ice_x.shape
    levels = ocean_x.shape[1]
    chunks = field_sems.shape[0] // 3
    step = rows // chunks
    copies = fetch_all(
        (
            (ice_x, ice.at[0]),
            (ice_y, ice.at[1]),
            (ice_t, ice.at[2]),
            (thick, thick_v),
            (grounded, grounded_v),
            (wet, wet_v),
            (ice_links, links_v.at[0]),
            (ocean_links, links_v.at[1]),
        ),
        sems,
    )
    field_copies = fetch_all(
        [
            (source.at[pl.ds(h * step, step)], field.at[f, pl.ds(h * step, step)])
            for f, source in reversed(list(enumerate((ocean_x, ocean_y, ocean_t))))
            for h in range(chunks)
        ],
        field_sems,
    )
    places = Places(levels, layers)
    odd = odd_place()

    def send(at, size, lasts, firsts):
        pair[at : at + size, :] = jnp.where(odd, firsts, lasts)
        cross[at : at + size, :] = jnp.where(odd, lasts, firsts)

    lane = iota((1, LANES), 1)
    for copy in copies:
        copy.wait()
    for tile, value in enumerate(pack_ice(lambda f, k: ice[f, k], layers)):
        out[(1 + tile) * rows : (2 + tile) * rows, :] = value
    upper = iota((TILE, 1), 0) >= HALO
    half = ice_pairs(layers)
    for m in range(half):
        ends = []
        for index in (m, m + half):
            f, k = divmod(min(index, 3 * layers - 1), layers)
            ends.append((ice[f, k, rows - TILE :, :], ice[f, k, :TILE, :]))
        send(
            places.ice + m * TILE,
            TILE,
            jnp.where(upper, ends[0][0], turn(ends[1][0], HALO, 0)),
            jnp.where(upper, turn(ends[1][1], HALO, 0), ends[0][1]),
        )
    planes[THICK] = thick_v[...]
    planes[GROUNDED] = grounded_v[...].astype(F32)
    planes[WET] = wet_v[...].astype(F32)
    for k in range(2):
        link = upright(links_v[k].astype(F32)) + 1.0
        planes[ICE_LINK + k] = jnp.broadcast_to(link, (rows, LANES))
    for at, j in (
        (places.thick, THICK), (places.grounded, GROUNDED), (places.wet, WET), (places.link, ICE_LINK),
    ):
        send(at, TILE, planes[j, rows - TILE :, :], planes[j, :TILE, :])
    total = jnp.zeros((levels, LANES), F32)
    for n, f in enumerate((2, 1, 0)):
        for h in range(chunks):
            field_copies[n * chunks + h].wait()
            for i in range(h * step, (h + 1) * step):
                j = f * rows + i
                turned = turn(field[f, i], 2 * j, 1)
                total = jnp.where((lane + 1) % LANES // 2 == j, turned, total)
        send(f * levels, levels, field[f, rows - 1], field[f, 0])
        if f == 2:
            for i in range(rows):
                planes[OCEAN_T, i : i + 1, :] = field[2, i, 0:1, :]
            out[0:rows, :] = pack_planes({j: planes[j] for j in range(PLANES)})
    out[(1 + ice_tiles(layers)) * rows :, :] = total


def plane_halo(block, group):
    lane = iota((1, LANES), 1)
    turned = turn(block, -16 * group, 1)
    return jnp.where((lane < HALO) | (lane >= LANES - HALO), turned, 0.0)


def merged_planes(parts, rows, n_narrow):
    return merged([p[0:rows, :] for p in parts], right_lanes(16), left_lanes(16), n_narrow)


def merged_ice(parts, rows, n_tiles, n_narrow):
    return [
        merged(
            [p[(1 + t) * rows : (2 + t) * rows, :] for p in parts],
            right_lanes(8), left_lanes(8), n_narrow,
        )
        for t in range(n_tiles)
    ]


def ranks(own_col, member_col, order_sub, order_lane, own_row):
    hits = (own_col == own_row) & member_col & (order_sub < order_lane)
    return jnp.sum(hits.astype(F32), axis=0, keepdims=True)


def ocean_slots(link_col, rows, n_wide, cap, block):
    link_row = spread(link_col)
    parts = []
    for link in (link_col, link_row):
        number = link - 1.0
        tile = divide(number, rows)
        inner = number - tile * rows
        ok = link > 0.5
        parts.append(
            (
                tile,
                (
                    ok,
                    ok & (inner >= rows - RIM) & (tile < n_wide - 1.5),
                    ok & (inner < RIM) & (tile > 0.5),
                ),
            )
        )
    (tile_col, member_col), (tile_row, member_row) = parts
    order_sub, order_lane = iota((rows, LANES), 0), iota((rows, LANES), 1)
    place = iota((n_wide * block, LANES), 0).astype(F32)
    total = jnp.zeros((n_wide * block, LANES), F32)
    for k, shift in enumerate((0.0, 1.0, -1.0)):
        rank = ranks(tile_col, member_col[k], order_sub, order_lane, tile_row)
        target = jnp.where(
            member_row[k], (tile_row + shift) * block + (k * cap + rank), -1.0
        )
        total = total + (place == target).astype(F32)
    return total[:, :rows]


def draft_slots(link_col, rows, n_wide, cap, block):
    link_row = spread(link_col)
    tile_col, tile_row = divide(link_col - 1.0, rows), divide(link_row - 1.0, rows)
    order_sub, order_lane = iota((rows, LANES), 0), iota((rows, LANES), 1)
    rank = ranks(tile_col, link_col > 0.5, order_sub, order_lane, tile_row)
    target = jnp.where(link_row > 0.5, tile_row * block + (3 * cap + rank), -1.0)
    place = iota((n_wide * block, LANES), 0).astype(F32)
    return (place == target).astype(F32)[:, :rows]


def exchange_order(n_wide):
    quarter = n_wide // 4
    if n_wide % 4:
        return list(range(n_wide))
    return [q * quarter + j for q in ORDER for j in reversed(range(quarter))]


def blocks_kernel(n_wide, n_narrow, cap, block, n_parts, *refs):
    parts, refs = refs[:n_parts], refs[n_parts:]
    planes, blocks = refs
    rows = planes.shape[1]
    lane = iota((1, LANES), 1)
    plane_block = merged_planes(parts, rows, n_narrow)
    thick_plane, grounded_plane, wet_plane = planes[THICK], planes[GROUNDED], planes[WET]
    wet_all = jnp.concatenate([wet_plane, plane_halo(plane_block, WET)], axis=1)
    warm = wet_all * jnp.concatenate([planes[OCEAN_T], plane_halo(plane_block, OCEAN_T)], axis=1)
    width = 2 * LANES
    row = iota((rows, width), 0)
    sums = []
    for value in (wet_all, warm):
        total = pltpu.roll(value, 1, 1) + pltpu.roll(value, width - 1, 1)
        total = total + jnp.where(row > 0, pltpu.roll(value, 1, 0), 0.0)
        sums.append(total + jnp.where(row < rows - 1, pltpu.roll(value, rows - 1, 0), 0.0))
    mixed = warm + DIFFUSE * (wet_all * sums[1] - warm * sums[0])
    draft = 0.9 * thick_plane * (1.0 - grounded_plane)
    own_slots = ocean_slots(planes[OCEAN_LINK][:, 0:1], rows, n_wide, cap, block)
    main = pick(own_slots, jnp.concatenate([mixed[:, :LANES], wet_plane], axis=1))
    count = n_wide * block
    slot = iota((count, 1), 0) % block
    first = main[:, :LANES] + pick(draft_slots(planes[ICE_LINK][:, 0:1], rows, n_wide, cap, block), draft)
    second = jnp.where(
        slot == 3 * cap,
        wet_plane[0:1, :],
        jnp.where(slot == 3 * cap + 1, wet_plane[rows - 1 : rows, :], main[:, LANES:]),
    )
    edge = (lane < HALO) | (lane >= LANES - HALO)
    mixed_edge = jnp.where(edge, mixed[:, LANES:], 0.0)
    wet_edge = wet_all[:, LANES:]
    warm_edge = warm[:, LANES:]
    packed = mixed_edge + pltpu.roll(wet_edge, 16 * PART_WET, 1)
    links = plane_halo(plane_block, OCEAN_LINK)
    if n_narrow == 2:
        third = pick(
            ocean_slots(jnp.max(links, axis=1, keepdims=True), rows, n_wide, cap, block), packed
        )
    else:
        third = pick(
            ocean_slots(links[:, 0:1], rows, n_wide, cap, block),
            jnp.where(right_lanes(16), packed, 0.0),
        ) + pick(
            ocean_slots(links[:, LANES - 1 : LANES], rows, n_wide, cap, block),
            jnp.where(left_lanes(16), packed, 0.0),
        )
    last = rows - 1
    ends = (
        pltpu.roll(warm_edge[0:1, :], 16 * EDGE_T0, 1)
        + pltpu.roll(warm_edge[last:, :], 16 * EDGE_T1, 1)
        + pltpu.roll(wet_edge[0:1, :], 16 * EDGE_W0, 1)
        + pltpu.roll(wet_edge[last:, :], 16 * EDGE_W1, 1)
    )
    third = jnp.where(
        slot == 3 * cap,
        warm[0:1, :LANES],
        jnp.where(slot == 3 * cap + 1, warm[last:, :LANES], third + ends),
    )
    for k, value in enumerate((first, second, third)):
        for j, tile in enumerate(exchange_order(n_wide)):
            blocks[j, k * block : (k + 1) * block, :] = value[tile * block : (tile + 1) * block, :]


def beyond_ice(up, down, places, layers, f, k):
    under = iota((TILE, 1), 0) < HALO
    index, half = f * layers + k, ice_pairs(layers)
    at = places.ice + index % half * TILE
    if index < half:
        return jnp.where(under, down(at, TILE), up(at, TILE))
    return turn(jnp.where(under, up(at, TILE), down(at, TILE)), HALO, 0)


def came_from(pair, cross):
    odd = odd_place()

    def up(at, size):
        return jnp.where(odd, pair[pl.ds(at, size), :], cross[pl.ds(at, size), :])

    def down(at, size):
        return jnp.where(odd, cross[pl.ds(at, size), :], pair[pl.ds(at, size), :])

    return up, down


def corners_kernel(levels, layers, pair, cross, out):
    places = Places(levels, layers)
    up, down = came_from(pair, cross)
    under = iota((TILE, 1), 0) < HALO
    tiles = pack_ice(lambda f, k: beyond_ice(up, down, places, layers, f, k), layers)
    planes = {}
    for j, at in zip(CORNER, (places.thick, places.grounded, places.link)):
        planes[j] = jnp.where(under, down(at, TILE), up(at, TILE))
    for n, tile in enumerate((pack_planes(planes), *tiles)):
        out[n * TILE : (n + 1) * TILE, :] = tile


def ocean_kernel(n_narrow, n_parts, n_tiles, layers, *refs):
    parts, refs = refs[:n_parts], refs[n_parts:]
    ocean_x, ocean_y, ocean_t, pair, cross, planes, out, top, field, held, sems = refs
    rows, levels, _ = ocean_x.shape
    places = Places(levels, layers)
    chunks = sems.shape[0] // 6
    step = rows // chunks
    reads = fetch_all(
        [
            (source.at[pl.ds(h * step, step)], field.at[f, pl.ds(h * step, step)])
            for f, source in enumerate((ocean_x, ocean_y, ocean_t))
            for h in range(chunks)
        ],
        sems,
    )
    up, down = came_from(pair, cross)
    lane = iota((1, LANES), 1)
    row = iota((rows, LANES), 0)
    first, last = lane == 0, lane == LANES - 1
    wet = planes[WET]
    wet_halo = plane_halo(merged_planes(parts, rows, n_narrow), WET)
    scale = DIFFUSE * wet
    coef = (
        scale * jnp.where(row > 0, turn(wet, 1, 0), up(places.wet + TILE - 1, 1)),
        scale * jnp.where(row < rows - 1, turn(wet, -1, 0), down(places.wet, 1)),
        scale * jnp.where(first, 0.0, turn(wet, 1, 1)),
        scale * jnp.where(last, 0.0, turn(wet, -1, 1)),
    )
    edge = first | last
    weight = jnp.where(first, turn(wet_halo, 1, 1), turn(wet_halo, -1, 1))
    weight = scale * jnp.where(edge, weight, 0.0)
    centre_coef = 1.0 - (coef[0] + coef[1] + coef[2] + coef[3] + weight)
    even = lane % 2 == 0
    strip_at = (1 + n_tiles) * rows
    came = merged([p[strip_at:, :] for p in parts], even, ~even, n_narrow)
    came = jnp.where(even, turn(came, 1, 1), turn(came, -1, 1))
    packed = [turn(weight[i : i + 1, :], 2 * i, 1) for i in range(rows)]
    packed = functools.reduce(lambda a, b: a + b, packed)
    packed = packed + turn(packed, 2 * rows, 1) + turn(packed, 4 * rows, 1)
    side = packed * came
    writes = []
    for f in range(3):
        reads[f * chunks].wait()
        for h in range(chunks):
            for i in range(h * step, (h + 1) * step):
                if i == (h + 1) * step - 1 and h < chunks - 1:
                    reads[f * chunks + h + 1].wait()
                centre = field[f, i]
                above = field[f, i - 1] if i > 0 else up(f * levels, levels)
                below = field[f, i + 1] if i < rows - 1 else down(f * levels, levels)
                value = centre * centre_coef[i : i + 1, :]
                value = value + above * coef[0][i : i + 1, :]
                value = value + below * coef[1][i : i + 1, :]
                value = value + turn(centre, 1, 1) * coef[2][i : i + 1, :]
                value = value + turn(centre, -1, 1) * coef[3][i : i + 1, :]
                value = value + jnp.where(edge, turn(side, -2 * (f * rows + i), 1), 0.0)
                held[f, i] = value
                if f == 2:
                    top[i] = value[0:TILE, :]
            part = pl.ds(h * step, step)
            level = pl.ds(TILE, levels - TILE) if f == 2 else pl.ds(0, levels)
            copy = pltpu.make_async_copy(
                held.at[f, part, level],
                out.at[f, part, level],
                sems.at[(3 + f) * chunks + h],
            )
            copy.start()
            writes.append(copy)
    for copy in writes:
        copy.wait()


def ice_slots(link_col, kind_col, rows, cap, block, count, n_wide):
    link_row = spread(link_col)
    kind_row = spread(kind_col)
    number = link_col - 1.0
    tile = divide(number, rows)
    inner = number - tile * rows
    tile_row = divide(link_row - 1.0, rows)
    ok = (link_col > 0.5) & (kind_col > -0.5)
    ok_row = (link_row > 0.5) & (kind_row > -0.5)
    hits = (tile == tile_row) & (kind_col == kind_row) & ok_row & (link_row < link_col)
    rank = jnp.sum(hits.astype(F32), axis=1, keepdims=True)
    place = iota((link_col.shape[0], count), 1).astype(F32)

    def hot(keep, target):
        return (place == jnp.where(keep, target, -1.0)).astype(F32)

    top, bottom = inner < 0.5, inner > rows - 1.5
    edge = ok & (top | bottom)
    near = jnp.where(top, tile - 1.0, tile + 1.0)
    near_ok = edge & (near > -0.5) & (near < n_wide - 0.5)
    slot = hot(ok, tile * block + kind_col * cap + rank)
    near_edge = hot(near_ok, near * block + jnp.where(top, 3.0 * cap + 1.0, 3.0 * cap))
    own_edge = hot(edge, tile * block + jnp.where(top, 3.0 * cap, 3.0 * cap + 1.0))
    near_slot = hot(near_ok, near * block)
    own_slot = hot(edge, tile * block)
    return slot, near_edge, own_edge, near_slot, own_slot, bottom.astype(F32)


def around(value):
    return turn(value, 1, 0) + turn(value, -1, 0) + turn(value, 1, 1) + turn(value, -1, 1)


def sweep_layer(vel, k, layers, rate, friction):
    u, v = vel(0, k), vel(1, k)
    ends = [[turn(w, s, axis) for axis in (0, 1) for s in (-1, 1)] for w in (u, v)]
    ux, uy = ends[0][0] - ends[0][1], ends[0][2] - ends[0][3]
    vx, vy = ends[1][0] - ends[1][1], ends[1][2] - ends[1][3]
    cross = uy + vx
    eps2 = ux * (ux + vy) + vy * vy + 0.25 * (cross * cross)
    if k < layers - 1:
        uz, vz = vel(0, k + 1) - u, vel(1, k + 1) - v
        eps2 = eps2 + (uz * uz + vz * vz)
    eps2 = 0.25 * eps2
    eta = rate * jnp.exp((-1.0 / 3.0) * jnp.log(eps2 + STRAIN_FLOOR))
    links_up_down = float((k > 0) + (k < layers - 1))
    diagonal = eta * (2.0 + links_up_down) + 0.5 * around(eta) + friction
    sums = []
    for f, w in enumerate((u, v)):
        total = 0.5 * (ends[f][0] + ends[f][1] + ends[f][2] + ends[f][3])
        if k > 0:
            total = total + vel(f, k - 1)
        if k < layers - 1:
            total = total + vel(f, k + 1)
        sums.append(eta * total + 0.5 * around(eta * w))
    return sums, 1.0 / diagonal, eta * eps2


FLAT = ("thick", "grounded", "inside")


def first_kernel(n_wide, n_narrow, cap, block, n_parts, levels, *refs):
    parts, refs = refs[:n_parts], refs[n_parts:]
    corners, refs = refs[:n_parts], refs[n_parts:]
    ice, pair, cross, planes, sums, inverse, rate, flat, hots, ends, vel = refs
    _, layers, rows, _ = ice.shape
    places = Places(levels, layers)
    n_tiles = ice_tiles(layers)
    up, down = came_from(pair, cross)
    lane = iota((1, LANES), 1)
    width = 2 * LANES
    tall = rows + TILE
    wide_lane = iota((1, width), 1)
    place_wide = lax.axis_index("wide")
    has_right, has_left = narrow_sides(n_narrow)
    has_up, has_down = place_wide > 0, place_wide < n_wide - 1
    under = iota((TILE, 1), 0) < HALO

    def rim(at):
        return jnp.where(under, down(at, TILE), up(at, TILE))

    def below(a, b):
        return jnp.concatenate([a, b], axis=0)

    corner_planes = merged(
        [c[0:TILE, :] for c in corners], right_lanes(16), left_lanes(16), n_narrow
    )
    corner_ice = [
        merged(
            [c[(1 + t) * TILE : (2 + t) * TILE, :] for c in corners],
            right_lanes(8), left_lanes(8), n_narrow,
        )
        for t in range(n_tiles)
    ]
    block_tall = below(merged_planes(parts, rows, n_narrow), corner_planes)
    flat[0] = jnp.concatenate(
        [below(planes[THICK], rim(places.thick)), plane_halo(block_tall, THICK)], axis=1
    )
    grounded_tall = jnp.concatenate(
        [below(planes[GROUNDED], rim(places.grounded)), plane_halo(block_tall, GROUNDED)], axis=1
    )
    flat[1] = grounded_tall
    tall_row = iota((tall, 1), 0)
    inside = (
        ((tall_row < rows) | ((tall_row < rows + HALO) & has_down) | ((tall_row >= rows + HALO) & has_up))
        & (
            (wide_lane < LANES)
            | ((wide_lane < LANES + HALO) & has_right)
            | ((wide_lane >= width - HALO) & has_left)
        )
    ).astype(F32)
    flat[2] = inside
    kind = jnp.where(
        tall_row < rows,
        0.0,
        jnp.where(tall_row < rows + RIM, 2.0, jnp.where(tall_row >= tall - RIM, 1.0, -1.0)),
    )
    count = n_wide * block
    own_link = below(planes[ICE_LINK], rim(places.link))[:, 0:1]
    slots = (rows, cap, block, count, n_wide)
    found = list(ice_slots(own_link, kind, *slots)[:3])
    links = plane_halo(block_tall, ICE_LINK)
    if n_narrow == 2:
        sides = [jnp.max(links, axis=1, keepdims=True)]
    else:
        sides = [links[:, 0:1], links[:, LANES - 1 : LANES]]
    for link in sides:
        slot, _, _, near_slot, own_slot, bottom = ice_slots(link, kind, *slots)
        ends[(len(found) - 3) // 3] = jnp.broadcast_to(bottom, (tall, LANES))
        found += [slot, near_slot, own_slot]
    for n, hot in enumerate(found):
        hots[n * tall : (n + 1) * tall, :] = hot
    ocean_link = planes[OCEAN_LINK][:, 0:1]
    ocean_row = spread(ocean_link)
    tile = divide(ocean_link - 1.0, rows)
    tile_row = divide(ocean_row - 1.0, rows)
    hits = (tile == tile_row) & (ocean_row > 0.5) & (ocean_row < ocean_link)
    rank = jnp.sum(hits.astype(F32), axis=1, keepdims=True)
    target = jnp.where(ocean_link > 0.5, tile * block + 3 * cap + rank, -1.0)
    hots[len(found) * tall :, :] = (iota((rows, count), 1).astype(F32) == target).astype(F32)
    strips = [
        below(a, b) for a, b in zip(merged_ice(parts, rows, n_tiles, n_narrow), corner_ice)
    ]
    edge = (lane < HALO) | (lane >= LANES - HALO)
    for index in range(3 * layers):
        f, k = divmod(index, layers)
        beyond = beyond_ice(up, down, places, layers, f, k)
        t, group = ice_group(index)
        beside = jnp.where(edge, turn(strips[t], -8 * group, 1), 0.0)
        value = jnp.concatenate([below(ice[f, k], beyond), beside], axis=1)
        if f < 2:
            vel[f, k] = value
        else:
            rate[k] = jnp.exp(0.25 * value) * inside
    friction = 0.1 + 9.9 * grounded_tall
    for k in range(layers):
        both, over, _ = sweep_layer(lambda f, n: vel[f, n], k, layers, rate[k], friction)
        for f in range(2):
            sums[f, k] = both[f]
        inverse[k] = over * inside


def final_kernel(n_wide, n_narrow, cap, block, *refs):
    (
        blocks, hots, ends, planes, ice, top, sums, inverse, rate, flat, ocean_in,
        ice_out, ocean_out, thick_out, melt_out,
        vel, result, thin, melted, new_top, sems,
    ) = refs
    _, layers, rows, _ = ice.shape
    tall, width = flat.shape[1:]
    lane = iota((1, LANES), 1)
    order = exchange_order(n_wide)
    parts = [
        jnp.concatenate(
            [blocks[order.index(t), n * block : (n + 1) * block, :] for t in range(n_wide)], axis=0
        )
        for n in range(3)
    ]
    found = pick(hots[...], jnp.concatenate(parts, axis=1))

    def got(n, part):
        return found[n * tall : (n + 1) * tall, part * LANES : (part + 1) * LANES]

    wet_main = got(0, 1)
    mixed_main = got(0, 0) + DIFFUSE * (wet_main * got(1, 2) - got(1, 1) * got(2, 2))
    sides = []
    for n in range(3, 3 * (1 if n_narrow == 2 else 2) + 3, 3):
        value, near, own = got(n, 2), got(n + 1, 2), got(n + 2, 2)

        def group(row, j):
            return turn(row, -16 * j, 1)

        wet_got = group(value, PART_WET)
        bottom = ends[n // 3 - 1] > 0.5
        near_warm = jnp.where(bottom, group(near, EDGE_T0), group(near, EDGE_T1))
        near_wet = jnp.where(bottom, group(near, EDGE_W0), group(near, EDGE_W1))
        own_warm = jnp.where(bottom, group(own, EDGE_T1), group(own, EDGE_T0))
        sides.append((value + DIFFUSE * (wet_got * near_warm - near_wet * own_warm), wet_got))
    if len(sides) == 1:
        mixed_side, wet_side = sides[0]
    else:
        mixed_side, wet_side = (jnp.where(lane < HALO, a, b) for a, b in zip(*sides))
    mixed_tall = jnp.concatenate([mixed_main, mixed_side], axis=1)
    wet_tall = jnp.concatenate([wet_main, wet_side], axis=1)
    thick_tall, grounded_tall, inside = flat[0], flat[1], flat[2]
    open_ice = 1.0 - grounded_tall
    draft_tall = 0.9 * thick_tall * open_ice
    melt_tall = GAMMA_MELT * (mixed_tall - wet_tall * (0.0832 - 0.761 * draft_tall))
    new_thick = (thick_tall - TIME_STEP * melt_tall * open_ice) * inside
    thin[...] = new_thick[:rows, :LANES]
    n_hots = hots.shape[0] - rows
    ocean_draft = found[n_hots:, :LANES]
    heat_top = jnp.concatenate([top[i, 0:1, :] for i in range(rows)], axis=0)
    coupled = (planes[OCEAN_LINK] > 0.5).astype(F32)
    melt = GAMMA_MELT * (heat_top - (0.0832 - 0.761 * ocean_draft)) * planes[WET] * coupled
    melted[...] = melt
    cooled = heat_top - 0.2 * melt
    new_top[...] = top[...]
    for i in range(rows):
        new_top[i, 0:1, :] = cooled[i : i + 1, :]
    writes = fetch_all(
        (
            (new_top, ocean_out.at[2, :, pl.ds(0, TILE), :]),
            (thin, thick_out),
            (melted, melt_out),
        ),
        sems,
    )
    surface = new_thick * (0.1 + 0.9 * grounded_tall)
    scale = (-0.5 * SLOPE_SCALE) * new_thick
    stress = (
        scale * (turn(surface, -1, 0) - turn(surface, 1, 0)),
        scale * (turn(surface, -1, 1) - turn(surface, 1, 1)),
    )
    friction = 0.1 + 9.9 * grounded_tall
    for f in range(2):
        for k in range(layers):
            vel[0, f, k] = (sums[f, k] + stress[f]) * inverse[k]
    for sweep in range(1, PICARD):
        last = sweep == PICARD - 1
        old = sweep - 1
        for k in range(layers):
            both, over, heat = sweep_layer(
                lambda f, n: vel[old, f, n], k, layers, rate[k], friction
            )
            for f in range(2):
                value = (both[f] + stress[f]) * over
                if last:
                    result[f, k] = value[:rows, :LANES]
                else:
                    vel[sweep, f, k] = value * inside
            if last:
                result[2, k] = ice[2, k] + HEATING_RATE * heat[:rows, :LANES]
                copy = pltpu.make_async_copy(
                    result.at[:, k], ice_out.at[:, k], sems.at[len(writes)]
                )
                copy.start()
                writes.append(copy)
    for copy in writes:
        copy.wait()


def local(
    ice_x, ice_y, ice_temp, ocean_x, ocean_y, ocean_temp, thick, grounded_mask, wet_mask, ice_links, ocean_links,
):
    n_wide, n_narrow = lax.axis_size("wide"), lax.axis_size("narrow")
    rows, layers, columns = ice_x.shape
    levels = ocean_x.shape[1]
    cap = max(1, 2 * rows // n_wide)
    block = -(-max(4 * cap, 3 * cap + 2) // TILE) * TILE
    assert columns == LANES and ice_links.shape[0] == rows

    def stay(value):
        return pltpu.with_memory_space_constraint(value, pltpu.HBM)

    ice_fields = [stay(x.transpose(1, 0, 2)) for x in (ice_x, ice_y, ice_temp)]
    links = [stay(x.reshape(1, rows)) for x in (ice_links, ocean_links)]
    fields = [stay(x) for x in (ocean_x, ocean_y, ocean_temp)]
    planes_in = [stay(x) for x in (thick, grounded_mask, wet_mask)]
    here = pl.BlockSpec(memory_space=pltpu.VMEM)
    far = pl.BlockSpec(memory_space=pltpu.HBM)
    unread = pl.BlockSpec(memory_space=pl.ANY)
    dma = pltpu.SemaphoreType.DMA

    def array(*shape):
        return jax.ShapeDtypeStruct(shape, F32)

    def kept(*shape):
        return pltpu.VMEM(shape, F32)

    def near(*values):
        return [pltpu.with_memory_space_constraint(value, pltpu.VMEM) for value in values]

    def call(kernel, name, microseconds, out_shape, in_specs, out_specs, scratch=(), **more):
        estimate = pl.CostEstimate(
            flops=int(microseconds * 1.0e9), bytes_accessed=int(microseconds * 3.0e6), transcendentals=0
        )
        return pl.pallas_call(
            kernel, name=name, out_shape=out_shape, in_specs=in_specs, out_specs=out_specs,
            scratch_shapes=scratch, compiler_params=VMEM, cost_estimate=estimate, **more,
        )

    n_tiles = ice_tiles(layers)
    places = Places(levels, layers)
    chunks = 1
    message, to_pair, to_cross, planes, ice = call(
        edges_kernel, "edges", 4.0,
        (
            kept((1 + n_tiles) * rows + levels, LANES), kept(places.end, LANES), kept(places.end, LANES),
            kept(PLANES, rows, LANES), kept(3, layers, rows, LANES),
        ),
        [far] * 11, (here,) * 5,
        [
            pltpu.VMEM((3, rows, levels, LANES), F32),
            pltpu.VMEM((rows, LANES), F32),
            pltpu.VMEM((rows, LANES), jnp.int32),
            pltpu.VMEM((rows, LANES), jnp.int32),
            pltpu.VMEM((2, 1, rows), jnp.int32),
            dma((8,)),
            dma((3 * chunks,)),
        ],
    )(*ice_fields, *fields, *planes_in, *links)

    def narrow(value):
        if n_narrow == 2:
            return [lax.ppermute(value, "narrow", [(0, 1), (1, 0)])]
        ahead = [(i, i + 1) for i in range(n_narrow - 1)]
        return [
            lax.ppermute(value, "narrow", [(j, i) for i, j in ahead]),
            lax.ppermute(value, "narrow", ahead),
        ]

    parts = narrow(message)
    n_parts = len(parts)
    assert n_wide % 2 == 0
    swaps = [[(i, i + 1) for i in range(start, n_wide - 1, 2)] for start in (0, 1)]
    pair, cross = (
        lax.ppermute(value, "wide", swap + [(j, i) for i, j in swap])
        for value, swap in zip((to_pair, to_cross), swaps)
    )
    blocks = call(
        functools.partial(blocks_kernel, n_wide, n_narrow, cap, block, n_parts), "blocks", 4.0,
        kept(n_wide, 3 * block, LANES), [here] * (n_parts + 1), here,
    )(*near(*parts, planes))
    blocks = lax.all_to_all(
        blocks, "wide", split_axis=0, concat_axis=0, tiled=True, axis_index_groups=[exchange_order(n_wide)]
    )
    corners = narrow(
        call(
            functools.partial(corners_kernel, levels, layers), "corners", 1.0,
            kept((1 + n_tiles) * TILE, LANES), [here] * 2, here,
        )(*near(pair, cross))
    )
    ocean, top = call(
        functools.partial(ocean_kernel, n_narrow, n_parts, n_tiles, layers), "ocean", 4.0,
        (array(3, rows, levels, LANES), kept(rows, TILE, LANES)),
        [here] * n_parts + [far] * 3 + [here] * 3, (far, here),
        [
            pltpu.VMEM((3, rows, levels, LANES), F32),
            pltpu.VMEM((3, rows, levels, LANES), F32),
            dma((6 * chunks,)),
        ],
    )(*near(*parts), *fields, *near(pair, cross, planes))
    wide = 2 * LANES
    tall = rows + TILE
    n_sides = 1 if n_narrow == 2 else 2
    sums, inverse, rate, flat, hots, ends = call(
        functools.partial(first_kernel, n_wide, n_narrow, cap, block, n_parts, levels), "first", 4.0,
        (
            kept(2, layers, tall, wide), kept(layers, tall, wide), kept(layers, tall, wide), kept(3, tall, wide),
            kept((3 + 3 * n_sides) * tall + rows, n_wide * block), kept(n_sides, tall, LANES),
        ),
        [here] * (2 * n_parts + 4), (here,) * 6,
        [pltpu.VMEM((2, layers, tall, wide), F32)],
    )(*near(*parts, *corners, ice, pair, cross, planes))
    ice, ocean, thick_out, melt_out = call(
        functools.partial(final_kernel, n_wide, n_narrow, cap, block), "final", 3.0,
        (
            array(3, layers, rows, LANES), array(3, rows, levels, LANES),
            array(rows, LANES), array(rows, LANES),
        ),
        [here] * 10 + [far], (far,) * 4,
        [
            pltpu.VMEM((PICARD - 1, 2, layers, tall, wide), F32),
            pltpu.VMEM((3, layers, rows, LANES), F32),
            pltpu.VMEM((rows, LANES), F32),
            pltpu.VMEM((rows, LANES), F32),
            pltpu.VMEM((rows, TILE, LANES), F32),
            dma((3 + layers,)),
        ],
        input_output_aliases={10: 1},
    )(*near(blocks, hots, ends, planes, ice, top, sums, inverse, rate, flat), ocean)
    return ice.transpose(0, 2, 1, 3), ocean, thick_out, melt_out


def solution(mesh):
    column = P("wide", None, "narrow")
    plane = P("wide", "narrow")
    return jax.shard_map(
        local,
        mesh=mesh,
        in_specs=(column,) * 6 + (plane,) * 5,
        out_specs=(P(None, "wide", None, "narrow"), P(None, "wide", None, "narrow"), plane, plane),
        check_vma=False,
    )
```

```python
import functools

import jax
import jax.numpy as jnp
from jax import lax
from jax.experimental import pallas as pl
from jax.experimental.pallas import tpu as pltpu
from jax.sharding import PartitionSpec as P

PICARD = 2
DIFFUSE = 0.2
GAMMA_MELT = 0.5
TIME_STEP = 0.05
SLOPE_SCALE = 0.1
STRAIN_FLOOR = 0.01
HEATING_RATE = 0.01

LANES = 128
TILE = 8
ORDER = (2, 3, 0, 1)
HALO = 4
RIM = 3
VMEM = pltpu.CompilerParams(vmem_limit_bytes=16 * 1024 * 1024)
F32 = jnp.float32

THICK, GROUNDED, OCEAN_T, WET, ICE_LINK, OCEAN_LINK = range(6)
PLANES = 6
CORNER = (THICK, GROUNDED, ICE_LINK)
PART, EDGE_T0, EDGE_T1, EDGE_W0, PART_WET, EDGE_W1 = range(6)


def iota(shape, axis):
    return lax.broadcasted_iota(jnp.int32, shape, axis)


def right_lanes(period):
    lane = iota((1, LANES), 1)
    return lane % period < HALO


def left_lanes(period):
    lane = iota((1, LANES), 1)
    return lane % period >= period - HALO


def spread(column, count=LANES):
    rows = column.shape[0]
    eye = iota((rows, count), 0) == iota((rows, count), 1)
    return jnp.sum(jnp.where(eye, column, 0.0), axis=0, keepdims=True)


def upright(row):
    count = row.shape[1]
    eye = iota((count, count), 0) == iota((count, count), 1)
    return jnp.sum(jnp.where(eye, row, 0.0), axis=1, keepdims=True)


def turn(value, shift, axis):
    shift %= value.shape[axis]
    return pltpu.roll(value, shift, axis) if shift else value


def fetch_all(pairs, sems):
    copies = [pltpu.make_async_copy(a, b, sems.at[i]) for i, (a, b) in enumerate(pairs)]
    for copy in copies:
        copy.start()
    return copies


def divide(whole, part):
    return jnp.floor((whole + 0.5) * (1.0 / part))


def pick(hot, value):
    hot = hot.astype(jnp.bfloat16)
    pieces = []
    for _ in range(3):
        pieces.append(value.astype(jnp.bfloat16))
        value = value - pieces[-1].astype(F32)
    a, b, c = (jnp.dot(hot, p, preferred_element_type=F32) for p in pieces)
    return (c + b) + a


def narrow_sides(n_narrow):
    place = lax.axis_index("narrow")
    return place < n_narrow - 1, place > 0


def merged(parts, right, left, n_narrow):
    has_right, has_left = narrow_sides(n_narrow)
    from_right, from_left = parts[0], parts[-1]
    if len(parts) == 1:
        keep = (right & has_right) | (left & has_left)
        return jnp.where(keep, from_right, 0.0)
    return jnp.where(right, from_right, jnp.where(left, from_left, 0.0))


def ice_group(index):
    return divmod(index, LANES // 8)


def ice_tiles(layers):
    return ice_group(3 * layers - 1)[0] + 1


def ice_pairs(layers):
    return -(-3 * layers // 2)


class Places:
    def __init__(self, levels, layers):
        self.ice = 3 * levels
        self.thick = self.ice + ice_pairs(layers) * TILE
        self.grounded = self.thick + TILE
        self.wet = self.grounded + TILE
        self.link = self.wet + TILE
        self.end = self.link + TILE


def odd_place():
    return lax.axis_index("wide") % 2 == 1


def pack_ice(tile_of, layers):
    lane = iota((1, LANES), 1)
    tiles = [None] * ice_tiles(layers)
    for index in range(3 * layers):
        tile, group = ice_group(index)
        turned = turn(tile_of(*divmod(index, layers)), 8 * group, 1)
        before = jnp.zeros_like(turned) if group == 0 else tiles[tile]
        tiles[tile] = jnp.where((lane + HALO) % LANES // 8 == group, turned, before)
    return tiles


def pack_planes(planes):
    lane = iota((1, LANES), 1)
    total = None
    for j, plane in planes.items():
        turned = turn(plane, 16 * j, 1)
        before = jnp.zeros_like(turned) if total is None else total
        total = jnp.where((lane + HALO) % LANES // 16 == j, turned, before)
    return total


def edges_kernel(
    ice_x, ice_y, ice_t, ocean_x, ocean_y, ocean_t, thick, grounded, wet, ice_links, ocean_links,
    out, pair, cross, planes, ice, field, thick_v, grounded_v, wet_v, links_v, sems, field_sems,
):
    layers, rows, _ = ice_x.shape
    levels = ocean_x.shape[1]
    chunks = field_sems.shape[0] // 3
    step = rows // chunks
    copies = fetch_all(
        (
            (ice_x, ice.at[0]),
            (ice_y, ice.at[1]),
            (ice_t, ice.at[2]),
            (thick, thick_v),
            (grounded, grounded_v),
            (wet, wet_v),
            (ice_links, links_v.at[0]),
            (ocean_links, links_v.at[1]),
        ),
        sems,
    )
    field_copies = fetch_all(
        [
            (source.at[pl.ds(h * step, step)], field.at[f, pl.ds(h * step, step)])
            for f, source in reversed(list(enumerate((ocean_x, ocean_y, ocean_t))))
            for h in range(chunks)
        ],
        field_sems,
    )
    places = Places(levels, layers)
    odd = odd_place()

    def send(at, size, lasts, firsts):
        pair[at : at + size, :] = jnp.where(odd, firsts, lasts)
        cross[at : at + size, :] = jnp.where(odd, lasts, firsts)

    lane = iota((1, LANES), 1)
    for copy in copies:
        copy.wait()
    for tile, value in enumerate(pack_ice(lambda f, k: ice[f, k], layers)):
        out[(1 + tile) * rows : (2 + tile) * rows, :] = value
    upper = iota((TILE, 1), 0) >= HALO
    half = ice_pairs(layers)
    for m in range(half):
        ends = []
        for index in (m, m + half):
            f, k = divmod(min(index, 3 * layers - 1), layers)
            ends.append((ice[f, k, rows - TILE :, :], ice[f, k, :TILE, :]))
        send(
            places.ice + m * TILE,
            TILE,
            jnp.where(upper, ends[0][0], turn(ends[1][0], HALO, 0)),
            jnp.where(upper, turn(ends[1][1], HALO, 0), ends[0][1]),
        )
    planes[THICK] = thick_v[...]
    planes[GROUNDED] = grounded_v[...].astype(F32)
    planes[WET] = wet_v[...].astype(F32)
    for k in range(2):
        link = upright(links_v[k].astype(F32)) + 1.0
        planes[ICE_LINK + k] = jnp.broadcast_to(link, (rows, LANES))
    for at, j in (
        (places.thick, THICK), (places.grounded, GROUNDED), (places.wet, WET), (places.link, ICE_LINK),
    ):
        send(at, TILE, planes[j, rows - TILE :, :], planes[j, :TILE, :])
    total = jnp.zeros((levels, LANES), F32)
    for n, f in enumerate((2, 1, 0)):
        for h in range(chunks):
            field_copies[n * chunks + h].wait()
            for i in range(h * step, (h + 1) * step):
                j = f * rows + i
                turned = turn(field[f, i], 2 * j, 1)
                total = jnp.where((lane + 1) % LANES // 2 == j, turned, total)
        send(f * levels, levels, field[f, rows - 1], field[f, 0])
        if f == 2:
            for i in range(rows):
                planes[OCEAN_T, i : i + 1, :] = field[2, i, 0:1, :]
            out[0:rows, :] = pack_planes({j: planes[j] for j in range(PLANES)})
    out[(1 + ice_tiles(layers)) * rows :, :] = total


def plane_halo(block, group):
    lane = iota((1, LANES), 1)
    turned = turn(block, -16 * group, 1)
    return jnp.where((lane < HALO) | (lane >= LANES - HALO), turned, 0.0)


def merged_planes(parts, rows, n_narrow):
    return merged([p[0:rows, :] for p in parts], right_lanes(16), left_lanes(16), n_narrow)


def merged_ice(parts, rows, n_tiles, n_narrow):
    return [
        merged(
            [p[(1 + t) * rows : (2 + t) * rows, :] for p in parts],
            right_lanes(8), left_lanes(8), n_narrow,
        )
        for t in range(n_tiles)
    ]


def ranks(own_col, member_col, order_sub, order_lane, own_row):
    hits = (own_col == own_row) & member_col & (order_sub < order_lane)
    return jnp.sum(hits.astype(F32), axis=0, keepdims=True)


def ocean_slots(link_col, rows, n_wide, cap, block):
    link_row = spread(link_col)
    parts = []
    for link in (link_col, link_row):
        number = link - 1.0
        tile = divide(number, rows)
        inner = number - tile * rows
        ok = link > 0.5
        parts.append(
            (
                tile,
                (
                    ok,
                    ok & (inner >= rows - RIM) & (tile < n_wide - 1.5),
                    ok & (inner < RIM) & (tile > 0.5),
                ),
            )
        )
    (tile_col, member_col), (tile_row, member_row) = parts
    order_sub, order_lane = iota((rows, LANES), 0), iota((rows, LANES), 1)
    place = iota((n_wide * block, LANES), 0).astype(F32)
    total = jnp.zeros((n_wide * block, LANES), F32)
    for k, shift in enumerate((0.0, 1.0, -1.0)):
        rank = ranks(tile_col, member_col[k], order_sub, order_lane, tile_row)
        target = jnp.where(
            member_row[k], (tile_row + shift) * block + (k * cap + rank), -1.0
        )
        total = total + (place == target).astype(F32)
    return total[:, :rows]


def draft_slots(link_col, rows, n_wide, cap, block):
    link_row = spread(link_col)
    tile_col, tile_row = divide(link_col - 1.0, rows), divide(link_row - 1.0, rows)
    order_sub, order_lane = iota((rows, LANES), 0), iota((rows, LANES), 1)
    rank = ranks(tile_col, link_col > 0.5, order_sub, order_lane, tile_row)
    target = jnp.where(link_row > 0.5, tile_row * block + (3 * cap + rank), -1.0)
    place = iota((n_wide * block, LANES), 0).astype(F32)
    return (place == target).astype(F32)[:, :rows]


def exchange_order(n_wide):
    quarter = n_wide // 4
    if n_wide % 4:
        return list(range(n_wide))
    return [q * quarter + j for q in ORDER for j in reversed(range(quarter))]


def blocks_kernel(n_wide, n_narrow, cap, block, n_parts, *refs):
    parts, refs = refs[:n_parts], refs[n_parts:]
    planes, blocks = refs
    rows = planes.shape[1]
    lane = iota((1, LANES), 1)
    plane_block = merged_planes(parts, rows, n_narrow)
    thick_plane, grounded_plane, wet_plane = planes[THICK], planes[GROUNDED], planes[WET]
    wet_all = jnp.concatenate([wet_plane, plane_halo(plane_block, WET)], axis=1)
    warm = wet_all * jnp.concatenate([planes[OCEAN_T], plane_halo(plane_block, OCEAN_T)], axis=1)
    width = 2 * LANES
    row = iota((rows, width), 0)
    sums = []
    for value in (wet_all, warm):
        total = pltpu.roll(value, 1, 1) + pltpu.roll(value, width - 1, 1)
        total = total + jnp.where(row > 0, pltpu.roll(value, 1, 0), 0.0)
        sums.append(total + jnp.where(row < rows - 1, pltpu.roll(value, rows - 1, 0), 0.0))
    mixed = warm + DIFFUSE * (wet_all * sums[1] - warm * sums[0])
    draft = 0.9 * thick_plane * (1.0 - grounded_plane)
    own_slots = ocean_slots(planes[OCEAN_LINK][:, 0:1], rows, n_wide, cap, block)
    main = pick(own_slots, jnp.concatenate([mixed[:, :LANES], wet_plane], axis=1))
    count = n_wide * block
    slot = iota((count, 1), 0) % block
    first = main[:, :LANES] + pick(draft_slots(planes[ICE_LINK][:, 0:1], rows, n_wide, cap, block), draft)
    second = jnp.where(
        slot == 3 * cap,
        wet_plane[0:1, :],
        jnp.where(slot == 3 * cap + 1, wet_plane[rows - 1 : rows, :], main[:, LANES:]),
    )
    edge = (lane < HALO) | (lane >= LANES - HALO)
    mixed_edge = jnp.where(edge, mixed[:, LANES:], 0.0)
    wet_edge = wet_all[:, LANES:]
    warm_edge = warm[:, LANES:]
    packed = mixed_edge + pltpu.roll(wet_edge, 16 * PART_WET, 1)
    links = plane_halo(plane_block, OCEAN_LINK)
    if n_narrow == 2:
        third = pick(
            ocean_slots(jnp.max(links, axis=1, keepdims=True), rows, n_wide, cap, block), packed
        )
    else:
        third = pick(
            ocean_slots(links[:, 0:1], rows, n_wide, cap, block),
            jnp.where(right_lanes(16), packed, 0.0),
        ) + pick(
            ocean_slots(links[:, LANES - 1 : LANES], rows, n_wide, cap, block),
            jnp.where(left_lanes(16), packed, 0.0),
        )
    last = rows - 1
    ends = (
        pltpu.roll(warm_edge[0:1, :], 16 * EDGE_T0, 1)
        + pltpu.roll(warm_edge[last:, :], 16 * EDGE_T1, 1)
        + pltpu.roll(wet_edge[0:1, :], 16 * EDGE_W0, 1)
        + pltpu.roll(wet_edge[last:, :], 16 * EDGE_W1, 1)
    )
    third = jnp.where(
        slot == 3 * cap,
        warm[0:1, :LANES],
        jnp.where(slot == 3 * cap + 1, warm[last:, :LANES], third + ends),
    )
    for k, value in enumerate((first, second, third)):
        for j, tile in enumerate(exchange_order(n_wide)):
            blocks[j, k * block : (k + 1) * block, :] = value[tile * block : (tile + 1) * block, :]


def beyond_ice(up, down, places, layers, f, k):
    under = iota((TILE, 1), 0) < HALO
    index, half = f * layers + k, ice_pairs(layers)
    at = places.ice + index % half * TILE
    if index < half:
        return jnp.where(under, down(at, TILE), up(at, TILE))
    return turn(jnp.where(under, up(at, TILE), down(at, TILE)), HALO, 0)


def came_from(pair, cross):
    odd = odd_place()

    def up(at, size):
        return jnp.where(odd, pair[pl.ds(at, size), :], cross[pl.ds(at, size), :])

    def down(at, size):
        return jnp.where(odd, cross[pl.ds(at, size), :], pair[pl.ds(at, size), :])

    return up, down


def corners_kernel(levels, layers, pair, cross, out):
    places = Places(levels, layers)
    up, down = came_from(pair, cross)
    under = iota((TILE, 1), 0) < HALO
    tiles = pack_ice(lambda f, k: beyond_ice(up, down, places, layers, f, k), layers)
    planes = {}
    for j, at in zip(CORNER, (places.thick, places.grounded, places.link)):
        planes[j] = jnp.where(under, down(at, TILE), up(at, TILE))
    for n, tile in enumerate((pack_planes(planes), *tiles)):
        out[n * TILE : (n + 1) * TILE, :] = tile


def ocean_kernel(n_narrow, n_parts, n_tiles, layers, *refs):
    parts, refs = refs[:n_parts], refs[n_parts:]
    field, pair, cross, planes, out, top, held, sems = refs
    _, rows, levels, _ = field.shape
    places = Places(levels, layers)
    chunks = sems.shape[0] // 3
    step = rows // chunks
    up, down = came_from(pair, cross)
    lane = iota((1, LANES), 1)
    row = iota((rows, LANES), 0)
    first, last = lane == 0, lane == LANES - 1
    wet = planes[WET]
    wet_halo = plane_halo(merged_planes(parts, rows, n_narrow), WET)
    scale = DIFFUSE * wet
    coef = (
        scale * jnp.where(row > 0, turn(wet, 1, 0), up(places.wet + TILE - 1, 1)),
        scale * jnp.where(row < rows - 1, turn(wet, -1, 0), down(places.wet, 1)),
        scale * jnp.where(first, 0.0, turn(wet, 1, 1)),
        scale * jnp.where(last, 0.0, turn(wet, -1, 1)),
    )
    edge = first | last
    weight = jnp.where(first, turn(wet_halo, 1, 1), turn(wet_halo, -1, 1))
    weight = scale * jnp.where(edge, weight, 0.0)
    centre_coef = 1.0 - (coef[0] + coef[1] + coef[2] + coef[3] + weight)
    even = lane % 2 == 0
    strip_at = (1 + n_tiles) * rows
    came = merged([p[strip_at:, :] for p in parts], even, ~even, n_narrow)
    came = jnp.where(even, turn(came, 1, 1), turn(came, -1, 1))
    packed = [turn(weight[i : i + 1, :], 2 * i, 1) for i in range(rows)]
    packed = functools.reduce(lambda a, b: a + b, packed)
    packed = packed + turn(packed, 2 * rows, 1) + turn(packed, 4 * rows, 1)
    side = packed * came
    writes = []
    for f in range(3):
        for h in range(chunks):
            for i in range(h * step, (h + 1) * step):
                centre = field[f, i]
                above = field[f, i - 1] if i > 0 else up(f * levels, levels)
                below = field[f, i + 1] if i < rows - 1 else down(f * levels, levels)
                value = centre * centre_coef[i : i + 1, :]
                value = value + above * coef[0][i : i + 1, :]
                value = value + below * coef[1][i : i + 1, :]
                value = value + turn(centre, 1, 1) * coef[2][i : i + 1, :]
                value = value + turn(centre, -1, 1) * coef[3][i : i + 1, :]
                value = value + jnp.where(edge, turn(side, -2 * (f * rows + i), 1), 0.0)
                held[f, i] = value
                if f == 2:
                    top[i] = value[0:TILE, :]
            part = pl.ds(h * step, step)
            level = pl.ds(TILE, levels - TILE) if f == 2 else pl.ds(0, levels)
            copy = pltpu.make_async_copy(
                held.at[f, part, level],
                out.at[f, part, level],
                sems.at[f * chunks + h],
            )
            copy.start()
            writes.append(copy)
    for copy in writes:
        copy.wait()


def ice_slots(link_col, kind_col, rows, cap, block, count, n_wide):
    link_row = spread(link_col)
    kind_row = spread(kind_col)
    number = link_col - 1.0
    tile = divide(number, rows)
    inner = number - tile * rows
    tile_row = divide(link_row - 1.0, rows)
    ok = (link_col > 0.5) & (kind_col > -0.5)
    ok_row = (link_row > 0.5) & (kind_row > -0.5)
    hits = (tile == tile_row) & (kind_col == kind_row) & ok_row & (link_row < link_col)
    rank = jnp.sum(hits.astype(F32), axis=1, keepdims=True)
    place = iota((link_col.shape[0], count), 1).astype(F32)

    def hot(keep, target):
        return (place == jnp.where(keep, target, -1.0)).astype(F32)

    top, bottom = inner < 0.5, inner > rows - 1.5
    edge = ok & (top | bottom)
    near = jnp.where(top, tile - 1.0, tile + 1.0)
    near_ok = edge & (near > -0.5) & (near < n_wide - 0.5)
    slot = hot(ok, tile * block + kind_col * cap + rank)
    near_edge = hot(near_ok, near * block + jnp.where(top, 3.0 * cap + 1.0, 3.0 * cap))
    own_edge = hot(edge, tile * block + jnp.where(top, 3.0 * cap, 3.0 * cap + 1.0))
    near_slot = hot(near_ok, near * block)
    own_slot = hot(edge, tile * block)
    return slot, near_edge, own_edge, near_slot, own_slot, bottom.astype(F32)


def around(value):
    return turn(value, 1, 0) + turn(value, -1, 0) + turn(value, 1, 1) + turn(value, -1, 1)


def sweep_layer(vel, k, layers, rate, friction):
    u, v = vel(0, k), vel(1, k)
    ends = [[turn(w, s, axis) for axis in (0, 1) for s in (-1, 1)] for w in (u, v)]
    ux, uy = ends[0][0] - ends[0][1], ends[0][2] - ends[0][3]
    vx, vy = ends[1][0] - ends[1][1], ends[1][2] - ends[1][3]
    cross = uy + vx
    eps2 = ux * (ux + vy) + vy * vy + 0.25 * (cross * cross)
    if k < layers - 1:
        uz, vz = vel(0, k + 1) - u, vel(1, k + 1) - v
        eps2 = eps2 + (uz * uz + vz * vz)
    eps2 = 0.25 * eps2
    eta = rate * jnp.exp((-1.0 / 3.0) * jnp.log(eps2 + STRAIN_FLOOR))
    links_up_down = float((k > 0) + (k < layers - 1))
    diagonal = eta * (2.0 + links_up_down) + 0.5 * around(eta) + friction
    sums = []
    for f, w in enumerate((u, v)):
        total = 0.5 * (ends[f][0] + ends[f][1] + ends[f][2] + ends[f][3])
        if k > 0:
            total = total + vel(f, k - 1)
        if k < layers - 1:
            total = total + vel(f, k + 1)
        sums.append(eta * total + 0.5 * around(eta * w))
    return sums, 1.0 / diagonal, eta * eps2


FLAT = ("thick", "grounded", "inside")


def first_kernel(n_wide, n_narrow, cap, block, n_parts, levels, *refs):
    parts, refs = refs[:n_parts], refs[n_parts:]
    corners, refs = refs[:n_parts], refs[n_parts:]
    ice, pair, cross, planes, sums, inverse, rate, flat, hots, ends, vel = refs
    _, layers, rows, _ = ice.shape
    places = Places(levels, layers)
    n_tiles = ice_tiles(layers)
    up, down = came_from(pair, cross)
    lane = iota((1, LANES), 1)
    width = 2 * LANES
    tall = rows + TILE
    wide_lane = iota((1, width), 1)
    place_wide = lax.axis_index("wide")
    has_right, has_left = narrow_sides(n_narrow)
    has_up, has_down = place_wide > 0, place_wide < n_wide - 1
    under = iota((TILE, 1), 0) < HALO

    def rim(at):
        return jnp.where(under, down(at, TILE), up(at, TILE))

    def below(a, b):
        return jnp.concatenate([a, b], axis=0)

    corner_planes = merged(
        [c[0:TILE, :] for c in corners], right_lanes(16), left_lanes(16), n_narrow
    )
    corner_ice = [
        merged(
            [c[(1 + t) * TILE : (2 + t) * TILE, :] for c in corners],
            right_lanes(8), left_lanes(8), n_narrow,
        )
        for t in range(n_tiles)
    ]
    block_tall = below(merged_planes(parts, rows, n_narrow), corner_planes)
    flat[0] = jnp.concatenate(
        [below(planes[THICK], rim(places.thick)), plane_halo(block_tall, THICK)], axis=1
    )
    grounded_tall = jnp.concatenate(
        [below(planes[GROUNDED], rim(places.grounded)), plane_halo(block_tall, GROUNDED)], axis=1
    )
    flat[1] = grounded_tall
    tall_row = iota((tall, 1), 0)
    inside = (
        ((tall_row < rows) | ((tall_row < rows + HALO) & has_down) | ((tall_row >= rows + HALO) & has_up))
        & (
            (wide_lane < LANES)
            | ((wide_lane < LANES + HALO) & has_right)
            | ((wide_lane >= width - HALO) & has_left)
        )
    ).astype(F32)
    flat[2] = inside
    kind = jnp.where(
        tall_row < rows,
        0.0,
        jnp.where(tall_row < rows + RIM, 2.0, jnp.where(tall_row >= tall - RIM, 1.0, -1.0)),
    )
    count = n_wide * block
    own_link = below(planes[ICE_LINK], rim(places.link))[:, 0:1]
    slots = (rows, cap, block, count, n_wide)
    found = list(ice_slots(own_link, kind, *slots)[:3])
    links = plane_halo(block_tall, ICE_LINK)
    if n_narrow == 2:
        sides = [jnp.max(links, axis=1, keepdims=True)]
    else:
        sides = [links[:, 0:1], links[:, LANES - 1 : LANES]]
    for link in sides:
        slot, _, _, near_slot, own_slot, bottom = ice_slots(link, kind, *slots)
        ends[(len(found) - 3) // 3] = jnp.broadcast_to(bottom, (tall, LANES))
        found += [slot, near_slot, own_slot]
    for n, hot in enumerate(found):
        hots[n * tall : (n + 1) * tall, :] = hot
    ocean_link = planes[OCEAN_LINK][:, 0:1]
    ocean_row = spread(ocean_link)
    tile = divide(ocean_link - 1.0, rows)
    tile_row = divide(ocean_row - 1.0, rows)
    hits = (tile == tile_row) & (ocean_row > 0.5) & (ocean_row < ocean_link)
    rank = jnp.sum(hits.astype(F32), axis=1, keepdims=True)
    target = jnp.where(ocean_link > 0.5, tile * block + 3 * cap + rank, -1.0)
    hots[len(found) * tall :, :] = (iota((rows, count), 1).astype(F32) == target).astype(F32)
    strips = [
        below(a, b) for a, b in zip(merged_ice(parts, rows, n_tiles, n_narrow), corner_ice)
    ]
    edge = (lane < HALO) | (lane >= LANES - HALO)
    for index in range(3 * layers):
        f, k = divmod(index, layers)
        beyond = beyond_ice(up, down, places, layers, f, k)
        t, group = ice_group(index)
        beside = jnp.where(edge, turn(strips[t], -8 * group, 1), 0.0)
        value = jnp.concatenate([below(ice[f, k], beyond), beside], axis=1)
        if f < 2:
            vel[f, k] = value
        else:
            rate[k] = jnp.exp(0.25 * value) * inside
    friction = 0.1 + 9.9 * grounded_tall
    for k in range(layers):
        both, over, _ = sweep_layer(lambda f, n: vel[f, n], k, layers, rate[k], friction)
        for f in range(2):
            sums[f, k] = both[f]
        inverse[k] = over * inside


def final_kernel(n_wide, n_narrow, cap, block, *refs):
    (
        blocks, hots, ends, planes, ice, top, sums, inverse, rate, flat, ocean_in,
        ice_out, ocean_out, thick_out, melt_out,
        vel, result, thin, melted, new_top, sems,
    ) = refs
    _, layers, rows, _ = ice.shape
    tall, width = flat.shape[1:]
    lane = iota((1, LANES), 1)
    order = exchange_order(n_wide)
    parts = [
        jnp.concatenate(
            [blocks[order.index(t), n * block : (n + 1) * block, :] for t in range(n_wide)], axis=0
        )
        for n in range(3)
    ]
    found = pick(hots[...], jnp.concatenate(parts, axis=1))

    def got(n, part):
        return found[n * tall : (n + 1) * tall, part * LANES : (part + 1) * LANES]

    wet_main = got(0, 1)
    mixed_main = got(0, 0) + DIFFUSE * (wet_main * got(1, 2) - got(1, 1) * got(2, 2))
    sides = []
    for n in range(3, 3 * (1 if n_narrow == 2 else 2) + 3, 3):
        value, near, own = got(n, 2), got(n + 1, 2), got(n + 2, 2)

        def group(row, j):
            return turn(row, -16 * j, 1)

        wet_got = group(value, PART_WET)
        bottom = ends[n // 3 - 1] > 0.5
        near_warm = jnp.where(bottom, group(near, EDGE_T0), group(near, EDGE_T1))
        near_wet = jnp.where(bottom, group(near, EDGE_W0), group(near, EDGE_W1))
        own_warm = jnp.where(bottom, group(own, EDGE_T1), group(own, EDGE_T0))
        sides.append((value + DIFFUSE * (wet_got * near_warm - near_wet * own_warm), wet_got))
    if len(sides) == 1:
        mixed_side, wet_side = sides[0]
    else:
        mixed_side, wet_side = (jnp.where(lane < HALO, a, b) for a, b in zip(*sides))
    mixed_tall = jnp.concatenate([mixed_main, mixed_side], axis=1)
    wet_tall = jnp.concatenate([wet_main, wet_side], axis=1)
    thick_tall, grounded_tall, inside = flat[0], flat[1], flat[2]
    open_ice = 1.0 - grounded_tall
    draft_tall = 0.9 * thick_tall * open_ice
    melt_tall = GAMMA_MELT * (mixed_tall - wet_tall * (0.0832 - 0.761 * draft_tall))
    new_thick = (thick_tall - TIME_STEP * melt_tall * open_ice) * inside
    thin[...] = new_thick[:rows, :LANES]
    n_hots = hots.shape[0] - rows
    ocean_draft = found[n_hots:, :LANES]
    heat_top = jnp.concatenate([top[i, 0:1, :] for i in range(rows)], axis=0)
    coupled = (planes[OCEAN_LINK] > 0.5).astype(F32)
    melt = GAMMA_MELT * (heat_top - (0.0832 - 0.761 * ocean_draft)) * planes[WET] * coupled
    melted[...] = melt
    cooled = heat_top - 0.2 * melt
    new_top[...] = top[...]
    for i in range(rows):
        new_top[i, 0:1, :] = cooled[i : i + 1, :]
    writes = fetch_all(
        (
            (new_top, ocean_out.at[2, :, pl.ds(0, TILE), :]),
            (thin, thick_out),
            (melted, melt_out),
        ),
        sems,
    )
    surface = new_thick * (0.1 + 0.9 * grounded_tall)
    scale = (-0.5 * SLOPE_SCALE) * new_thick
    stress = (
        scale * (turn(surface, -1, 0) - turn(surface, 1, 0)),
        scale * (turn(surface, -1, 1) - turn(surface, 1, 1)),
    )
    friction = 0.1 + 9.9 * grounded_tall
    for f in range(2):
        for k in range(layers):
            vel[0, f, k] = (sums[f, k] + stress[f]) * inverse[k]
    for sweep in range(1, PICARD):
        last = sweep == PICARD - 1
        old = sweep - 1
        for k in range(layers):
            both, over, heat = sweep_layer(
                lambda f, n: vel[old, f, n], k, layers, rate[k], friction
            )
            for f in range(2):
                value = (both[f] + stress[f]) * over
                if last:
                    result[f, k] = value[:rows, :LANES]
                else:
                    vel[sweep, f, k] = value * inside
            if last:
                result[2, k] = ice[2, k] + HEATING_RATE * heat[:rows, :LANES]
                copy = pltpu.make_async_copy(
                    result.at[:, k], ice_out.at[:, k], sems.at[len(writes)]
                )
                copy.start()
                writes.append(copy)
    for copy in writes:
        copy.wait()


def local(
    ice_x, ice_y, ice_temp, ocean_x, ocean_y, ocean_temp, thick, grounded_mask, wet_mask, ice_links, ocean_links,
):
    n_wide, n_narrow = lax.axis_size("wide"), lax.axis_size("narrow")
    rows, layers, columns = ice_x.shape
    levels = ocean_x.shape[1]
    cap = max(1, 2 * rows // n_wide)
    block = -(-max(4 * cap, 3 * cap + 2) // TILE) * TILE
    assert columns == LANES and ice_links.shape[0] == rows

    def stay(value):
        return pltpu.with_memory_space_constraint(value, pltpu.HBM)

    ice_fields = [stay(x.transpose(1, 0, 2)) for x in (ice_x, ice_y, ice_temp)]
    links = [stay(x.reshape(1, rows)) for x in (ice_links, ocean_links)]
    fields = [stay(x) for x in (ocean_x, ocean_y, ocean_temp)]
    planes_in = [stay(x) for x in (thick, grounded_mask, wet_mask)]
    here = pl.BlockSpec(memory_space=pltpu.VMEM)
    far = pl.BlockSpec(memory_space=pltpu.HBM)
    unread = pl.BlockSpec(memory_space=pl.ANY)
    dma = pltpu.SemaphoreType.DMA

    def array(*shape):
        return jax.ShapeDtypeStruct(shape, F32)

    def kept(*shape):
        return pltpu.VMEM(shape, F32)

    def near(*values):
        return [pltpu.with_memory_space_constraint(value, pltpu.VMEM) for value in values]

    def call(kernel, name, microseconds, out_shape, in_specs, out_specs, scratch=(), **more):
        estimate = pl.CostEstimate(
            flops=int(microseconds * 1.0e9), bytes_accessed=int(microseconds * 3.0e6), transcendentals=0
        )
        return pl.pallas_call(
            kernel, name=name, out_shape=out_shape, in_specs=in_specs, out_specs=out_specs,
            scratch_shapes=scratch, compiler_params=VMEM, cost_estimate=estimate, **more,
        )

    n_tiles = ice_tiles(layers)
    places = Places(levels, layers)
    chunks = 1
    message, to_pair, to_cross, planes, ice, field = call(
        edges_kernel, "edges", 4.0,
        (
            kept((1 + n_tiles) * rows + levels, LANES), kept(places.end, LANES), kept(places.end, LANES),
            kept(PLANES, rows, LANES), kept(3, layers, rows, LANES), kept(3, rows, levels, LANES),
        ),
        [far] * 11, (here,) * 6,
        [
            pltpu.VMEM((rows, LANES), F32),
            pltpu.VMEM((rows, LANES), jnp.int32),
            pltpu.VMEM((rows, LANES), jnp.int32),
            pltpu.VMEM((2, 1, rows), jnp.int32),
            dma((8,)),
            dma((3 * chunks,)),
        ],
    )(*ice_fields, *fields, *planes_in, *links)

    def narrow(value):
        if n_narrow == 2:
            return [lax.ppermute(value, "narrow", [(0, 1), (1, 0)])]
        ahead = [(i, i + 1) for i in range(n_narrow - 1)]
        return [
            lax.ppermute(value, "narrow", [(j, i) for i, j in ahead]),
            lax.ppermute(value, "narrow", ahead),
        ]

    parts = narrow(message)
    n_parts = len(parts)
    assert n_wide % 2 == 0
    swaps = [[(i, i + 1) for i in range(start, n_wide - 1, 2)] for start in (0, 1)]
    pair, cross = (
        lax.ppermute(value, "wide", swap + [(j, i) for i, j in swap])
        for value, swap in zip((to_pair, to_cross), swaps)
    )
    blocks = call(
        functools.partial(blocks_kernel, n_wide, n_narrow, cap, block, n_parts), "blocks", 4.0,
        kept(n_wide, 3 * block, LANES), [here] * (n_parts + 1), here,
    )(*near(*parts, planes))
    blocks = lax.all_to_all(
        blocks, "wide", split_axis=0, concat_axis=0, tiled=True, axis_index_groups=[exchange_order(n_wide)]
    )
    corners = narrow(
        call(
            functools.partial(corners_kernel, levels, layers), "corners", 1.0,
            kept((1 + n_tiles) * TILE, LANES), [here] * 2, here,
        )(*near(pair, cross))
    )
    ocean, top = call(
        functools.partial(ocean_kernel, n_narrow, n_parts, n_tiles, layers), "ocean", 4.0,
        (array(3, rows, levels, LANES), kept(rows, TILE, LANES)),
        [here] * (n_parts + 4), (far, here),
        [
            pltpu.VMEM((3, rows, levels, LANES), F32),
            dma((3 * chunks,)),
        ],
    )(*near(*parts, field, pair, cross, planes))
    wide = 2 * LANES
    tall = rows + TILE
    n_sides = 1 if n_narrow == 2 else 2
    sums, inverse, rate, flat, hots, ends = call(
        functools.partial(first_kernel, n_wide, n_narrow, cap, block, n_parts, levels), "first", 4.0,
        (
            kept(2, layers, tall, wide), kept(layers, tall, wide), kept(layers, tall, wide), kept(3, tall, wide),
            kept((3 + 3 * n_sides) * tall + rows, n_wide * block), kept(n_sides, tall, LANES),
        ),
        [here] * (2 * n_parts + 4), (here,) * 6,
        [pltpu.VMEM((2, layers, tall, wide), F32)],
    )(*near(*parts, *corners, ice, pair, cross, planes))
    ice, ocean, thick_out, melt_out = call(
        functools.partial(final_kernel, n_wide, n_narrow, cap, block), "final", 3.0,
        (
            array(3, layers, rows, LANES), array(3, rows, levels, LANES),
            array(rows, LANES), array(rows, LANES),
        ),
        [here] * 10 + [far], (far,) * 4,
        [
            pltpu.VMEM((PICARD - 1, 2, layers, tall, wide), F32),
            pltpu.VMEM((3, layers, rows, LANES), F32),
            pltpu.VMEM((rows, LANES), F32),
            pltpu.VMEM((rows, LANES), F32),
            pltpu.VMEM((rows, TILE, LANES), F32),
            dma((3 + layers,)),
        ],
        input_output_aliases={10: 1},
    )(*near(blocks, hots, ends, planes, ice, top, sums, inverse, rate, flat), ocean)
    return ice.transpose(0, 2, 1, 3), ocean, thick_out, melt_out


def solution(mesh):
    column = P("wide", None, "narrow")
    plane = P("wide", "narrow")
    return jax.shard_map(
        local,
        mesh=mesh,
        in_specs=(column,) * 6 + (plane,) * 5,
        out_specs=(P(None, "wide", None, "narrow"), P(None, "wide", None, "narrow"), plane, plane),
        check_vma=False,
    )
```

```python
import functools

import jax
import jax.numpy as jnp
from jax import lax
from jax.experimental import pallas as pl
from jax.experimental.pallas import tpu as pltpu
from jax.sharding import PartitionSpec as P

PICARD = 2
DIFFUSE = 0.2
GAMMA_MELT = 0.5
TIME_STEP = 0.05
SLOPE_SCALE = 0.1
STRAIN_FLOOR = 0.01
HEATING_RATE = 0.01

LANES = 128
TILE = 8
ORDER = (2, 3, 0, 1)
HALO = 4
RIM = 3
VMEM = pltpu.CompilerParams(vmem_limit_bytes=16 * 1024 * 1024)
F32 = jnp.float32

THICK, GROUNDED, OCEAN_T, WET, ICE_LINK, OCEAN_LINK = range(6)
PLANES = 6
CORNER = (THICK, GROUNDED, ICE_LINK)
PART, EDGE_T0, EDGE_T1, EDGE_W0, PART_WET, EDGE_W1 = range(6)


def iota(shape, axis):
    return lax.broadcasted_iota(jnp.int32, shape, axis)


def right_lanes(period):
    lane = iota((1, LANES), 1)
    return lane % period < HALO


def left_lanes(period):
    lane = iota((1, LANES), 1)
    return lane % period >= period - HALO


def spread(column, count=LANES):
    rows = column.shape[0]
    eye = iota((rows, count), 0) == iota((rows, count), 1)
    return jnp.sum(jnp.where(eye, column, 0.0), axis=0, keepdims=True)


def upright(row):
    count = row.shape[1]
    eye = iota((count, count), 0) == iota((count, count), 1)
    return jnp.sum(jnp.where(eye, row, 0.0), axis=1, keepdims=True)


def turn(value, shift, axis):
    shift %= value.shape[axis]
    return pltpu.roll(value, shift, axis) if shift else value


def fetch_all(pairs, sems):
    copies = [pltpu.make_async_copy(a, b, sems.at[i]) for i, (a, b) in enumerate(pairs)]
    for copy in copies:
        copy.start()
    return copies


def divide(whole, part):
    return jnp.floor((whole + 0.5) * (1.0 / part))


def pick(hot, value):
    hot = hot.astype(jnp.bfloat16)
    pieces = []
    for _ in range(3):
        pieces.append(value.astype(jnp.bfloat16))
        value = value - pieces[-1].astype(F32)
    a, b, c = (jnp.dot(hot, p, preferred_element_type=F32) for p in pieces)
    return (c + b) + a


def narrow_sides(n_narrow):
    place = lax.axis_index("narrow")
    return place < n_narrow - 1, place > 0


def merged(parts, right, left, n_narrow):
    has_right, has_left = narrow_sides(n_narrow)
    from_right, from_left = parts[0], parts[-1]
    if len(parts) == 1:
        keep = (right & has_right) | (left & has_left)
        return jnp.where(keep, from_right, 0.0)
    return jnp.where(right, from_right, jnp.where(left, from_left, 0.0))


def ice_group(index):
    return divmod(index, LANES // 8)


def ice_tiles(layers):
    return ice_group(3 * layers - 1)[0] + 1


def ice_pairs(layers):
    return -(-3 * layers // 2)


class Places:
    def __init__(self, levels, layers):
        self.ice = 3 * levels
        self.thick = self.ice + ice_pairs(layers) * TILE
        self.grounded = self.thick + TILE
        self.wet = self.grounded + TILE
        self.link = self.wet + TILE
        self.end = self.link + TILE


def odd_place():
    return lax.axis_index("wide") % 2 == 1


def pack_ice(tile_of, layers):
    lane = iota((1, LANES), 1)
    tiles = [None] * ice_tiles(layers)
    for index in range(3 * layers):
        tile, group = ice_group(index)
        turned = turn(tile_of(*divmod(index, layers)), 8 * group, 1)
        before = jnp.zeros_like(turned) if group == 0 else tiles[tile]
        tiles[tile] = jnp.where((lane + HALO) % LANES // 8 == group, turned, before)
    return tiles


def pack_planes(planes):
    lane = iota((1, LANES), 1)
    total = None
    for j, plane in planes.items():
        turned = turn(plane, 16 * j, 1)
        before = jnp.zeros_like(turned) if total is None else total
        total = jnp.where((lane + HALO) % LANES // 16 == j, turned, before)
    return total


def edges_kernel(
    ice_x, ice_y, ice_t, ocean_x, ocean_y, ocean_t, thick, grounded, wet, ice_links, ocean_links,
    out, pair, cross, planes, ice, field, thick_v, grounded_v, wet_v, links_v, sems, field_sems,
):
    layers, rows, _ = ice_x.shape
    levels = ocean_x.shape[1]
    chunks = field_sems.shape[0] // 3
    step = rows // chunks
    copies = fetch_all(
        (
            (ice_x, ice.at[0]),
            (ice_y, ice.at[1]),
            (ice_t, ice.at[2]),
            (thick, thick_v),
            (grounded, grounded_v),
            (wet, wet_v),
            (ice_links, links_v.at[0]),
            (ocean_links, links_v.at[1]),
        ),
        sems,
    )
    field_copies = fetch_all(
        [
            (source.at[pl.ds(h * step, step)], field.at[f, pl.ds(h * step, step)])
            for f, source in reversed(list(enumerate((ocean_x, ocean_y, ocean_t))))
            for h in range(chunks)
        ],
        field_sems,
    )
    places = Places(levels, layers)
    odd = odd_place()

    def send(at, size, lasts, firsts):
        pair[at : at + size, :] = jnp.where(odd, firsts, lasts)
        cross[at : at + size, :] = jnp.where(odd, lasts, firsts)

    lane = iota((1, LANES), 1)
    for copy in copies:
        copy.wait()
    for tile, value in enumerate(pack_ice(lambda f, k: ice[f, k], layers)):
        out[(1 + tile) * rows : (2 + tile) * rows, :] = value
    upper = iota((TILE, 1), 0) >= HALO
    half = ice_pairs(layers)
    for m in range(half):
        ends = []
        for index in (m, m + half):
            f, k = divmod(min(index, 3 * layers - 1), layers)
            ends.append((ice[f, k, rows - TILE :, :], ice[f, k, :TILE, :]))
        send(
            places.ice + m * TILE,
            TILE,
            jnp.where(upper, ends[0][0], turn(ends[1][0], HALO, 0)),
            jnp.where(upper, turn(ends[1][1], HALO, 0), ends[0][1]),
        )
    planes[THICK] = thick_v[...]
    planes[GROUNDED] = grounded_v[...].astype(F32)
    planes[WET] = wet_v[...].astype(F32)
    for k in range(2):
        link = upright(links_v[k].astype(F32)) + 1.0
        planes[ICE_LINK + k] = jnp.broadcast_to(link, (rows, LANES))
    for at, j in (
        (places.thick, THICK), (places.grounded, GROUNDED), (places.wet, WET), (places.link, ICE_LINK),
    ):
        send(at, TILE, planes[j, rows - TILE :, :], planes[j, :TILE, :])
    total = jnp.zeros((levels, LANES), F32)
    for n, f in enumerate((2, 1, 0)):
        for h in range(chunks):
            field_copies[n * chunks + h].wait()
            for i in range(h * step, (h + 1) * step):
                j = f * rows + i
                turned = turn(field[f, i], 2 * j, 1)
                total = jnp.where((lane + 1) % LANES // 2 == j, turned, total)
        send(f * levels, levels, field[f, rows - 1], field[f, 0])
        if f == 2:
            for i in range(rows):
                planes[OCEAN_T, i : i + 1, :] = field[2, i, 0:1, :]
            out[0:rows, :] = pack_planes({j: planes[j] for j in range(PLANES)})
    out[(1 + ice_tiles(layers)) * rows :, :] = total


def plane_halo(block, group):
    lane = iota((1, LANES), 1)
    turned = turn(block, -16 * group, 1)
    return jnp.where((lane < HALO) | (lane >= LANES - HALO), turned, 0.0)


def merged_planes(parts, rows, n_narrow):
    return merged([p[0:rows, :] for p in parts], right_lanes(16), left_lanes(16), n_narrow)


def merged_ice(parts, rows, n_tiles, n_narrow):
    return [
        merged(
            [p[(1 + t) * rows : (2 + t) * rows, :] for p in parts],
            right_lanes(8), left_lanes(8), n_narrow,
        )
        for t in range(n_tiles)
    ]


def ranks(own_col, member_col, order_sub, order_lane, own_row):
    hits = (own_col == own_row) & member_col & (order_sub < order_lane)
    return jnp.sum(hits.astype(F32), axis=0, keepdims=True)


def ocean_slots(link_col, rows, n_wide, cap, block):
    link_row = spread(link_col)
    parts = []
    for link in (link_col, link_row):
        number = link - 1.0
        tile = divide(number, rows)
        inner = number - tile * rows
        ok = link > 0.5
        parts.append(
            (
                tile,
                (
                    ok,
                    ok & (inner >= rows - RIM) & (tile < n_wide - 1.5),
                    ok & (inner < RIM) & (tile > 0.5),
                ),
            )
        )
    (tile_col, member_col), (tile_row, member_row) = parts
    order_sub, order_lane = iota((rows, LANES), 0), iota((rows, LANES), 1)
    place = iota((n_wide * block, LANES), 0).astype(F32)
    total = jnp.zeros((n_wide * block, LANES), F32)
    for k, shift in enumerate((0.0, 1.0, -1.0)):
        rank = ranks(tile_col, member_col[k], order_sub, order_lane, tile_row)
        target = jnp.where(
            member_row[k], (tile_row + shift) * block + (k * cap + rank), -1.0
        )
        total = total + (place == target).astype(F32)
    return total[:, :rows]


def draft_slots(link_col, rows, n_wide, cap, block):
    link_row = spread(link_col)
    tile_col, tile_row = divide(link_col - 1.0, rows), divide(link_row - 1.0, rows)
    order_sub, order_lane = iota((rows, LANES), 0), iota((rows, LANES), 1)
    rank = ranks(tile_col, link_col > 0.5, order_sub, order_lane, tile_row)
    target = jnp.where(link_row > 0.5, tile_row * block + (3 * cap + rank), -1.0)
    place = iota((n_wide * block, LANES), 0).astype(F32)
    return (place == target).astype(F32)[:, :rows]


def exchange_order(n_wide):
    quarter = n_wide // 4
    if n_wide % 4:
        return list(range(n_wide))
    return [q * quarter + j for q in ORDER for j in reversed(range(quarter))]


def blocks_kernel(n_wide, n_narrow, cap, block, n_parts, *refs):
    parts, refs = refs[:n_parts], refs[n_parts:]
    planes, blocks = refs
    rows = planes.shape[1]
    lane = iota((1, LANES), 1)
    plane_block = merged_planes(parts, rows, n_narrow)
    thick_plane, grounded_plane, wet_plane = planes[THICK], planes[GROUNDED], planes[WET]
    wet_all = jnp.concatenate([wet_plane, plane_halo(plane_block, WET)], axis=1)
    warm = wet_all * jnp.concatenate([planes[OCEAN_T], plane_halo(plane_block, OCEAN_T)], axis=1)
    width = 2 * LANES
    row = iota((rows, width), 0)
    sums = []
    for value in (wet_all, warm):
        total = pltpu.roll(value, 1, 1) + pltpu.roll(value, width - 1, 1)
        total = total + jnp.where(row > 0, pltpu.roll(value, 1, 0), 0.0)
        sums.append(total + jnp.where(row < rows - 1, pltpu.roll(value, rows - 1, 0), 0.0))
    mixed = warm + DIFFUSE * (wet_all * sums[1] - warm * sums[0])
    draft = 0.9 * thick_plane * (1.0 - grounded_plane)
    own_slots = ocean_slots(planes[OCEAN_LINK][:, 0:1], rows, n_wide, cap, block)
    main = pick(own_slots, jnp.concatenate([mixed[:, :LANES], wet_plane], axis=1))
    count = n_wide * block
    slot = iota((count, 1), 0) % block
    first = main[:, :LANES] + pick(draft_slots(planes[ICE_LINK][:, 0:1], rows, n_wide, cap, block), draft)
    second = jnp.where(
        slot == 3 * cap,
        wet_plane[0:1, :],
        jnp.where(slot == 3 * cap + 1, wet_plane[rows - 1 : rows, :], main[:, LANES:]),
    )
    edge = (lane < HALO) | (lane >= LANES - HALO)
    mixed_edge = jnp.where(edge, mixed[:, LANES:], 0.0)
    wet_edge = wet_all[:, LANES:]
    warm_edge = warm[:, LANES:]
    packed = mixed_edge + pltpu.roll(wet_edge, 16 * PART_WET, 1)
    links = plane_halo(plane_block, OCEAN_LINK)
    if n_narrow == 2:
        third = pick(
            ocean_slots(jnp.max(links, axis=1, keepdims=True), rows, n_wide, cap, block), packed
        )
    else:
        third = pick(
            ocean_slots(links[:, 0:1], rows, n_wide, cap, block),
            jnp.where(right_lanes(16), packed, 0.0),
        ) + pick(
            ocean_slots(links[:, LANES - 1 : LANES], rows, n_wide, cap, block),
            jnp.where(left_lanes(16), packed, 0.0),
        )
    last = rows - 1
    ends = (
        pltpu.roll(warm_edge[0:1, :], 16 * EDGE_T0, 1)
        + pltpu.roll(warm_edge[last:, :], 16 * EDGE_T1, 1)
        + pltpu.roll(wet_edge[0:1, :], 16 * EDGE_W0, 1)
        + pltpu.roll(wet_edge[last:, :], 16 * EDGE_W1, 1)
    )
    third = jnp.where(
        slot == 3 * cap,
        warm[0:1, :LANES],
        jnp.where(slot == 3 * cap + 1, warm[last:, :LANES], third + ends),
    )
    for k, value in enumerate((first, second, third)):
        for j, tile in enumerate(exchange_order(n_wide)):
            blocks[j, k * block : (k + 1) * block, :] = value[tile * block : (tile + 1) * block, :]


def beyond_ice(up, down, places, layers, f, k):
    under = iota((TILE, 1), 0) < HALO
    index, half = f * layers + k, ice_pairs(layers)
    at = places.ice + index % half * TILE
    if index < half:
        return jnp.where(under, down(at, TILE), up(at, TILE))
    return turn(jnp.where(under, up(at, TILE), down(at, TILE)), HALO, 0)


def came_from(pair, cross):
    odd = odd_place()

    def up(at, size):
        return jnp.where(odd, pair[pl.ds(at, size), :], cross[pl.ds(at, size), :])

    def down(at, size):
        return jnp.where(odd, cross[pl.ds(at, size), :], pair[pl.ds(at, size), :])

    return up, down


def corners_kernel(levels, layers, pair, cross, out):
    places = Places(levels, layers)
    up, down = came_from(pair, cross)
    under = iota((TILE, 1), 0) < HALO
    tiles = pack_ice(lambda f, k: beyond_ice(up, down, places, layers, f, k), layers)
    planes = {}
    for j, at in zip(CORNER, (places.thick, places.grounded, places.link)):
        planes[j] = jnp.where(under, down(at, TILE), up(at, TILE))
    for n, tile in enumerate((pack_planes(planes), *tiles)):
        out[n * TILE : (n + 1) * TILE, :] = tile


def own_hots(planes, rim_link, n_wide, cap, block, hots):
    rows = planes.shape[1]
    tall = rows + TILE
    tall_row = iota((tall, 1), 0)
    kind = jnp.where(
        tall_row < rows,
        0.0,
        jnp.where(tall_row < rows + RIM, 2.0, jnp.where(tall_row >= tall - RIM, 1.0, -1.0)),
    )
    count = n_wide * block
    own_link = jnp.concatenate([planes[ICE_LINK], rim_link], axis=0)[:, 0:1]
    slots = (rows, cap, block, count, n_wide)
    found = list(ice_slots(own_link, kind, *slots)[:3])
    for n, hot in enumerate(found):
        hots[n * tall : (n + 1) * tall, :] = hot
    ocean_link = planes[OCEAN_LINK][:, 0:1]
    ocean_row = spread(ocean_link)
    tile = divide(ocean_link - 1.0, rows)
    tile_row = divide(ocean_row - 1.0, rows)
    hits = (tile == tile_row) & (ocean_row > 0.5) & (ocean_row < ocean_link)
    rank = jnp.sum(hits.astype(F32), axis=1, keepdims=True)
    target = jnp.where(ocean_link > 0.5, tile * block + 3 * cap + rank, -1.0)
    hots[len(found) * tall :, :] = (iota((rows, count), 1).astype(F32) == target).astype(F32)


def ocean_kernel(n_wide, n_narrow, cap, block, n_parts, n_tiles, layers, *refs):
    parts, refs = refs[:n_parts], refs[n_parts:]
    field, pair, cross, planes, out, top, hots, held, sems = refs
    _, rows, levels, _ = field.shape
    places = Places(levels, layers)
    chunks = sems.shape[0] // 3
    step = rows // chunks
    up, down = came_from(pair, cross)
    lane = iota((1, LANES), 1)
    row = iota((rows, LANES), 0)
    first, last = lane == 0, lane == LANES - 1
    wet = planes[WET]
    wet_halo = plane_halo(merged_planes(parts, rows, n_narrow), WET)
    scale = DIFFUSE * wet
    coef = (
        scale * jnp.where(row > 0, turn(wet, 1, 0), up(places.wet + TILE - 1, 1)),
        scale * jnp.where(row < rows - 1, turn(wet, -1, 0), down(places.wet, 1)),
        scale * jnp.where(first, 0.0, turn(wet, 1, 1)),
        scale * jnp.where(last, 0.0, turn(wet, -1, 1)),
    )
    edge = first | last
    weight = jnp.where(first, turn(wet_halo, 1, 1), turn(wet_halo, -1, 1))
    weight = scale * jnp.where(edge, weight, 0.0)
    centre_coef = 1.0 - (coef[0] + coef[1] + coef[2] + coef[3] + weight)
    even = lane % 2 == 0
    strip_at = (1 + n_tiles) * rows
    came = merged([p[strip_at:, :] for p in parts], even, ~even, n_narrow)
    came = jnp.where(even, turn(came, 1, 1), turn(came, -1, 1))
    packed = [turn(weight[i : i + 1, :], 2 * i, 1) for i in range(rows)]
    packed = functools.reduce(lambda a, b: a + b, packed)
    packed = packed + turn(packed, 2 * rows, 1) + turn(packed, 4 * rows, 1)
    side = packed * came
    writes = []
    for f in range(3):
        for h in range(chunks):
            for i in range(h * step, (h + 1) * step):
                centre = field[f, i]
                above = field[f, i - 1] if i > 0 else up(f * levels, levels)
                below = field[f, i + 1] if i < rows - 1 else down(f * levels, levels)
                value = centre * centre_coef[i : i + 1, :]
                value = value + above * coef[0][i : i + 1, :]
                value = value + below * coef[1][i : i + 1, :]
                value = value + turn(centre, 1, 1) * coef[2][i : i + 1, :]
                value = value + turn(centre, -1, 1) * coef[3][i : i + 1, :]
                value = value + jnp.where(edge, turn(side, -2 * (f * rows + i), 1), 0.0)
                held[f, i] = value
                if f == 2:
                    top[i] = value[0:TILE, :]
            part = pl.ds(h * step, step)
            level = pl.ds(TILE, levels - TILE) if f == 2 else pl.ds(0, levels)
            copy = pltpu.make_async_copy(
                held.at[f, part, level],
                out.at[f, part, level],
                sems.at[f * chunks + h],
            )
            copy.start()
            writes.append(copy)
    under = iota((TILE, 1), 0) < HALO
    rim_link = jnp.where(under, down(places.link, TILE), up(places.link, TILE))
    own_hots(planes, rim_link, n_wide, cap, block, hots)
    for copy in writes:
        copy.wait()


def ice_slots(link_col, kind_col, rows, cap, block, count, n_wide):
    link_row = spread(link_col)
    kind_row = spread(kind_col)
    number = link_col - 1.0
    tile = divide(number, rows)
    inner = number - tile * rows
    tile_row = divide(link_row - 1.0, rows)
    ok = (link_col > 0.5) & (kind_col > -0.5)
    ok_row = (link_row > 0.5) & (kind_row > -0.5)
    hits = (tile == tile_row) & (kind_col == kind_row) & ok_row & (link_row < link_col)
    rank = jnp.sum(hits.astype(F32), axis=1, keepdims=True)
    place = iota((link_col.shape[0], count), 1).astype(F32)

    def hot(keep, target):
        return (place == jnp.where(keep, target, -1.0)).astype(F32)

    top, bottom = inner < 0.5, inner > rows - 1.5
    edge = ok & (top | bottom)
    near = jnp.where(top, tile - 1.0, tile + 1.0)
    near_ok = edge & (near > -0.5) & (near < n_wide - 0.5)
    slot = hot(ok, tile * block + kind_col * cap + rank)
    near_edge = hot(near_ok, near * block + jnp.where(top, 3.0 * cap + 1.0, 3.0 * cap))
    own_edge = hot(edge, tile * block + jnp.where(top, 3.0 * cap, 3.0 * cap + 1.0))
    near_slot = hot(near_ok, near * block)
    own_slot = hot(edge, tile * block)
    return slot, near_edge, own_edge, near_slot, own_slot, bottom.astype(F32)


def around(value):
    return turn(value, 1, 0) + turn(value, -1, 0) + turn(value, 1, 1) + turn(value, -1, 1)


def sweep_layer(vel, k, layers, rate, friction):
    u, v = vel(0, k), vel(1, k)
    ends = [[turn(w, s, axis) for axis in (0, 1) for s in (-1, 1)] for w in (u, v)]
    ux, uy = ends[0][0] - ends[0][1], ends[0][2] - ends[0][3]
    vx, vy = ends[1][0] - ends[1][1], ends[1][2] - ends[1][3]
    cross = uy + vx
    eps2 = ux * (ux + vy) + vy * vy + 0.25 * (cross * cross)
    if k < layers - 1:
        uz, vz = vel(0, k + 1) - u, vel(1, k + 1) - v
        eps2 = eps2 + (uz * uz + vz * vz)
    eps2 = 0.25 * eps2
    eta = rate * jnp.exp((-1.0 / 3.0) * jnp.log(eps2 + STRAIN_FLOOR))
    links_up_down = float((k > 0) + (k < layers - 1))
    diagonal = eta * (2.0 + links_up_down) + 0.5 * around(eta) + friction
    sums = []
    for f, w in enumerate((u, v)):
        total = 0.5 * (ends[f][0] + ends[f][1] + ends[f][2] + ends[f][3])
        if k > 0:
            total = total + vel(f, k - 1)
        if k < layers - 1:
            total = total + vel(f, k + 1)
        sums.append(eta * total + 0.5 * around(eta * w))
    return sums, 1.0 / diagonal, eta * eps2


FLAT = ("thick", "grounded", "inside")


def first_kernel(n_wide, n_narrow, cap, block, n_parts, levels, *refs):
    parts, refs = refs[:n_parts], refs[n_parts:]
    corners, refs = refs[:n_parts], refs[n_parts:]
    ice, pair, cross, planes, sums, inverse, rate, flat, hots, ends, vel = refs
    _, layers, rows, _ = ice.shape
    places = Places(levels, layers)
    n_tiles = ice_tiles(layers)
    up, down = came_from(pair, cross)
    lane = iota((1, LANES), 1)
    width = 2 * LANES
    tall = rows + TILE
    wide_lane = iota((1, width), 1)
    place_wide = lax.axis_index("wide")
    has_right, has_left = narrow_sides(n_narrow)
    has_up, has_down = place_wide > 0, place_wide < n_wide - 1
    under = iota((TILE, 1), 0) < HALO

    def rim(at):
        return jnp.where(under, down(at, TILE), up(at, TILE))

    def below(a, b):
        return jnp.concatenate([a, b], axis=0)

    corner_planes = merged(
        [c[0:TILE, :] for c in corners], right_lanes(16), left_lanes(16), n_narrow
    )
    corner_ice = [
        merged(
            [c[(1 + t) * TILE : (2 + t) * TILE, :] for c in corners],
            right_lanes(8), left_lanes(8), n_narrow,
        )
        for t in range(n_tiles)
    ]
    block_tall = below(merged_planes(parts, rows, n_narrow), corner_planes)
    flat[0] = jnp.concatenate(
        [below(planes[THICK], rim(places.thick)), plane_halo(block_tall, THICK)], axis=1
    )
    grounded_tall = jnp.concatenate(
        [below(planes[GROUNDED], rim(places.grounded)), plane_halo(block_tall, GROUNDED)], axis=1
    )
    flat[1] = grounded_tall
    tall_row = iota((tall, 1), 0)
    inside = (
        ((tall_row < rows) | ((tall_row < rows + HALO) & has_down) | ((tall_row >= rows + HALO) & has_up))
        & (
            (wide_lane < LANES)
            | ((wide_lane < LANES + HALO) & has_right)
            | ((wide_lane >= width - HALO) & has_left)
        )
    ).astype(F32)
    flat[2] = inside
    kind = jnp.where(
        tall_row < rows,
        0.0,
        jnp.where(tall_row < rows + RIM, 2.0, jnp.where(tall_row >= tall - RIM, 1.0, -1.0)),
    )
    count = n_wide * block
    found = []
    slots = (rows, cap, block, count, n_wide)
    links = plane_halo(block_tall, ICE_LINK)
    if n_narrow == 2:
        sides = [jnp.max(links, axis=1, keepdims=True)]
    else:
        sides = [links[:, 0:1], links[:, LANES - 1 : LANES]]
    for link in sides:
        slot, _, _, near_slot, own_slot, bottom = ice_slots(link, kind, *slots)
        ends[len(found) // 3] = jnp.broadcast_to(bottom, (tall, LANES))
        found += [slot, near_slot, own_slot]
    for n, hot in enumerate(found):
        hots[n * tall : (n + 1) * tall, :] = hot
    strips = [
        below(a, b) for a, b in zip(merged_ice(parts, rows, n_tiles, n_narrow), corner_ice)
    ]
    edge = (lane < HALO) | (lane >= LANES - HALO)
    for index in range(3 * layers):
        f, k = divmod(index, layers)
        beyond = beyond_ice(up, down, places, layers, f, k)
        t, group = ice_group(index)
        beside = jnp.where(edge, turn(strips[t], -8 * group, 1), 0.0)
        value = jnp.concatenate([below(ice[f, k], beyond), beside], axis=1)
        if f < 2:
            vel[f, k] = value
        else:
            rate[k] = jnp.exp(0.25 * value) * inside
    friction = 0.1 + 9.9 * grounded_tall
    for k in range(layers):
        both, over, _ = sweep_layer(lambda f, n: vel[f, n], k, layers, rate[k], friction)
        for f in range(2):
            sums[f, k] = both[f]
        inverse[k] = over * inside


def final_kernel(n_wide, n_narrow, cap, block, *refs):
    (
        blocks, own, hots, ends, planes, ice, top, sums, inverse, rate, flat, ocean_in,
        ice_out, ocean_out, thick_out, melt_out,
        vel, result, thin, melted, new_top, sems,
    ) = refs
    _, layers, rows, _ = ice.shape
    tall, width = flat.shape[1:]
    lane = iota((1, LANES), 1)
    order = exchange_order(n_wide)
    parts = [
        jnp.concatenate(
            [blocks[order.index(t), n * block : (n + 1) * block, :] for t in range(n_wide)], axis=0
        )
        for n in range(3)
    ]
    n_own = 3 * tall
    hot = jnp.concatenate([own[0:n_own, :], hots[...], own[n_own:, :]], axis=0)
    found = pick(hot, jnp.concatenate(parts, axis=1))

    def got(n, part):
        return found[n * tall : (n + 1) * tall, part * LANES : (part + 1) * LANES]

    wet_main = got(0, 1)
    mixed_main = got(0, 0) + DIFFUSE * (wet_main * got(1, 2) - got(1, 1) * got(2, 2))
    sides = []
    for n in range(3, 3 * (1 if n_narrow == 2 else 2) + 3, 3):
        value, near, own = got(n, 2), got(n + 1, 2), got(n + 2, 2)

        def group(row, j):
            return turn(row, -16 * j, 1)

        wet_got = group(value, PART_WET)
        bottom = ends[n // 3 - 1] > 0.5
        near_warm = jnp.where(bottom, group(near, EDGE_T0), group(near, EDGE_T1))
        near_wet = jnp.where(bottom, group(near, EDGE_W0), group(near, EDGE_W1))
        own_warm = jnp.where(bottom, group(own, EDGE_T1), group(own, EDGE_T0))
        sides.append((value + DIFFUSE * (wet_got * near_warm - near_wet * own_warm), wet_got))
    if len(sides) == 1:
        mixed_side, wet_side = sides[0]
    else:
        mixed_side, wet_side = (jnp.where(lane < HALO, a, b) for a, b in zip(*sides))
    mixed_tall = jnp.concatenate([mixed_main, mixed_side], axis=1)
    wet_tall = jnp.concatenate([wet_main, wet_side], axis=1)
    thick_tall, grounded_tall, inside = flat[0], flat[1], flat[2]
    open_ice = 1.0 - grounded_tall
    draft_tall = 0.9 * thick_tall * open_ice
    melt_tall = GAMMA_MELT * (mixed_tall - wet_tall * (0.0832 - 0.761 * draft_tall))
    new_thick = (thick_tall - TIME_STEP * melt_tall * open_ice) * inside
    thin[...] = new_thick[:rows, :LANES]
    n_hots = n_own + hots.shape[0]
    ocean_draft = found[n_hots:, :LANES]
    heat_top = jnp.concatenate([top[i, 0:1, :] for i in range(rows)], axis=0)
    coupled = (planes[OCEAN_LINK] > 0.5).astype(F32)
    melt = GAMMA_MELT * (heat_top - (0.0832 - 0.761 * ocean_draft)) * planes[WET] * coupled
    melted[...] = melt
    cooled = heat_top - 0.2 * melt
    new_top[...] = top[...]
    for i in range(rows):
        new_top[i, 0:1, :] = cooled[i : i + 1, :]
    writes = fetch_all(
        (
            (new_top, ocean_out.at[2, :, pl.ds(0, TILE), :]),
            (thin, thick_out),
            (melted, melt_out),
        ),
        sems,
    )
    surface = new_thick * (0.1 + 0.9 * grounded_tall)
    scale = (-0.5 * SLOPE_SCALE) * new_thick
    stress = (
        scale * (turn(surface, -1, 0) - turn(surface, 1, 0)),
        scale * (turn(surface, -1, 1) - turn(surface, 1, 1)),
    )
    friction = 0.1 + 9.9 * grounded_tall
    for f in range(2):
        for k in range(layers):
            vel[0, f, k] = (sums[f, k] + stress[f]) * inverse[k]
    for sweep in range(1, PICARD):
        last = sweep == PICARD - 1
        old = sweep - 1
        for k in range(layers):
            both, over, heat = sweep_layer(
                lambda f, n: vel[old, f, n], k, layers, rate[k], friction
            )
            for f in range(2):
                value = (both[f] + stress[f]) * over
                if last:
                    result[f, k] = value[:rows, :LANES]
                else:
                    vel[sweep, f, k] = value * inside
            if last:
                result[2, k] = ice[2, k] + HEATING_RATE * heat[:rows, :LANES]
                copy = pltpu.make_async_copy(
                    result.at[:, k], ice_out.at[:, k], sems.at[len(writes)]
                )
                copy.start()
                writes.append(copy)
    for copy in writes:
        copy.wait()


def local(
    ice_x, ice_y, ice_temp, ocean_x, ocean_y, ocean_temp, thick, grounded_mask, wet_mask, ice_links, ocean_links,
):
    n_wide, n_narrow = lax.axis_size("wide"), lax.axis_size("narrow")
    rows, layers, columns = ice_x.shape
    levels = ocean_x.shape[1]
    cap = max(1, 2 * rows // n_wide)
    block = -(-max(4 * cap, 3 * cap + 2) // TILE) * TILE
    assert columns == LANES and ice_links.shape[0] == rows

    def stay(value):
        return pltpu.with_memory_space_constraint(value, pltpu.HBM)

    ice_fields = [stay(x.transpose(1, 0, 2)) for x in (ice_x, ice_y, ice_temp)]
    links = [stay(x.reshape(1, rows)) for x in (ice_links, ocean_links)]
    fields = [stay(x) for x in (ocean_x, ocean_y, ocean_temp)]
    planes_in = [stay(x) for x in (thick, grounded_mask, wet_mask)]
    here = pl.BlockSpec(memory_space=pltpu.VMEM)
    far = pl.BlockSpec(memory_space=pltpu.HBM)
    unread = pl.BlockSpec(memory_space=pl.ANY)
    dma = pltpu.SemaphoreType.DMA

    def array(*shape):
        return jax.ShapeDtypeStruct(shape, F32)

    def kept(*shape):
        return pltpu.VMEM(shape, F32)

    def near(*values):
        return [pltpu.with_memory_space_constraint(value, pltpu.VMEM) for value in values]

    def call(kernel, name, microseconds, out_shape, in_specs, out_specs, scratch=(), **more):
        estimate = pl.CostEstimate(
            flops=int(microseconds * 1.0e9), bytes_accessed=int(microseconds * 3.0e6), transcendentals=0
        )
        return pl.pallas_call(
            kernel, name=name, out_shape=out_shape, in_specs=in_specs, out_specs=out_specs,
            scratch_shapes=scratch, compiler_params=VMEM, cost_estimate=estimate, **more,
        )

    n_tiles = ice_tiles(layers)
    places = Places(levels, layers)
    chunks = 1
    message, to_pair, to_cross, planes, ice, field = call(
        edges_kernel, "edges", 4.0,
        (
            kept((1 + n_tiles) * rows + levels, LANES), kept(places.end, LANES), kept(places.end, LANES),
            kept(PLANES, rows, LANES), kept(3, layers, rows, LANES), kept(3, rows, levels, LANES),
        ),
        [far] * 11, (here,) * 6,
        [
            pltpu.VMEM((rows, LANES), F32),
            pltpu.VMEM((rows, LANES), jnp.int32),
            pltpu.VMEM((rows, LANES), jnp.int32),
            pltpu.VMEM((2, 1, rows), jnp.int32),
            dma((8,)),
            dma((3 * chunks,)),
        ],
    )(*ice_fields, *fields, *planes_in, *links)

    def narrow(value):
        if n_narrow == 2:
            return [lax.ppermute(value, "narrow", [(0, 1), (1, 0)])]
        ahead = [(i, i + 1) for i in range(n_narrow - 1)]
        return [
            lax.ppermute(value, "narrow", [(j, i) for i, j in ahead]),
            lax.ppermute(value, "narrow", ahead),
        ]

    parts = narrow(message)
    n_parts = len(parts)
    assert n_wide % 2 == 0
    swaps = [[(i, i + 1) for i in range(start, n_wide - 1, 2)] for start in (0, 1)]
    pair, cross = (
        lax.ppermute(value, "wide", swap + [(j, i) for i, j in swap])
        for value, swap in zip((to_pair, to_cross), swaps)
    )
    blocks = call(
        functools.partial(blocks_kernel, n_wide, n_narrow, cap, block, n_parts), "blocks", 4.0,
        kept(n_wide, 3 * block, LANES), [here] * (n_parts + 1), here,
    )(*near(*parts, planes))
    blocks = lax.all_to_all(
        blocks, "wide", split_axis=0, concat_axis=0, tiled=True, axis_index_groups=[exchange_order(n_wide)]
    )
    corners = narrow(
        call(
            functools.partial(corners_kernel, levels, layers), "corners", 1.0,
            kept((1 + n_tiles) * TILE, LANES), [here] * 2, here,
        )(*near(pair, cross))
    )
    tall = rows + TILE
    ocean, top, own = call(
        functools.partial(ocean_kernel, n_wide, n_narrow, cap, block, n_parts, n_tiles, layers), "ocean", 4.0,
        (array(3, rows, levels, LANES), kept(rows, TILE, LANES), kept(3 * tall + rows, n_wide * block)),
        [here] * (n_parts + 4), (far, here, here),
        [
            pltpu.VMEM((3, rows, levels, LANES), F32),
            dma((3 * chunks,)),
        ],
    )(*near(*parts, field, pair, cross, planes))
    wide = 2 * LANES
    tall = rows + TILE
    n_sides = 1 if n_narrow == 2 else 2
    sums, inverse, rate, flat, hots, ends = call(
        functools.partial(first_kernel, n_wide, n_narrow, cap, block, n_parts, levels), "first", 4.0,
        (
            kept(2, layers, tall, wide), kept(layers, tall, wide), kept(layers, tall, wide), kept(3, tall, wide),
            kept(3 * n_sides * tall, n_wide * block), kept(n_sides, tall, LANES),
        ),
        [here] * (2 * n_parts + 4), (here,) * 6,
        [pltpu.VMEM((2, layers, tall, wide), F32)],
    )(*near(*parts, *corners, ice, pair, cross, planes))
    ice, ocean, thick_out, melt_out = call(
        functools.partial(final_kernel, n_wide, n_narrow, cap, block), "final", 3.0,
        (
            array(3, layers, rows, LANES), array(3, rows, levels, LANES),
            array(rows, LANES), array(rows, LANES),
        ),
        [here] * 11 + [far], (far,) * 4,
        [
            pltpu.VMEM((PICARD - 1, 2, layers, tall, wide), F32),
            pltpu.VMEM((3, layers, rows, LANES), F32),
            pltpu.VMEM((rows, LANES), F32),
            pltpu.VMEM((rows, LANES), F32),
            pltpu.VMEM((rows, TILE, LANES), F32),
            dma((3 + layers,)),
        ],
        input_output_aliases={11: 1},
    )(*near(blocks, own, hots, ends, planes, ice, top, sums, inverse, rate, flat), ocean)
    return ice.transpose(0, 2, 1, 3), ocean, thick_out, melt_out


def solution(mesh):
    column = P("wide", None, "narrow")
    plane = P("wide", "narrow")
    return jax.shard_map(
        local,
        mesh=mesh,
        in_specs=(column,) * 6 + (plane,) * 5,
        out_specs=(P(None, "wide", None, "narrow"), P(None, "wide", None, "narrow"), plane, plane),
        check_vma=False,
    )
```

```python
import functools

import jax
import jax.numpy as jnp
from jax import lax
from jax.experimental import pallas as pl
from jax.experimental.pallas import tpu as pltpu
from jax.sharding import PartitionSpec as P

PICARD = 2
DIFFUSE = 0.2
GAMMA_MELT = 0.5
TIME_STEP = 0.05
SLOPE_SCALE = 0.1
STRAIN_FLOOR = 0.01
HEATING_RATE = 0.01

LANES = 128
TILE = 8
ORDER = (2, 3, 0, 1)
HALO = 4
RIM = 3
VMEM = pltpu.CompilerParams(vmem_limit_bytes=16 * 1024 * 1024)
F32 = jnp.float32

THICK, GROUNDED, OCEAN_T, WET, ICE_LINK, OCEAN_LINK = range(6)
PLANES = 6
CORNER = (THICK, GROUNDED, ICE_LINK)
PART, EDGE_T0, EDGE_T1, EDGE_W0, PART_WET, EDGE_W1 = range(6)


def iota(shape, axis):
    return lax.broadcasted_iota(jnp.int32, shape, axis)


def right_lanes(period):
    lane = iota((1, LANES), 1)
    return lane % period < HALO


def left_lanes(period):
    lane = iota((1, LANES), 1)
    return lane % period >= period - HALO


def spread(column, count=LANES):
    rows = column.shape[0]
    eye = iota((rows, count), 0) == iota((rows, count), 1)
    return jnp.sum(jnp.where(eye, column, 0.0), axis=0, keepdims=True)


def upright(row):
    count = row.shape[1]
    eye = iota((count, count), 0) == iota((count, count), 1)
    return jnp.sum(jnp.where(eye, row, 0.0), axis=1, keepdims=True)


def turn(value, shift, axis):
    shift %= value.shape[axis]
    return pltpu.roll(value, shift, axis) if shift else value


def fetch_all(pairs, sems):
    copies = [pltpu.make_async_copy(a, b, sems.at[i]) for i, (a, b) in enumerate(pairs)]
    for copy in copies:
        copy.start()
    return copies


def divide(whole, part):
    return jnp.floor((whole + 0.5) * (1.0 / part))


def pick(hot, value):
    hot = hot.astype(jnp.bfloat16)
    pieces = []
    for _ in range(3):
        pieces.append(value.astype(jnp.bfloat16))
        value = value - pieces[-1].astype(F32)
    a, b, c = (jnp.dot(hot, p, preferred_element_type=F32) for p in pieces)
    return (c + b) + a


def narrow_sides(n_narrow):
    place = lax.axis_index("narrow")
    return place < n_narrow - 1, place > 0


def merged(parts, right, left, n_narrow):
    has_right, has_left = narrow_sides(n_narrow)
    from_right, from_left = parts[0], parts[-1]
    if len(parts) == 1:
        keep = (right & has_right) | (left & has_left)
        return jnp.where(keep, from_right, 0.0)
    return jnp.where(right, from_right, jnp.where(left, from_left, 0.0))


def ice_group(index):
    return divmod(index, LANES // 8)


def ice_tiles(layers):
    return ice_group(3 * layers - 1)[0] + 1


def ice_pairs(layers):
    return -(-3 * layers // 2)


class Places:
    def __init__(self, levels, layers):
        self.ice = 3 * levels
        self.thick = self.ice + ice_pairs(layers) * TILE
        self.grounded = self.thick + TILE
        self.wet = self.grounded + TILE
        self.link = self.wet + TILE
        self.end = self.link + TILE


def odd_place():
    return lax.axis_index("wide") % 2 == 1


def pack_ice(tile_of, layers):
    lane = iota((1, LANES), 1)
    tiles = [None] * ice_tiles(layers)
    for index in range(3 * layers):
        tile, group = ice_group(index)
        turned = turn(tile_of(*divmod(index, layers)), 8 * group, 1)
        before = jnp.zeros_like(turned) if group == 0 else tiles[tile]
        tiles[tile] = jnp.where((lane + HALO) % LANES // 8 == group, turned, before)
    return tiles


def pack_planes(planes):
    lane = iota((1, LANES), 1)
    total = None
    for j, plane in planes.items():
        turned = turn(plane, 16 * j, 1)
        before = jnp.zeros_like(turned) if total is None else total
        total = jnp.where((lane + HALO) % LANES // 16 == j, turned, before)
    return total


def edges_kernel(
    ice_x, ice_y, ice_t, ocean_x, ocean_y, ocean_t, thick, grounded, wet, ice_links, ocean_links,
    out, pair, cross, planes, ice, field, thick_v, grounded_v, wet_v, links_v, sems, field_sems,
):
    layers, rows, _ = ice_x.shape
    levels = ocean_x.shape[1]
    chunks = field_sems.shape[0] // 3
    step = rows // chunks
    copies = fetch_all(
        (
            (ice_x, ice.at[0]),
            (ice_y, ice.at[1]),
            (ice_t, ice.at[2]),
            (thick, thick_v),
            (grounded, grounded_v),
            (wet, wet_v),
            (ice_links, links_v.at[0]),
            (ocean_links, links_v.at[1]),
        ),
        sems,
    )
    field_copies = fetch_all(
        [
            (source.at[pl.ds(h * step, step)], field.at[f, pl.ds(h * step, step)])
            for f, source in reversed(list(enumerate((ocean_x, ocean_y, ocean_t))))
            for h in range(chunks)
        ],
        field_sems,
    )
    places = Places(levels, layers)
    odd = odd_place()

    def send(at, size, lasts, firsts):
        pair[at : at + size, :] = jnp.where(odd, firsts, lasts)
        cross[at : at + size, :] = jnp.where(odd, lasts, firsts)

    lane = iota((1, LANES), 1)
    for copy in copies:
        copy.wait()
    for tile, value in enumerate(pack_ice(lambda f, k: ice[f, k], layers)):
        out[(1 + tile) * rows : (2 + tile) * rows, :] = value
    upper = iota((TILE, 1), 0) >= HALO
    half = ice_pairs(layers)
    for m in range(half):
        ends = []
        for index in (m, m + half):
            f, k = divmod(min(index, 3 * layers - 1), layers)
            ends.append((ice[f, k, rows - TILE :, :], ice[f, k, :TILE, :]))
        send(
            places.ice + m * TILE,
            TILE,
            jnp.where(upper, ends[0][0], turn(ends[1][0], HALO, 0)),
            jnp.where(upper, turn(ends[1][1], HALO, 0), ends[0][1]),
        )
    planes[THICK] = thick_v[...]
    planes[GROUNDED] = grounded_v[...].astype(F32)
    planes[WET] = wet_v[...].astype(F32)
    for k in range(2):
        link = upright(links_v[k].astype(F32)) + 1.0
        planes[ICE_LINK + k] = jnp.broadcast_to(link, (rows, LANES))
    for at, j in (
        (places.thick, THICK), (places.grounded, GROUNDED), (places.wet, WET), (places.link, ICE_LINK),
    ):
        send(at, TILE, planes[j, rows - TILE :, :], planes[j, :TILE, :])
    total = jnp.zeros((levels, LANES), F32)
    for n, f in enumerate((2, 1, 0)):
        for h in range(chunks):
            field_copies[n * chunks + h].wait()
            for i in range(h * step, (h + 1) * step):
                j = f * rows + i
                turned = turn(field[f, i], 2 * j, 1)
                total = jnp.where((lane + 1) % LANES // 2 == j, turned, total)
        send(f * levels, levels, field[f, rows - 1], field[f, 0])
        if f == 2:
            for i in range(rows):
                planes[OCEAN_T, i : i + 1, :] = field[2, i, 0:1, :]
            out[0:rows, :] = pack_planes({j: planes[j] for j in range(PLANES)})
    out[(1 + ice_tiles(layers)) * rows :, :] = total


def plane_halo(block, group):
    lane = iota((1, LANES), 1)
    turned = turn(block, -16 * group, 1)
    return jnp.where((lane < HALO) | (lane >= LANES - HALO), turned, 0.0)


def merged_planes(parts, rows, n_narrow):
    return merged([p[0:rows, :] for p in parts], right_lanes(16), left_lanes(16), n_narrow)


def merged_ice(parts, rows, n_tiles, n_narrow):
    return [
        merged(
            [p[(1 + t) * rows : (2 + t) * rows, :] for p in parts],
            right_lanes(8), left_lanes(8), n_narrow,
        )
        for t in range(n_tiles)
    ]


def ranks(own_col, member_col, order_sub, order_lane, own_row):
    hits = (own_col == own_row) & member_col & (order_sub < order_lane)
    return jnp.sum(hits.astype(F32), axis=0, keepdims=True)


def ocean_slots(link_col, rows, n_wide, cap, block):
    link_row = spread(link_col)
    parts = []
    for link in (link_col, link_row):
        number = link - 1.0
        tile = divide(number, rows)
        inner = number - tile * rows
        ok = link > 0.5
        parts.append(
            (
                tile,
                (
                    ok,
                    ok & (inner >= rows - RIM) & (tile < n_wide - 1.5),
                    ok & (inner < RIM) & (tile > 0.5),
                ),
            )
        )
    (tile_col, member_col), (tile_row, member_row) = parts
    order_sub, order_lane = iota((rows, LANES), 0), iota((rows, LANES), 1)
    place = iota((n_wide * block, LANES), 0).astype(F32)
    total = jnp.zeros((n_wide * block, LANES), F32)
    for k, shift in enumerate((0.0, 1.0, -1.0)):
        rank = ranks(tile_col, member_col[k], order_sub, order_lane, tile_row)
        target = jnp.where(
            member_row[k], (tile_row + shift) * block + (k * cap + rank), -1.0
        )
        total = total + (place == target).astype(F32)
    return total[:, :rows]


def draft_slots(link_col, rows, n_wide, cap, block):
    link_row = spread(link_col)
    tile_col, tile_row = divide(link_col - 1.0, rows), divide(link_row - 1.0, rows)
    order_sub, order_lane = iota((rows, LANES), 0), iota((rows, LANES), 1)
    rank = ranks(tile_col, link_col > 0.5, order_sub, order_lane, tile_row)
    target = jnp.where(link_row > 0.5, tile_row * block + (3 * cap + rank), -1.0)
    place = iota((n_wide * block, LANES), 0).astype(F32)
    return (place == target).astype(F32)[:, :rows]


def exchange_order(n_wide):
    quarter = n_wide // 4
    if n_wide % 4:
        return list(range(n_wide))
    return [q * quarter + j for q in ORDER for j in reversed(range(quarter))]


def blocks_kernel(n_wide, n_narrow, cap, block, n_parts, *refs):
    parts, refs = refs[:n_parts], refs[n_parts:]
    planes, blocks = refs
    rows = planes.shape[1]
    lane = iota((1, LANES), 1)
    plane_block = merged_planes(parts, rows, n_narrow)
    thick_plane, grounded_plane, wet_plane = planes[THICK], planes[GROUNDED], planes[WET]
    wet_all = jnp.concatenate([wet_plane, plane_halo(plane_block, WET)], axis=1)
    warm = wet_all * jnp.concatenate([planes[OCEAN_T], plane_halo(plane_block, OCEAN_T)], axis=1)
    width = 2 * LANES
    row = iota((rows, width), 0)
    sums = []
    for value in (wet_all, warm):
        total = pltpu.roll(value, 1, 1) + pltpu.roll(value, width - 1, 1)
        total = total + jnp.where(row > 0, pltpu.roll(value, 1, 0), 0.0)
        sums.append(total + jnp.where(row < rows - 1, pltpu.roll(value, rows - 1, 0), 0.0))
    mixed = warm + DIFFUSE * (wet_all * sums[1] - warm * sums[0])
    draft = 0.9 * thick_plane * (1.0 - grounded_plane)
    own_slots = ocean_slots(planes[OCEAN_LINK][:, 0:1], rows, n_wide, cap, block)
    main = pick(own_slots, jnp.concatenate([mixed[:, :LANES], wet_plane], axis=1))
    count = n_wide * block
    slot = iota((count, 1), 0) % block
    first = main[:, :LANES] + pick(draft_slots(planes[ICE_LINK][:, 0:1], rows, n_wide, cap, block), draft)
    second = jnp.where(
        slot == 3 * cap,
        wet_plane[0:1, :],
        jnp.where(slot == 3 * cap + 1, wet_plane[rows - 1 : rows, :], main[:, LANES:]),
    )
    edge = (lane < HALO) | (lane >= LANES - HALO)
    mixed_edge = jnp.where(edge, mixed[:, LANES:], 0.0)
    wet_edge = wet_all[:, LANES:]
    warm_edge = warm[:, LANES:]
    packed = mixed_edge + pltpu.roll(wet_edge, 16 * PART_WET, 1)
    links = plane_halo(plane_block, OCEAN_LINK)
    if n_narrow == 2:
        third = pick(
            ocean_slots(jnp.max(links, axis=1, keepdims=True), rows, n_wide, cap, block), packed
        )
    else:
        third = pick(
            ocean_slots(links[:, 0:1], rows, n_wide, cap, block),
            jnp.where(right_lanes(16), packed, 0.0),
        ) + pick(
            ocean_slots(links[:, LANES - 1 : LANES], rows, n_wide, cap, block),
            jnp.where(left_lanes(16), packed, 0.0),
        )
    last = rows - 1
    ends = (
        pltpu.roll(warm_edge[0:1, :], 16 * EDGE_T0, 1)
        + pltpu.roll(warm_edge[last:, :], 16 * EDGE_T1, 1)
        + pltpu.roll(wet_edge[0:1, :], 16 * EDGE_W0, 1)
        + pltpu.roll(wet_edge[last:, :], 16 * EDGE_W1, 1)
    )
    third = jnp.where(
        slot == 3 * cap,
        warm[0:1, :LANES],
        jnp.where(slot == 3 * cap + 1, warm[last:, :LANES], third + ends),
    )
    for k, value in enumerate((first, second, third)):
        for j, tile in enumerate(exchange_order(n_wide)):
            blocks[j, k * block : (k + 1) * block, :] = value[tile * block : (tile + 1) * block, :]


def beyond_ice(up, down, places, layers, f, k):
    under = iota((TILE, 1), 0) < HALO
    index, half = f * layers + k, ice_pairs(layers)
    at = places.ice + index % half * TILE
    if index < half:
        return jnp.where(under, down(at, TILE), up(at, TILE))
    return turn(jnp.where(under, up(at, TILE), down(at, TILE)), HALO, 0)


def came_from(pair, cross):
    odd = odd_place()

    def up(at, size):
        return jnp.where(odd, pair[pl.ds(at, size), :], cross[pl.ds(at, size), :])

    def down(at, size):
        return jnp.where(odd, cross[pl.ds(at, size), :], pair[pl.ds(at, size), :])

    return up, down


def corners_kernel(levels, layers, pair, cross, out):
    places = Places(levels, layers)
    up, down = came_from(pair, cross)
    under = iota((TILE, 1), 0) < HALO
    tiles = pack_ice(lambda f, k: beyond_ice(up, down, places, layers, f, k), layers)
    planes = {}
    for j, at in zip(CORNER, (places.thick, places.grounded, places.link)):
        planes[j] = jnp.where(under, down(at, TILE), up(at, TILE))
    for n, tile in enumerate((pack_planes(planes), *tiles)):
        out[n * TILE : (n + 1) * TILE, :] = tile


def own_hots(planes, rim_link, n_wide, cap, block, hots):
    rows = planes.shape[1]
    tall = rows + TILE
    tall_row = iota((tall, 1), 0)
    kind = jnp.where(
        tall_row < rows,
        0.0,
        jnp.where(tall_row < rows + RIM, 2.0, jnp.where(tall_row >= tall - RIM, 1.0, -1.0)),
    )
    count = n_wide * block
    own_link = jnp.concatenate([planes[ICE_LINK], rim_link], axis=0)[:, 0:1]
    slots = (rows, cap, block, count, n_wide)
    found = list(ice_slots(own_link, kind, *slots)[:3])
    for n, hot in enumerate(found):
        hots[n * tall : (n + 1) * tall, :] = hot
    ocean_link = planes[OCEAN_LINK][:, 0:1]
    ocean_row = spread(ocean_link)
    tile = divide(ocean_link - 1.0, rows)
    tile_row = divide(ocean_row - 1.0, rows)
    hits = (tile == tile_row) & (ocean_row > 0.5) & (ocean_row < ocean_link)
    rank = jnp.sum(hits.astype(F32), axis=1, keepdims=True)
    target = jnp.where(ocean_link > 0.5, tile * block + 3 * cap + rank, -1.0)
    hots[len(found) * tall :, :] = (iota((rows, count), 1).astype(F32) == target).astype(F32)


def ocean_kernel(n_wide, n_narrow, cap, block, n_parts, n_tiles, layers, *refs):
    parts, refs = refs[:n_parts], refs[n_parts:]
    field, pair, cross, planes, out, top, hots, held, sems = refs
    _, rows, levels, _ = field.shape
    places = Places(levels, layers)
    chunks = sems.shape[0] // 3
    step = rows // chunks
    up, down = came_from(pair, cross)
    lane = iota((1, LANES), 1)
    row = iota((rows, LANES), 0)
    first, last = lane == 0, lane == LANES - 1
    wet = planes[WET]
    wet_halo = plane_halo(merged_planes(parts, rows, n_narrow), WET)
    scale = DIFFUSE * wet
    coef = (
        scale * jnp.where(row > 0, turn(wet, 1, 0), up(places.wet + TILE - 1, 1)),
        scale * jnp.where(row < rows - 1, turn(wet, -1, 0), down(places.wet, 1)),
        scale * jnp.where(first, 0.0, turn(wet, 1, 1)),
        scale * jnp.where(last, 0.0, turn(wet, -1, 1)),
    )
    edge = first | last
    weight = jnp.where(first, turn(wet_halo, 1, 1), turn(wet_halo, -1, 1))
    weight = scale * jnp.where(edge, weight, 0.0)
    centre_coef = 1.0 - (coef[0] + coef[1] + coef[2] + coef[3] + weight)
    even = lane % 2 == 0
    strip_at = (1 + n_tiles) * rows
    came = merged([p[strip_at:, :] for p in parts], even, ~even, n_narrow)
    came = jnp.where(even, turn(came, 1, 1), turn(came, -1, 1))
    packed = [turn(weight[i : i + 1, :], 2 * i, 1) for i in range(rows)]
    packed = functools.reduce(lambda a, b: a + b, packed)
    packed = packed + turn(packed, 2 * rows, 1) + turn(packed, 4 * rows, 1)
    side = packed * came
    writes = []
    for f in range(3):
        for h in range(chunks):
            for i in range(h * step, (h + 1) * step):
                centre = field[f, i]
                above = field[f, i - 1] if i > 0 else up(f * levels, levels)
                below = field[f, i + 1] if i < rows - 1 else down(f * levels, levels)
                value = centre * centre_coef[i : i + 1, :]
                value = value + above * coef[0][i : i + 1, :]
                value = value + below * coef[1][i : i + 1, :]
                value = value + turn(centre, 1, 1) * coef[2][i : i + 1, :]
                value = value + turn(centre, -1, 1) * coef[3][i : i + 1, :]
                value = value + jnp.where(edge, turn(side, -2 * (f * rows + i), 1), 0.0)
                held[f, i] = value
                if f == 2:
                    top[i] = value[0:TILE, :]
            part = pl.ds(h * step, step)
            level = pl.ds(TILE, levels - TILE) if f == 2 else pl.ds(0, levels)
            copy = pltpu.make_async_copy(
                held.at[f, part, level],
                out.at[f, part, level],
                sems.at[f * chunks + h],
            )
            copy.start()
            writes.append(copy)
    under = iota((TILE, 1), 0) < HALO
    rim_link = jnp.where(under, down(places.link, TILE), up(places.link, TILE))
    own_hots(planes, rim_link, n_wide, cap, block, hots)
    for copy in writes:
        copy.wait()


def ice_slots(link_col, kind_col, rows, cap, block, count, n_wide):
    link_row = spread(link_col)
    kind_row = spread(kind_col)
    number = link_col - 1.0
    tile = divide(number, rows)
    inner = number - tile * rows
    tile_row = divide(link_row - 1.0, rows)
    ok = (link_col > 0.5) & (kind_col > -0.5)
    ok_row = (link_row > 0.5) & (kind_row > -0.5)
    hits = (tile == tile_row) & (kind_col == kind_row) & ok_row & (link_row < link_col)
    rank = jnp.sum(hits.astype(F32), axis=1, keepdims=True)
    place = iota((link_col.shape[0], count), 1).astype(F32)

    def hot(keep, target):
        return (place == jnp.where(keep, target, -1.0)).astype(F32)

    top, bottom = inner < 0.5, inner > rows - 1.5
    edge = ok & (top | bottom)
    near = jnp.where(top, tile - 1.0, tile + 1.0)
    near_ok = edge & (near > -0.5) & (near < n_wide - 0.5)
    slot = hot(ok, tile * block + kind_col * cap + rank)
    near_edge = hot(near_ok, near * block + jnp.where(top, 3.0 * cap + 1.0, 3.0 * cap))
    own_edge = hot(edge, tile * block + jnp.where(top, 3.0 * cap, 3.0 * cap + 1.0))
    near_slot = hot(near_ok, near * block)
    own_slot = hot(edge, tile * block)
    return slot, near_edge, own_edge, near_slot, own_slot, bottom.astype(F32)


def around(value):
    return turn(value, 1, 0) + turn(value, -1, 0) + turn(value, 1, 1) + turn(value, -1, 1)


def sweep_layer(vel, k, layers, rate, friction):
    u, v = vel(0, k), vel(1, k)
    ends = [[turn(w, s, axis) for axis in (0, 1) for s in (-1, 1)] for w in (u, v)]
    ux, uy = ends[0][0] - ends[0][1], ends[0][2] - ends[0][3]
    vx, vy = ends[1][0] - ends[1][1], ends[1][2] - ends[1][3]
    cross = uy + vx
    eps2 = ux * (ux + vy) + vy * vy + 0.25 * (cross * cross)
    if k < layers - 1:
        uz, vz = vel(0, k + 1) - u, vel(1, k + 1) - v
        eps2 = eps2 + (uz * uz + vz * vz)
    eps2 = 0.25 * eps2
    eta = rate * jnp.exp((-1.0 / 3.0) * jnp.log(eps2 + STRAIN_FLOOR))
    links_up_down = float((k > 0) + (k < layers - 1))
    diagonal = eta * (2.0 + links_up_down) + 0.5 * around(eta) + friction
    sums = []
    for f, w in enumerate((u, v)):
        total = 0.5 * (ends[f][0] + ends[f][1] + ends[f][2] + ends[f][3])
        if k > 0:
            total = total + vel(f, k - 1)
        if k < layers - 1:
            total = total + vel(f, k + 1)
        sums.append(eta * total + 0.5 * around(eta * w))
    return sums, 1.0 / diagonal, eta * eps2


FLAT = ("thick", "grounded", "inside")


def first_kernel(n_wide, n_narrow, cap, block, n_parts, levels, *refs):
    parts, refs = refs[:n_parts], refs[n_parts:]
    corners, refs = refs[:n_parts], refs[n_parts:]
    ice, pair, cross, planes, sums, inverse, rate, flat, hots, ends, vel = refs
    _, layers, rows, _ = ice.shape
    places = Places(levels, layers)
    n_tiles = ice_tiles(layers)
    up, down = came_from(pair, cross)
    lane = iota((1, LANES), 1)
    width = 2 * LANES
    tall = rows + TILE
    wide_lane = iota((1, width), 1)
    place_wide = lax.axis_index("wide")
    has_right, has_left = narrow_sides(n_narrow)
    has_up, has_down = place_wide > 0, place_wide < n_wide - 1
    under = iota((TILE, 1), 0) < HALO

    def rim(at):
        return jnp.where(under, down(at, TILE), up(at, TILE))

    def below(a, b):
        return jnp.concatenate([a, b], axis=0)

    corner_planes = merged(
        [c[0:TILE, :] for c in corners], right_lanes(16), left_lanes(16), n_narrow
    )
    corner_ice = [
        merged(
            [c[(1 + t) * TILE : (2 + t) * TILE, :] for c in corners],
            right_lanes(8), left_lanes(8), n_narrow,
        )
        for t in range(n_tiles)
    ]
    block_tall = below(merged_planes(parts, rows, n_narrow), corner_planes)
    flat[0] = jnp.concatenate(
        [below(planes[THICK], rim(places.thick)), plane_halo(block_tall, THICK)], axis=1
    )
    grounded_tall = jnp.concatenate(
        [below(planes[GROUNDED], rim(places.grounded)), plane_halo(block_tall, GROUNDED)], axis=1
    )
    flat[1] = grounded_tall
    tall_row = iota((tall, 1), 0)
    inside = (
        ((tall_row < rows) | ((tall_row < rows + HALO) & has_down) | ((tall_row >= rows + HALO) & has_up))
        & (
            (wide_lane < LANES)
            | ((wide_lane < LANES + HALO) & has_right)
            | ((wide_lane >= width - HALO) & has_left)
        )
    ).astype(F32)
    flat[2] = inside
    kind = jnp.where(
        tall_row < rows,
        0.0,
        jnp.where(tall_row < rows + RIM, 2.0, jnp.where(tall_row >= tall - RIM, 1.0, -1.0)),
    )
    count = n_wide * block
    found = []
    slots = (rows, cap, block, count, n_wide)
    links = plane_halo(block_tall, ICE_LINK)
    if n_narrow == 2:
        sides = [jnp.max(links, axis=1, keepdims=True)]
    else:
        sides = [links[:, 0:1], links[:, LANES - 1 : LANES]]
    for link in sides:
        slot, _, _, near_slot, own_slot, bottom = ice_slots(link, kind, *slots)
        ends[len(found) // 3] = jnp.broadcast_to(bottom, (tall, LANES))
        found += [slot, near_slot, own_slot]
    for n, hot in enumerate(found):
        hots[n * tall : (n + 1) * tall, :] = hot
    strips = [
        below(a, b) for a, b in zip(merged_ice(parts, rows, n_tiles, n_narrow), corner_ice)
    ]
    edge = (lane < HALO) | (lane >= LANES - HALO)
    for index in range(3 * layers):
        f, k = divmod(index, layers)
        beyond = beyond_ice(up, down, places, layers, f, k)
        t, group = ice_group(index)
        beside = jnp.where(edge, turn(strips[t], -8 * group, 1), 0.0)
        value = jnp.concatenate([below(ice[f, k], beyond), beside], axis=1)
        if f < 2:
            vel[f, k] = value
        else:
            rate[k] = jnp.exp(0.25 * value) * inside
    friction = 0.1 + 9.9 * grounded_tall
    for k in range(layers):
        both, over, _ = sweep_layer(lambda f, n: vel[f, n], k, layers, rate[k], friction)
        for f in range(2):
            sums[f, k] = both[f]
        inverse[k] = over * inside


def final_kernel(n_wide, n_narrow, cap, block, *refs):
    (
        blocks, own, hots, ends, planes, ice, top, sums, inverse, rate, flat, ocean_in,
        ice_out, ocean_out, thick_out, melt_out,
        vel, result, thin, melted, new_top, sems,
    ) = refs
    _, layers, rows, _ = ice.shape
    tall, width = flat.shape[1:]
    lane = iota((1, LANES), 1)
    order = exchange_order(n_wide)
    parts = [
        jnp.concatenate(
            [blocks[order.index(t), n * block : (n + 1) * block, :] for t in range(n_wide)], axis=0
        )
        for n in range(3)
    ]
    n_own = 3 * tall
    hot = jnp.concatenate([own[0:n_own, :], hots[...], own[n_own:, :]], axis=0)
    found = pick(hot, jnp.concatenate(parts, axis=1))

    def got(n, part):
        return found[n * tall : (n + 1) * tall, part * LANES : (part + 1) * LANES]

    wet_main = got(0, 1)
    mixed_main = got(0, 0) + DIFFUSE * (wet_main * got(1, 2) - got(1, 1) * got(2, 2))
    sides = []
    for n in range(3, 3 * (1 if n_narrow == 2 else 2) + 3, 3):
        value, near, own = got(n, 2), got(n + 1, 2), got(n + 2, 2)

        def group(row, j):
            return turn(row, -16 * j, 1)

        wet_got = group(value, PART_WET)
        bottom = ends[n // 3 - 1] > 0.5
        near_warm = jnp.where(bottom, group(near, EDGE_T0), group(near, EDGE_T1))
        near_wet = jnp.where(bottom, group(near, EDGE_W0), group(near, EDGE_W1))
        own_warm = jnp.where(bottom, group(own, EDGE_T1), group(own, EDGE_T0))
        sides.append((value + DIFFUSE * (wet_got * near_warm - near_wet * own_warm), wet_got))
    if len(sides) == 1:
        mixed_side, wet_side = sides[0]
    else:
        mixed_side, wet_side = (jnp.where(lane < HALO, a, b) for a, b in zip(*sides))
    mixed_tall = jnp.concatenate([mixed_main, mixed_side], axis=1)
    wet_tall = jnp.concatenate([wet_main, wet_side], axis=1)
    thick_tall, grounded_tall, inside = flat[0], flat[1], flat[2]
    open_ice = 1.0 - grounded_tall
    draft_tall = 0.9 * thick_tall * open_ice
    melt_tall = GAMMA_MELT * (mixed_tall - wet_tall * (0.0832 - 0.761 * draft_tall))
    new_thick = (thick_tall - TIME_STEP * melt_tall * open_ice) * inside
    thin[...] = new_thick[:rows, :LANES]
    n_hots = n_own + hots.shape[0]
    ocean_draft = found[n_hots:, :LANES]
    heat_top = jnp.concatenate([top[i, 0:1, :] for i in range(rows)], axis=0)
    coupled = (planes[OCEAN_LINK] > 0.5).astype(F32)
    melt = GAMMA_MELT * (heat_top - (0.0832 - 0.761 * ocean_draft)) * planes[WET] * coupled
    melted[...] = melt
    cooled = heat_top - 0.2 * melt
    new_top[...] = top[...]
    for i in range(rows):
        new_top[i, 0:1, :] = cooled[i : i + 1, :]
    writes = fetch_all(
        (
            (new_top, ocean_out.at[2, :, pl.ds(0, TILE), :]),
            (thin, thick_out),
            (melted, melt_out),
        ),
        sems,
    )
    surface = new_thick * (0.1 + 0.9 * grounded_tall)
    scale = (-0.5 * SLOPE_SCALE) * new_thick
    stress = (
        scale * (turn(surface, -1, 0) - turn(surface, 1, 0)),
        scale * (turn(surface, -1, 1) - turn(surface, 1, 1)),
    )
    friction = 0.1 + 9.9 * grounded_tall
    for f in range(2):
        for k in range(layers):
            vel[0, f, k] = (sums[f, k] + stress[f]) * inverse[k]
    cuts = [0, layers - layers // 4, layers]
    for sweep in range(1, PICARD):
        last = sweep == PICARD - 1
        old = sweep - 1
        for k in range(layers):
            both, over, heat = sweep_layer(
                lambda f, n: vel[old, f, n], k, layers, rate[k], friction
            )
            for f in range(2):
                value = (both[f] + stress[f]) * over
                if last:
                    result[f, k] = value[:rows, :LANES]
                else:
                    vel[sweep, f, k] = value * inside
            if last:
                result[2, k] = ice[2, k] + HEATING_RATE * heat[:rows, :LANES]
                if k + 1 in cuts:
                    part = pl.ds(cuts[cuts.index(k + 1) - 1], k + 1 - cuts[cuts.index(k + 1) - 1])
                    copy = pltpu.make_async_copy(
                        result.at[:, part], ice_out.at[:, part], sems.at[len(writes)]
                    )
                    copy.start()
                    writes.append(copy)
    for copy in writes:
        copy.wait()


def local(
    ice_x, ice_y, ice_temp, ocean_x, ocean_y, ocean_temp, thick, grounded_mask, wet_mask, ice_links, ocean_links,
):
    n_wide, n_narrow = lax.axis_size("wide"), lax.axis_size("narrow")
    rows, layers, columns = ice_x.shape
    levels = ocean_x.shape[1]
    cap = max(1, 2 * rows // n_wide)
    block = -(-max(4 * cap, 3 * cap + 2) // TILE) * TILE
    assert columns == LANES and ice_links.shape[0] == rows

    def stay(value):
        return pltpu.with_memory_space_constraint(value, pltpu.HBM)

    ice_fields = [stay(x.transpose(1, 0, 2)) for x in (ice_x, ice_y, ice_temp)]
    links = [stay(x.reshape(1, rows)) for x in (ice_links, ocean_links)]
    fields = [stay(x) for x in (ocean_x, ocean_y, ocean_temp)]
    planes_in = [stay(x) for x in (thick, grounded_mask, wet_mask)]
    here = pl.BlockSpec(memory_space=pltpu.VMEM)
    far = pl.BlockSpec(memory_space=pltpu.HBM)
    unread = pl.BlockSpec(memory_space=pl.ANY)
    dma = pltpu.SemaphoreType.DMA

    def array(*shape):
        return jax.ShapeDtypeStruct(shape, F32)

    def kept(*shape):
        return pltpu.VMEM(shape, F32)

    def near(*values):
        return [pltpu.with_memory_space_constraint(value, pltpu.VMEM) for value in values]

    def call(kernel, name, microseconds, out_shape, in_specs, out_specs, scratch=(), **more):
        estimate = pl.CostEstimate(
            flops=int(microseconds * 1.0e9), bytes_accessed=int(microseconds * 3.0e6), transcendentals=0
        )
        return pl.pallas_call(
            kernel, name=name, out_shape=out_shape, in_specs=in_specs, out_specs=out_specs,
            scratch_shapes=scratch, compiler_params=VMEM, cost_estimate=estimate, **more,
        )

    n_tiles = ice_tiles(layers)
    places = Places(levels, layers)
    chunks = 1
    message, to_pair, to_cross, planes, ice, field = call(
        edges_kernel, "edges", 4.0,
        (
            kept((1 + n_tiles) * rows + levels, LANES), kept(places.end, LANES), kept(places.end, LANES),
            kept(PLANES, rows, LANES), kept(3, layers, rows, LANES), kept(3, rows, levels, LANES),
        ),
        [far] * 11, (here,) * 6,
        [
            pltpu.VMEM((rows, LANES), F32),
            pltpu.VMEM((rows, LANES), jnp.int32),
            pltpu.VMEM((rows, LANES), jnp.int32),
            pltpu.VMEM((2, 1, rows), jnp.int32),
            dma((8,)),
            dma((3 * chunks,)),
        ],
    )(*ice_fields, *fields, *planes_in, *links)

    def narrow(value):
        if n_narrow == 2:
            return [lax.ppermute(value, "narrow", [(0, 1), (1, 0)])]
        ahead = [(i, i + 1) for i in range(n_narrow - 1)]
        return [
            lax.ppermute(value, "narrow", [(j, i) for i, j in ahead]),
            lax.ppermute(value, "narrow", ahead),
        ]

    parts = narrow(message)
    n_parts = len(parts)
    assert n_wide % 2 == 0
    swaps = [[(i, i + 1) for i in range(start, n_wide - 1, 2)] for start in (0, 1)]
    pair, cross = (
        lax.ppermute(value, "wide", swap + [(j, i) for i, j in swap])
        for value, swap in zip((to_pair, to_cross), swaps)
    )
    blocks = call(
        functools.partial(blocks_kernel, n_wide, n_narrow, cap, block, n_parts), "blocks", 4.0,
        kept(n_wide, 3 * block, LANES), [here] * (n_parts + 1), here,
    )(*near(*parts, planes))
    blocks = lax.all_to_all(
        blocks, "wide", split_axis=0, concat_axis=0, tiled=True, axis_index_groups=[exchange_order(n_wide)]
    )
    corners = narrow(
        call(
            functools.partial(corners_kernel, levels, layers), "corners", 1.0,
            kept((1 + n_tiles) * TILE, LANES), [here] * 2, here,
        )(*near(pair, cross))
    )
    tall = rows + TILE
    ocean, top, own = call(
        functools.partial(ocean_kernel, n_wide, n_narrow, cap, block, n_parts, n_tiles, layers), "ocean", 4.0,
        (array(3, rows, levels, LANES), kept(rows, TILE, LANES), kept(3 * tall + rows, n_wide * block)),
        [here] * (n_parts + 4), (far, here, here),
        [
            pltpu.VMEM((3, rows, levels, LANES), F32),
            dma((3 * chunks,)),
        ],
    )(*near(*parts, field, pair, cross, planes))
    wide = 2 * LANES
    tall = rows + TILE
    n_sides = 1 if n_narrow == 2 else 2
    sums, inverse, rate, flat, hots, ends = call(
        functools.partial(first_kernel, n_wide, n_narrow, cap, block, n_parts, levels), "first", 4.0,
        (
            kept(2, layers, tall, wide), kept(layers, tall, wide), kept(layers, tall, wide), kept(3, tall, wide),
            kept(3 * n_sides * tall, n_wide * block), kept(n_sides, tall, LANES),
        ),
        [here] * (2 * n_parts + 4), (here,) * 6,
        [pltpu.VMEM((2, layers, tall, wide), F32)],
    )(*near(*parts, *corners, ice, pair, cross, planes))
    ice, ocean, thick_out, melt_out = call(
        functools.partial(final_kernel, n_wide, n_narrow, cap, block), "final", 3.0,
        (
            array(3, layers, rows, LANES), array(3, rows, levels, LANES),
            array(rows, LANES), array(rows, LANES),
        ),
        [here] * 11 + [far], (far,) * 4,
        [
            pltpu.VMEM((PICARD - 1, 2, layers, tall, wide), F32),
            pltpu.VMEM((3, layers, rows, LANES), F32),
            pltpu.VMEM((rows, LANES), F32),
            pltpu.VMEM((rows, LANES), F32),
            pltpu.VMEM((rows, TILE, LANES), F32),
            dma((3 + layers,)),
        ],
        input_output_aliases={11: 1},
    )(*near(blocks, own, hots, ends, planes, ice, top, sums, inverse, rate, flat), ocean)
    return ice.transpose(0, 2, 1, 3), ocean, thick_out, melt_out


def solution(mesh):
    column = P("wide", None, "narrow")
    plane = P("wide", "narrow")
    return jax.shard_map(
        local,
        mesh=mesh,
        in_specs=(column,) * 6 + (plane,) * 5,
        out_specs=(P(None, "wide", None, "narrow"), P(None, "wide", None, "narrow"), plane, plane),
        check_vma=False,
    )
```
